32 devices in a mesh: req: 8 (over z, y), tensor: 4 (over x, core).
Axes of the slice: x: 2, y: 2, z: 4, core: 2. Of those that a mesh axis runs over, the one named last changes fastest.
Arguments:
- span_in: bfloat16 [16, 512, 2048], P('req'), may hold values from -6 to 6
- w_qkv: bfloat16 [3, 2048, 2048], P(None, None, 'tensor'), may hold values from -1 to 1
- qk_gain: bfloat16 [2, 2048], P(None, 'tensor'), may hold values from 0.099609375 to 1.8984375
- w_out: bfloat16 [2048, 2048], P('tensor'), may hold values from -1 to 1
- post_gain: bfloat16 [2048], P('tensor'), may hold values from 0.099609375 to 1.8984375
- kv_pool: bfloat16 [4, 512, 16, 2048], P(None, 'req', None, 'tensor'), may hold values from -66 to 66
- block_table: int32 [16, 32], replicated, may hold values from 0 to 63, as said below
- request_order: int32 [16], replicated, may hold values from 0 to 15, each once
- lengths: int32 [16], replicated, may hold values from 1 to 512, as said below
Outputs:
- span_out: bfloat16 [16, 512, 2048], P('req', None, 'tensor')
- relaid_cache: bfloat16 [4, 16, 512, 2048], P(None, 'req', None, 'tensor')
The draws below stay inside these ranges and needn't reach their ends.
Inputs may be any that keep to these rules, and one draw needn't show every extreme that they name: `block_table`: entry (r, j) is the slot, among the 64 slots of the req index j modulo the number of req devices, that holds block j of request r; each slot of each req index is named once. `lengths`: some request has exactly 512 cached tokens.
All inputs are finite; a program needn't handle non-finite values.
Results may differ from the reference program's by a relative error of at most 0.0095.
Values may be sent and summed in bfloat16 or wider, within the bound.
No kernel may reach another device: no remote copies, remote signals or barrier semaphores. Data moves between devices by JAX's collectives and lax.ppermute only.
A program may use at most 192 MiB of HBM per device.

```python
import jax
import jax.numpy as jnp
from jax import lax

D = 2048
HEADS = 16
HD = 128
LAY = 2
CTX = 512
BLK = 16
SPAN = 512
REQS = 16
BPD = 4
SLOTS = 64
N_REQ = 8
N_TENSOR = 4


def normal_clipped(key, shape_all):
    return jnp.clip(jax.random.normal(key, shape_all, jnp.float32), -6.0, 6.0)


def draw_w_qkv(key, part):
    shape_all = (3, D, D)
    values = normal_clipped(key, shape_all)
    return (values * D ** (-0.5)).astype(jnp.bfloat16)


def draw_w_out(key, part):
    shape_all = (D, D)
    values = normal_clipped(key, shape_all)
    return (values * D ** (-0.5)).astype(jnp.bfloat16)


def draw_block_table(key, part):
    subkeys = jax.random.split(key, N_REQ)

    def one_device(subkey):
        return jax.random.permutation(subkey, SLOTS)
    permuted = jax.vmap(one_device)(subkeys)
    shaped = permuted.reshape(N_REQ, REQS, BPD)
    return jnp.transpose(shaped, (1, 2, 0)).reshape(REQS, BPD * N_REQ).astype(jnp.int32)


def draw_lengths(key, part):
    first_key, second_key = jax.random.split(key)
    drawn_lengths = jax.random.randint(first_key, (REQS,), 1, CTX + 1)
    longest = jax.random.randint(second_key, (), 0, REQS)
    return jnp.where(jnp.arange(REQS) == longest, CTX, drawn_lengths).astype(jnp.int32)


def draw_kv_pool(key, part):
    shape_all = (2 * LAY, N_REQ * SLOTS, BLK, D)
    base_key = jax.random.fold_in(key, 0)
    values = normal_clipped(base_key, shape_all)
    return values.astype(jnp.bfloat16)


def level_of(key, dims, pieces, least, top_value):
    level, own = 1.0, jax.random.fold_in(key, 6)
    for axis_at, shards_of in pieces:
        heights = jnp.exp(jax.random.uniform(jax.random.fold_in(own, axis_at), (shards_of,), jnp.float32, least / len(pieces), top_value / len(pieces)))
        level = level * jnp.repeat(heights, dims[axis_at] // shards_of).reshape([-1 if axis == axis_at else 1 for axis in range(len(dims))])
    return level


def bell_draw(key, dims, spread, limit, cuts=(), kind=jnp.bfloat16):
    values = spread * jax.random.normal(key, dims, jnp.float32)
    if cuts:
        values = values * level_of(key, dims, cuts, -0.22, 0.18)
    return jnp.clip(values, -limit, limit).astype(kind)


def setup_inputs(seed: int = 0) -> dict:
    splits = jax.random.split(jax.random.key(seed), 10)
    span_in = bell_draw(splits[0], (REQS, SPAN, D), 1.0, 6.0, ((0, 8),))
    w_qkv = draw_w_qkv(jax.random.fold_in(splits[9], 71), 0)
    qk_gain = jnp.clip(1.0 + 0.18 * jax.random.normal(splits[2], (2, D), jnp.float32), 0.099609375, 1.8984375).astype(jnp.bfloat16)
    w_out = draw_w_out(jax.random.fold_in(splits[9], 71), 0)
    post_gain = jnp.clip(1.0 + 0.18 * jax.random.normal(splits[4], (D,), jnp.float32), 0.099609375, 1.8984375).astype(jnp.bfloat16)
    kv_pool = draw_kv_pool(jax.random.fold_in(splits[9], 71), 0)
    block_table = draw_block_table(jax.random.fold_in(splits[9], 71), 0)
    request_order = jax.random.permutation(splits[7], REQS).astype(jnp.int32)
    lengths = draw_lengths(jax.random.fold_in(splits[9], 71), 0)
    return dict(span_in=span_in, w_qkv=w_qkv, qk_gain=qk_gain, w_out=w_out, post_gain=post_gain, kv_pool=kv_pool, block_table=block_table, request_order=request_order, lengths=lengths)


norm_eps = 1e-06
rope_base = 500000.0

def rotate(values, positions):
    half_dim = values.shape[-1] // 2
    frequency = rope_base ** (-jnp.arange(half_dim, dtype=jnp.float32) * (2.0 / values.shape[-1]))
    angles = positions[:, None] * frequency[None, :]
    cosine = jnp.cos(angles)[:, None, :]
    sine_part = jnp.sin(angles)[:, None, :]
    first_half = values[..., :half_dim]
    second_half = values[..., half_dim:]
    return jnp.concatenate([first_half * cosine - second_half * sine_part, second_half * cosine + first_half * sine_part], axis=-1)

def reference(span_in, w_qkv, qk_gain, w_out, post_gain, kv_pool, block_table, request_order, lengths):
    token_ids = jnp.arange(CTX, dtype=jnp.int32)
    block_ids = token_ids // BLK
    offsets = token_ids % BLK
    slot_ids = jnp.take(block_table, request_order, axis=0)[:, block_ids]
    global_slots = ((block_ids % N_REQ)[None, :] * SLOTS + slot_ids).astype(jnp.int32)
    relaid_cache = kv_pool[:, global_slots, offsets[None, :], :]
    ordered_lengths = jnp.take(lengths, request_order)
    part_width = D // N_TENSOR

    def one_request(inputs):
        tokens, cached_len, cache_keys, cache_values = inputs
        queries = jnp.dot(tokens, w_qkv[0], preferred_element_type=jnp.float32)
        keys_new = jnp.dot(tokens, w_qkv[1], preferred_element_type=jnp.float32)
        values_new = jnp.dot(tokens, w_qkv[2], preferred_element_type=jnp.float32).astype(jnp.bfloat16)
        queries = queries * lax.rsqrt(lax.optimization_barrier(jnp.mean(queries * queries, axis=-1, keepdims=True)) + norm_eps) * qk_gain[0].astype(jnp.float32)
        keys_new = keys_new * lax.rsqrt(lax.optimization_barrier(jnp.mean(keys_new * keys_new, axis=-1, keepdims=True)) + norm_eps) * qk_gain[1].astype(jnp.float32)
        positions = cached_len.astype(jnp.float32) + jnp.arange(SPAN, dtype=jnp.float32)
        query_rot = rotate(queries.reshape(SPAN, HEADS, HD), positions).astype(jnp.bfloat16)
        key_rot = rotate(keys_new.reshape(SPAN, HEADS, HD), positions).astype(jnp.bfloat16)
        all_keys = jnp.concatenate([cache_keys.reshape(CTX, HEADS, HD), key_rot], axis=0)
        all_values = jnp.concatenate([cache_values.reshape(CTX, HEADS, HD), values_new.reshape(SPAN, HEADS, HD)], axis=0)
        scores = jnp.einsum('qhd,khd->hqk', query_rot.astype(jnp.float32), all_keys.astype(jnp.float32)) * HD ** (-0.5)
        cache_live = jnp.arange(CTX, dtype=jnp.int32) < cached_len
        causal = jnp.arange(SPAN)[None, :] <= jnp.arange(SPAN)[:, None]
        live_mask = jnp.concatenate([jnp.broadcast_to(cache_live[None, :], (SPAN, CTX)), causal], axis=1)
        scores = jnp.where(live_mask[None], scores, -1e+30)
        maxima = lax.optimization_barrier(jnp.max(scores, axis=-1, keepdims=True))
        exponent = jnp.exp(scores - maxima)
        weights = (exponent / lax.optimization_barrier(jnp.sum(exponent, axis=-1, keepdims=True))).astype(jnp.bfloat16)
        attended = jnp.einsum('hqk,khd->qhd', weights.astype(jnp.float32), all_values.astype(jnp.float32))
        attended = attended.astype(jnp.bfloat16).reshape(SPAN, D)
        total_sum = jnp.zeros((SPAN, D), jnp.float32)
        for group_no in range(N_TENSOR):
            low = group_no * part_width
            partial_value = jnp.dot(attended[:, low:low + part_width], w_out[low:low + part_width], preferred_element_type=jnp.float32)
            rounded = lax.optimization_barrier(partial_value.astype(jnp.bfloat16))
            total_sum = total_sum + rounded.astype(jnp.float32)
        normed = total_sum * lax.rsqrt(lax.optimization_barrier(jnp.mean(total_sum * total_sum, axis=-1, keepdims=True)) + norm_eps)
        return (tokens.astype(jnp.float32) + normed * post_gain.astype(jnp.float32)).astype(jnp.bfloat16)
    span_out = lax.map(one_request, (span_in, ordered_lengths, relaid_cache[0], relaid_cache[1]))
    return (span_out, relaid_cache)
```

```python
import functools
import math

import jax
import jax.numpy as jnp
from jax import lax
from jax.experimental import pallas as pl
from jax.experimental.pallas import tpu as pltpu
from jax.sharding import PartitionSpec as P

HD = 128
norm_eps = 1e-06
rope_base = 500000.0

ANY = pl.BlockSpec(memory_space=pl.ANY)
SMEM = pl.BlockSpec(memory_space=pltpu.SMEM)
VMEM_LIMIT = 48 * 1024 * 1024


def cost(flops, moved, exps=0):
    return pl.CostEstimate(flops=flops, bytes_accessed=moved, transcendentals=exps)


def params():
    return pltpu.CompilerParams(vmem_limit_bytes=VMEM_LIMIT)


def gather_body(offsets, first, planes, count, per_device, blocks, together, table, order, pool, *rest):
    outs, sems = rest[:-1], rest[-1]
    if together:
        outs = outs[-1:]
    else:
        outs = outs[-len(offsets) :]
    me = lax.axis_index("req")
    for at, offset in enumerate(offsets):
        target = offset if together else me ^ offset
        for p in range(per_device):
            request = order[target * per_device + p]
            for b in range(blocks):
                slot = table[request, b * count + me]
                place = outs[0].at[at, :, p, b] if together else outs[at].at[:, p, b]
                pltpu.make_async_copy(
                    pool.at[pl.ds(first, planes), slot], place, sems.at[0 if together else at]
                ).start()
    for at, out in enumerate(outs):
        pltpu.make_async_copy(out, out, sems.at[at]).wait()


def gather(pool, table, order, count, offsets, first, planes, together, after=()):
    per_device = order.shape[0] // count
    blocks = table.shape[1] // count
    piece = (planes, per_device, blocks) + pool.shape[2:]
    if together:
        shapes = [jax.ShapeDtypeStruct((len(offsets),) + piece, pool.dtype)]
    else:
        shapes = [jax.ShapeDtypeStruct(piece, pool.dtype) for _ in offsets]
    moved = 4 * len(offsets) * math.prod(piece)
    return pl.pallas_call(
        functools.partial(gather_body, offsets, first, planes, count, per_device, blocks, together),
        in_specs=[SMEM, SMEM, ANY] + [ANY] * len(after),
        out_specs=[ANY] * len(shapes),
        out_shape=shapes,
        scratch_shapes=[pltpu.SemaphoreType.DMA((len(shapes),))],
        cost_estimate=cost(0, moved),
        compiler_params=params(),
        name="gather_blocks",
    )(table, order, pool, *after)


def place_body(offsets, first, planes, count, per_device, blocks, together, filled, table, order, pool, *rest):
    sems, out = rest[-1], rest[-2]
    received = rest[1:] if filled else rest
    me = lax.axis_index("req")
    for p in range(per_device):
        request = order[me * per_device + p]
        for b in range(blocks):
            slot = table[request, b * count + me]
            pltpu.make_async_copy(
                pool.at[pl.ds(first, planes), slot],
                out.at[pl.ds(first, planes), p, b, me],
                sems.at[0],
            ).start()
    copies = []
    for at, offset in enumerate(offsets):
        source = me ^ offset
        piece = received[0].at[source] if together else received[at]
        copy = pltpu.make_async_copy(
            piece, out.at[pl.ds(first, planes), :, :, source], sems.at[1 + at]
        )
        copy.start()
        copies.append(copy)
    own = out.at[pl.ds(first, planes), :, :, me]
    pltpu.make_async_copy(own, own, sems.at[0]).wait()
    for copy in copies:
        copy.wait()


def place(pool, table, order, count, offsets, first, planes, together, received, filled=None):
    per_device = order.shape[0] // count
    blocks = table.shape[1] // count
    shape = (pool.shape[0], per_device, blocks, count) + pool.shape[2:]
    start = [] if filled is None else [filled]
    return pl.pallas_call(
        functools.partial(
            place_body, offsets, first, planes, count, per_device, blocks, together, filled is not None
        ),
        in_specs=[SMEM, SMEM, ANY] + [ANY] * (len(start) + len(received)),
        out_specs=ANY,
        out_shape=jax.ShapeDtypeStruct(shape, pool.dtype),
        scratch_shapes=[pltpu.SemaphoreType.DMA((1 + len(offsets),))],
        input_output_aliases={} if filled is None else {3: 0},
        cost_estimate=cost(0, 4 * math.prod(shape) * planes // pool.shape[0]),
        compiler_params=params(),
        name="place_blocks",
    )(table, order, pool, *start, *received)


def turned(values, cosine, sine):
    heads = []
    for head in range(values.shape[1] // HD):
        part = values[:, head * HD : (head + 1) * HD]
        swapped = jnp.concatenate([part[:, HD // 2 :], part[:, : HD // 2]], axis=1)
        heads.append(part * cosine + swapped * sine)
    return jnp.concatenate(heads, axis=1)


def project_body(x, w, gain, cosine, sine, q_out, k_out, v_out, squares):
    rows = x[...]
    for which, out in ((0, q_out), (1, k_out)):
        raw = jnp.dot(rows, w[which], preferred_element_type=jnp.float32)
        squares[:, which : which + 1] = jnp.sum(raw * raw, axis=1, keepdims=True)
        out[...] = turned(raw * gain[which : which + 1].astype(jnp.float32), cosine[...], sine[...])
    v_out[...] = jnp.dot(rows, w[2], preferred_element_type=jnp.float32).astype(v_out.dtype)


def project(x, w, gain, cosine, sine, block=256):
    rows, depth = x.shape
    width = w.shape[2]
    by_row = lambda i: (i, 0)
    return pl.pallas_call(
        project_body,
        grid=(rows // block,),
        in_specs=[
            pl.BlockSpec((block, depth), by_row),
            pl.BlockSpec((3, depth, width), lambda i: (0, 0, 0)),
            pl.BlockSpec((2, width), lambda i: (0, 0)),
            pl.BlockSpec((block, HD), by_row),
            pl.BlockSpec((block, HD), by_row),
        ],
        out_specs=[
            pl.BlockSpec((block, width), by_row),
            pl.BlockSpec((block, width), by_row),
            pl.BlockSpec((block, width), by_row),
            pl.BlockSpec((block, 2), by_row),
        ],
        out_shape=[
            jax.ShapeDtypeStruct((rows, width), jnp.float32),
            jax.ShapeDtypeStruct((rows, width), jnp.float32),
            jax.ShapeDtypeStruct((rows, width), jnp.bfloat16),
            jax.ShapeDtypeStruct((rows, 2), jnp.float32),
        ],
        cost_estimate=cost(6 * rows * depth * width, 2 * (rows * depth + 3 * depth * width + 5 * rows * width)),
        compiler_params=params(),
        name="project_qkv",
    )(x, w, gain, cosine, sine)


def attend_body(which, full_width, q_block, lengths, q, k, v, squares, cache_k, cache_v, out):
    span = q.shape[0]
    context = cache_k.shape[0]
    scales = lax.rsqrt(squares[...] / full_width + norm_eps)
    queries = (q[...] * (scales[:, 0:1] * (HD**-0.5 * math.log2(math.e)))).astype(jnp.bfloat16)
    keys = (k[...] * scales[:, 1:2]).astype(jnp.bfloat16)
    contract = (((1,), (1,)), ((), ()))
    live = lax.broadcasted_iota(jnp.int32, (1, context), 1) < lengths[which]
    for low in range(0, span, q_block):
        high = low + q_block
        part = queries[low:high]
        old = lax.dot_general(part, cache_k[...], contract, preferred_element_type=jnp.float32)
        new = lax.dot_general(part, keys[:high], contract, preferred_element_type=jnp.float32)
        old = jnp.where(live, old, -1e30)
        row = lax.broadcasted_iota(jnp.int32, (q_block, high), 0) + low
        column = lax.broadcasted_iota(jnp.int32, (q_block, high), 1)
        new = jnp.where(column <= row, new, -1e30)
        top = jnp.maximum(
            jnp.max(old, axis=1, keepdims=True), jnp.max(new, axis=1, keepdims=True)
        )
        old = jnp.exp2(old - top)
        new = jnp.exp2(new - top)
        total = jnp.sum(old, axis=1, keepdims=True) + jnp.sum(new, axis=1, keepdims=True)
        mixed = jnp.dot(old.astype(jnp.bfloat16), cache_v[...], preferred_element_type=jnp.float32)
        mixed += jnp.dot(new.astype(jnp.bfloat16), v[:high], preferred_element_type=jnp.float32)
        out[low:high] = (mixed / total).astype(out.dtype)


def attend(which, full_width, span, lengths, q, k, v, squares, cache, q_block=256):
    width = q.shape[1]
    context = cache.shape[2]
    q_block = min(q_block, span)
    head_rows = lambda h: (which, h)
    return pl.pallas_call(
        functools.partial(attend_body, which, full_width, q_block),
        grid=(width // HD,),
        in_specs=[
            SMEM,
            pl.BlockSpec((span, HD), head_rows),
            pl.BlockSpec((span, HD), head_rows),
            pl.BlockSpec((span, HD), head_rows),
            pl.BlockSpec((span, 2), lambda h: (which, 0)),
            pl.BlockSpec((None, None, context, HD), lambda h: (0, which, 0, h)),
            pl.BlockSpec((None, None, context, HD), lambda h: (1, which, 0, h)),
        ],
        out_specs=pl.BlockSpec((span, HD), lambda h: (0, h)),
        out_shape=jax.ShapeDtypeStruct((span, width), jnp.bfloat16),
        cost_estimate=cost(
            4 * span * (span + context) * width,
            span * width * 12 + context * width * 4,
            span * (span + context) * width // HD,
        ),
        compiler_params=params(),
        name="attend",
    )(lengths, q, k, v, squares, cache, cache)


def mix_body(count, *refs):
    parts, w, out, squares = refs[:count], refs[count], refs[count + 1], refs[count + 2]
    me = lax.axis_index("tensor")
    total = jnp.dot(parts[0][...], w[me], preferred_element_type=jnp.float32)
    for at in range(1, count):
        total += jnp.dot(parts[at][...], w[me ^ at], preferred_element_type=jnp.float32)
    out[...] = total
    squares[...] = jnp.sum(total * total, axis=1, keepdims=True)


def mix(parts, w, block=256):
    rows, depth = parts[0].shape
    width = w.shape[2]
    count = len(parts)
    block = min(block, rows)
    return pl.pallas_call(
        functools.partial(mix_body, count),
        grid=(rows // block,),
        in_specs=[pl.BlockSpec((block, depth), lambda i: (i, 0))] * count
        + [pl.BlockSpec((count, depth, width), lambda i: (0, 0, 0))],
        out_specs=[
            pl.BlockSpec((block, width), lambda i: (i, 0)),
            pl.BlockSpec((block, 1), lambda i: (i, 0)),
        ],
        out_shape=[
            jax.ShapeDtypeStruct((rows, width), jnp.float32),
            jax.ShapeDtypeStruct((rows, 1), jnp.float32),
        ],
        cost_estimate=cost(
            2 * rows * depth * width * count,
            2 * count * (rows * depth + depth * width) + 4 * rows * width,
        ),
        compiler_params=params(),
        name="mix_heads",
    )(*parts, w)


def permuted(value, axis, offset):
    size = lax.axis_size(axis)
    return lax.ppermute(value, axis, [(i, i ^ offset) for i in range(size)])


def on_device(
    span_in, w_qkv, qk_gain, w_out, post_gain, kv_pool, block_table, request_order, lengths
):
    req_count = lax.axis_size("req")
    tensor_count = lax.axis_size("tensor")
    req_index = lax.axis_index("req")
    tensor_index = lax.axis_index("tensor")
    per_device, span_len, full_width = span_in.shape
    part_width = w_qkv.shape[2]
    planes = kv_pool.shape[0]
    hand = functools.partial(gather, kv_pool, block_table, request_order, req_count)
    put = functools.partial(place, kv_pool, block_table, request_order, req_count)

    offsets = sorted(range(1, req_count), key=lambda s: (s & (req_count // 2 - 1), -s))
    sent = hand(offsets, 0, 2, False)
    received = [permuted(piece, "req", s) for piece, s in zip(sent, offsets)]

    w_split = jnp.transpose(w_out.reshape(part_width, tensor_count, -1), (1, 0, 2))
    w_mix = lax.all_to_all(w_split, "tensor", 0, 0)

    my_order = lax.dynamic_slice_in_dim(request_order, req_index * per_device, per_device)
    my_lengths = jnp.take(lengths, my_order, mode="clip")
    positions = (
        my_lengths.astype(jnp.float32)[:, None] + jnp.arange(span_len, dtype=jnp.float32)[None, :]
    ).reshape(-1)
    frequency = rope_base ** (-jnp.arange(HD // 2, dtype=jnp.float32) * (2.0 / HD))
    angles = positions[:, None] * frequency[None, :]
    cosine, sine = jnp.cos(angles), jnp.sin(angles)
    cosine = jnp.concatenate([cosine, cosine], axis=1)
    sine = jnp.concatenate([-sine, sine], axis=1)
    flat_in = span_in.reshape(-1, full_width)
    q_raw, k_raw, values, squares = project(flat_in, w_qkv, qk_gain, cosine, sine)
    squares = lax.psum(squares, "tensor")

    rest = planes - 2
    everyone = list(range(req_count))
    (sent_rest,) = hand(everyone, 2, rest, True, after=(q_raw,))
    received_rest = lax.all_to_all(sent_rest, "req", 0, 0)

    relaid = put(offsets, 0, 2, False, received)
    cache = relaid.reshape(planes, per_device, -1, part_width)
    outs, sums = [], []
    for p in range(per_device):
        attended = attend(
            p, full_width, span_len, my_lengths, q_raw, k_raw, values, squares, cache
        )
        parts = {0: attended}
        bit = tensor_count // 2
        while bit:
            for at in list(parts):
                parts[at ^ bit] = permuted(parts[at], "tensor", bit)
            bit //= 2
        out, total = mix([parts[at] for at in range(tensor_count)], w_mix)
        outs.append(out)
        sums.append(total)
    projected = jnp.concatenate(outs, axis=0)
    total = jnp.concatenate(sums, axis=0)
    row_sums = total
    for at in range(1, tensor_count):
        row_sums = row_sums + permuted(total, "tensor", at)
    scale_rows = lax.rsqrt(row_sums / full_width + norm_eps)
    residual = lax.dynamic_slice_in_dim(flat_in, tensor_index * part_width, part_width, 1)
    layer_out = (
        residual.astype(jnp.float32) + projected * scale_rows * post_gain.astype(jnp.float32)
    ).astype(jnp.bfloat16)

    relaid = put(offsets, 2, rest, True, [received_rest], filled=relaid)
    return (
        layer_out.reshape(per_device, span_len, part_width),
        relaid.reshape(planes, per_device, -1, part_width),
    )


def solution(mesh):
    placed = (
        P("req", None, None),
        P(None, None, "tensor"),
        P(None, "tensor"),
        P("tensor", None),
        P("tensor"),
        P(None, "req", None, "tensor"),
        P(),
        P(),
        P(),
    )
    return jax.shard_map(
        on_device,
        mesh=mesh,
        in_specs=placed,
        out_specs=(P("req", None, "tensor"), P(None, "req", None, "tensor")),
        check_vma=False,
    )
```

```python
import functools
import math

import jax
import jax.numpy as jnp
import numpy as np
from jax import lax
from jax.experimental import pallas as pl
from jax.experimental.pallas import tpu as pltpu
from jax.sharding import PartitionSpec as P

HD = 128
norm_eps = 1e-06
rope_base = 500000.0
LATE = (4, 1)

ANY = pl.BlockSpec(memory_space=pl.ANY)
SMEM = pl.BlockSpec(memory_space=pltpu.SMEM)
VMEM = pl.BlockSpec(memory_space=pltpu.VMEM)


def cost(flops, moved, exps=0):
    return pl.CostEstimate(flops=1, bytes_accessed=1, transcendentals=0)


def params(mib=60):
    return pltpu.CompilerParams(vmem_limit_bytes=mib << 20)


def in_vmem(*arrays):
    return [pltpu.with_memory_space_constraint(array, pltpu.VMEM) for array in arrays]


def in_hbm(*arrays):
    return [pltpu.with_memory_space_constraint(array, pltpu.HBM) for array in arrays]


def gather_body(targets, first, planes, count, per_device, blocks, together, table, order, pool, *rest):
    held, loaded, stored = rest[-3:]
    outs = rest[-4:-3] if together else rest[-3 - len(targets) : -3]
    me = lax.axis_index("req")
    for at, target in enumerate(targets):
        if not together:
            target = me ^ target
        for p in range(per_device):
            request = order[target * per_device + p]
            for b in range(blocks):
                slot = table[request, b * count + me]
                pltpu.make_async_copy(
                    pool.at[pl.ds(first, planes), slot], held.at[at, :, p, b], loaded.at[at]
                ).start()
    stores = []
    for at in range(len(targets)):
        pltpu.make_async_copy(held.at[at], held.at[at], loaded.at[at]).wait()
        place = outs[0].at[at] if together else outs[at]
        stores.append(pltpu.make_async_copy(held.at[at], place, stored.at[at]))
        stores[-1].start()
    for store in stores:
        store.wait()


def gather(pool, table, order, count, targets, first, planes, together, after=()):
    per_device = order.shape[0] // count
    blocks = table.shape[1] // count
    piece = (planes, per_device, blocks) + pool.shape[2:]
    whole = (len(targets),) + piece
    shapes = [whole] if together else [piece] * len(targets)
    return pl.pallas_call(
        functools.partial(gather_body, targets, first, planes, count, per_device, blocks, together),
        in_specs=[SMEM, SMEM, ANY] + [ANY] * len(after),
        out_specs=[ANY] * len(shapes),
        out_shape=[pltpu.HBM(shape, pool.dtype) for shape in shapes],
        scratch_shapes=[
            pltpu.VMEM(whole, pool.dtype),
            pltpu.SemaphoreType.DMA((len(targets),)),
            pltpu.SemaphoreType.DMA((len(targets),)),
        ],
        cost_estimate=cost(0, 4 * math.prod(whole)),
        compiler_params=params(8),
        name="gather_blocks",
    )(table, order, *in_hbm(pool), *after)


def place_body(offsets, first, planes, together, filled, *rest):
    out, held, loaded, stored = rest[-4:]
    received = rest[1:] if filled else rest
    me = lax.axis_index("req")
    for at, offset in enumerate(offsets):
        source = me ^ offset
        piece = received[0].at[source] if together else received[at]
        pltpu.make_async_copy(piece, held.at[:, :, :, source], loaded).start()
    pltpu.make_async_copy(held, held, loaded).wait()
    store = pltpu.make_async_copy(held, out.at[pl.ds(first, planes)], stored)
    store.start()
    store.wait()


def place(shape, offsets, first, planes, together, received, filled=None, after=(), weight=1):
    start = [] if filled is None else [filled]
    dtype = received[0].dtype
    return pl.pallas_call(
        functools.partial(place_body, offsets, first, planes, together, filled is not None),
        in_specs=[ANY] * (len(start) + len(received) + len(after)),
        out_specs=ANY,
        out_shape=pltpu.HBM(shape, dtype),
        scratch_shapes=[
            pltpu.VMEM((planes,) + shape[1:], dtype),
            pltpu.SemaphoreType.DMA,
            pltpu.SemaphoreType.DMA,
        ],
        input_output_aliases={} if filled is None else {0: 0},
        cost_estimate=pl.CostEstimate(flops=weight, bytes_accessed=weight, transcendentals=0),
        compiler_params=params(8),
        name="place_blocks",
    )(*start, *received, *after)


def hold_body(*refs):
    pass


def hold(values, after):
    return pl.pallas_call(
        hold_body,
        in_specs=[ANY] * (len(values) + len(after)),
        out_specs=[ANY] * len(values),
        out_shape=[pltpu.HBM(value.shape, value.dtype) for value in values],
        input_output_aliases={at: at for at in range(len(values))},
        cost_estimate=cost(0, 0),
        compiler_params=params(1),
        name="hold",
    )(*in_hbm(*values), *after)


def turned(values, cosine, sine):
    heads = []
    for head in range(values.shape[1] // HD):
        part = values[:, head * HD : (head + 1) * HD]
        heads.append(part * cosine + pltpu.roll(part, HD // 2, 1) * sine)
    return jnp.concatenate(heads, axis=1)


def as_lanes(*columns):
    rows = columns[0].shape[0]
    lane = lax.broadcasted_iota(jnp.int32, (rows, HD), 1)
    spread = jnp.zeros((rows, HD), jnp.float32)
    for at, column in enumerate(columns):
        spread = jnp.where(lane == at, column, spread)
    return jnp.transpose(spread)[:8]


def as_columns(lanes):
    padded = jnp.concatenate([lanes, jnp.zeros((HD - 8, lanes.shape[1]), jnp.float32)], axis=0)
    return jnp.transpose(padded)


def request_length(which, per_device, order, lengths):
    return lengths[order[lax.axis_index("req") * per_device + which]]


def project_body(per_device, block, after, order, lengths, frequency, steps, gain, x, w, *rest):
    q_out, k_out, v_out, squares, x_held, w_held, x_loaded, w_loaded = rest[after:]
    rows = x.shape[0]
    span = rows // per_device
    w_loads = [
        pltpu.make_async_copy(w.at[which], w_held.at[which], w_loaded.at[which]) for which in range(3)
    ]
    x_loads = [
        pltpu.make_async_copy(
            x.at[pl.ds(low, block)], x_held.at[pl.ds(low, block)], x_loaded.at[low // block]
        )
        for low in range(0, rows, block)
    ]
    for load in (w_loads[0], *x_loads, *w_loads[1:]):
        load.start()
    starts = []
    for p in range(per_device):
        length = request_length(p, per_device, order, lengths).astype(jnp.float32)
        angle = length * frequency[...]
        starts.append((jnp.cos(angle), jnp.sin(angle)))
    for which, out in ((0, q_out), (1, k_out), (2, v_out)):
        w_loads[which].wait()
        for low in range(0, rows, block):
            if which == 0:
                x_loads[low // block].wait()
            here = slice(low, low + block)
            raw = jnp.dot(x_held[here], w_held[which], preferred_element_type=jnp.float32)
            if which == 2:
                out[here] = raw.astype(out.dtype)
                continue
            step = slice(low % span, low % span + block)
            cos_start, sin_start = starts[low // span]
            cos_step, sin_step = steps[0, step], steps[1, step]
            cosine = cos_step * cos_start - sin_step * sin_start
            sine = sin_step * cos_start + cos_step * sin_start
            lane = lax.broadcasted_iota(jnp.int32, sine.shape, 1)
            sine = jnp.where(lane < HD // 2, -sine, sine)
            squared = raw * raw
            folded = squared[:, :HD]
            for at in range(HD, squared.shape[1], HD):
                folded += squared[:, at : at + HD]
            squares[which : which + 1, here] = jnp.sum(jnp.transpose(folded), axis=0, keepdims=True)
            out[here] = turned(raw * gain[which : which + 1].astype(jnp.float32), cosine, sine)


def project(per_device, order, lengths, x, w, gain, after=(), block=256):
    rows, depth = x.shape
    width = w.shape[2]
    span = rows // per_device
    half = rope_base ** (-np.arange(HD // 2, dtype=np.float32) * np.float32(2.0 / HD))
    frequency = np.concatenate([half, half]).astype(np.float32)[None]
    angles = np.arange(span, dtype=np.float32)[:, None] * frequency
    steps = np.stack([np.cos(angles), np.sin(angles)]).astype(np.float32)
    return pl.pallas_call(
        functools.partial(project_body, per_device, block, len(after)),
        in_specs=[SMEM, SMEM, VMEM, VMEM, VMEM, ANY, ANY] + [ANY] * len(after),
        out_specs=[VMEM] * 4,
        out_shape=[
            pltpu.VMEM((rows, width), jnp.float32),
            pltpu.VMEM((rows, width), jnp.float32),
            pltpu.VMEM((rows, width), jnp.bfloat16),
            jax.ShapeDtypeStruct((8, rows), jnp.float32),
        ],
        scratch_shapes=[
            pltpu.VMEM(x.shape, x.dtype),
            pltpu.VMEM(w.shape, w.dtype),
            pltpu.SemaphoreType.DMA((rows // block,)),
            pltpu.SemaphoreType.DMA((3,)),
        ],
        cost_estimate=cost(1, 1),
        compiler_params=params(20),
        name="project_qkv",
    )(order, lengths, jnp.asarray(frequency), jnp.asarray(steps), gain, *in_hbm(x, w), *after)


CONTRACT = (((1,), (1,)), ((), ()))


def attend_new_body(full_width, span, q_block, after, q, k, v, squares, *rest):
    q_out, mixed_out, state = rest[after:]
    heads = q.shape[1] // HD
    total = squares[0]
    for at in range(1, squares.shape[0]):
        total += squares[at]
    factors = lax.rsqrt(total / full_width + norm_eps)
    row = lax.broadcasted_iota(jnp.int32, (q_block, q_block), 0)
    column = lax.broadcasted_iota(jnp.int32, (q_block, q_block), 1)
    for base in range(0, q.shape[0], span):
        here = slice(base, base + span)
        scales = as_columns(factors[:, here])
        q_scale = scales[:, 0:1] * (HD**-0.5 * math.log2(math.e))
        k_scale = scales[:, 1:2]
        for head in range(heads):
            columns = slice(head * HD, (head + 1) * HD)
            queries = (q[here, columns] * q_scale).astype(jnp.bfloat16)
            keys = (k[here, columns] * k_scale).astype(jnp.bfloat16)
            values = jnp.transpose(v[here, columns])
            q_out[here, columns] = queries
            for low in range(0, span, q_block):
                high = low + q_block
                place = slice(base + low, base + high)
                part = queries[low:high]
                scores = lax.dot_general(
                    keys[low:high], part, CONTRACT, preferred_element_type=jnp.float32
                )
                scores = jnp.where(row <= column, scores, -1e30)
                top = jnp.max(scores, axis=0, keepdims=True)
                if low:
                    full = lax.dot_general(
                        keys[:low], part, CONTRACT, preferred_element_type=jnp.float32
                    )
                    top = jnp.maximum(top, jnp.max(full, axis=0, keepdims=True))
                scores = jnp.exp2(scores - top)
                total = jnp.sum(scores, axis=0, keepdims=True)
                mixed = jnp.dot(
                    values[:, low:high],
                    scores.astype(jnp.bfloat16),
                    preferred_element_type=jnp.float32,
                )
                if low:
                    full = jnp.exp2(full - top)
                    total += jnp.sum(full, axis=0, keepdims=True)
                    mixed += jnp.dot(
                        values[:, :low],
                        full.astype(jnp.bfloat16),
                        preferred_element_type=jnp.float32,
                    )
                mixed_out[columns, place] = mixed
                state[head : head + 1, place] = top
                state[heads + head : heads + head + 1, place] = total


def attend_new(full_width, span, q, k, v, squares, after=(), q_block=256):
    rows, width = q.shape
    q_block = min(q_block, span)
    stats = 2 * (width // HD)
    return pl.pallas_call(
        functools.partial(attend_new_body, full_width, span, q_block, len(after)),
        in_specs=[VMEM] * 4 + [ANY] * len(after),
        out_specs=[VMEM] * 3,
        out_shape=[
            pltpu.VMEM((rows, width), jnp.bfloat16),
            pltpu.VMEM((width, rows), jnp.float32),
            pltpu.VMEM((stats, rows), jnp.float32),
        ],
        cost_estimate=cost(1, 1),
        compiler_params=params(16),
        name="attend_new",
    )(*in_vmem(q, k, v), squares, *after)


def attend_old_body(which, span, offsets, q_block, filled, after, order, lengths, q, mixed, state, w, *rest):
    received, rest = rest[: len(offsets)], rest[len(offsets) :]
    rest = rest[int(filled) + after :]
    relaid, outs = rest[0], rest[1:-6]
    held, w_held, attended, loaded, w_loaded, stored = rest[-6:]
    me = lax.axis_index("req")
    for at, offset in enumerate(offsets):
        pltpu.make_async_copy(received[at].at[:, which], held.at[:, :, me ^ offset], loaded).start()
    w_load = pltpu.make_async_copy(w, w_held, w_loaded)
    w_load.start()
    pltpu.make_async_copy(held, held, loaded).wait()
    store = pltpu.make_async_copy(held, relaid.at[pl.ds(0, held.shape[0]), which], stored)
    store.start()
    context = math.prod(held.shape[1:4])
    length = request_length(which, q.shape[0] // span, order, lengths)
    live = lax.broadcasted_iota(jnp.int32, (context, q_block), 0) < length
    heads = q.shape[1] // HD
    for head in range(heads):
        columns = slice(head * HD, (head + 1) * HD)
        keys = held[0, :, :, :, columns].reshape(context, HD)
        values = jnp.transpose(held[1, :, :, :, columns].reshape(context, HD))
        for low in range(0, span, q_block):
            rows = slice(which * span + low, which * span + low + q_block)
            scores = lax.dot_general(
                keys, q[rows, columns], CONTRACT, preferred_element_type=jnp.float32
            )
            scores = jnp.where(live, scores, -1e30)
            before = state[head : head + 1, rows]
            top = jnp.maximum(before, jnp.max(scores, axis=0, keepdims=True))
            scores = jnp.exp2(scores - top)
            shrink = jnp.exp2(before - top)
            total = state[heads + head : heads + head + 1, rows] * shrink
            total += jnp.sum(scores, axis=0, keepdims=True)
            sums = mixed[columns, rows] * shrink
            sums += jnp.dot(values, scores.astype(jnp.bfloat16), preferred_element_type=jnp.float32)
            attended[low : low + q_block, columns] = jnp.transpose((sums / total)).astype(attended.dtype)
    w_load.wait()
    width = w.shape[1] // len(outs)
    mine = lax.axis_index("tensor")
    for at, out in enumerate(outs):
        group = pl.ds(pl.multiple_of((mine ^ at) * width, width), width)
        out[...] = jnp.dot(
            attended[...], w_held[:, group], preferred_element_type=jnp.float32
        ).astype(out.dtype)
    store.wait()


def attend_old(
    which,
    span,
    order,
    lengths,
    q,
    mixed,
    state,
    w,
    count,
    offsets,
    received,
    shape,
    filled=None,
    after=(),
    weight=1,
    q_block=256,
):
    width = q.shape[1]
    q_block = min(q_block, span)
    start = [] if filled is None else [filled]
    part = w.shape[1] // count
    dtype = received[0].dtype
    return pl.pallas_call(
        functools.partial(
            attend_old_body, which, span, offsets, q_block, filled is not None, len(after)
        ),
        in_specs=[SMEM, SMEM, VMEM, VMEM, VMEM] + [ANY] * (1 + len(received) + len(start) + len(after)),
        out_specs=[ANY] + [VMEM] * count,
        out_shape=[pltpu.HBM(shape, dtype)] + [pltpu.VMEM((span, part), jnp.bfloat16)] * count,
        scratch_shapes=[
            pltpu.VMEM(received[0].shape[:1] + shape[2:], dtype),
            pltpu.VMEM(w.shape, w.dtype),
            pltpu.VMEM((span, width), jnp.bfloat16),
            pltpu.SemaphoreType.DMA,
            pltpu.SemaphoreType.DMA,
            pltpu.SemaphoreType.DMA,
        ],
        input_output_aliases={} if filled is None else {6 + len(received): 0},
        cost_estimate=pl.CostEstimate(flops=weight, bytes_accessed=weight, transcendentals=0),
        compiler_params=params(16),
        name="attend_old",
    )(order, lengths, *in_vmem(q, mixed, state), *in_hbm(w), *received, *start, *after)


def add_body(first, second, *rest):
    out = rest[-1]
    out[...] = (first[...].astype(jnp.float32) + second[...].astype(jnp.float32)).astype(out.dtype)


def add(first, second, after=()):
    return pl.pallas_call(
        add_body,
        in_specs=[VMEM, VMEM] + [ANY] * len(after),
        out_specs=VMEM,
        out_shape=pltpu.VMEM(first.shape, first.dtype),
        cost_estimate=cost(1, 1),
        compiler_params=params(4),
        name="add_terms",
    )(*in_vmem(first, second), *after)


def total_body(which, first, second, third, *rest):
    out, squares = rest[-2:]
    total = first[...].astype(jnp.float32) + second[...].astype(jnp.float32)
    total += third[...].astype(jnp.float32)
    out[...] = total
    squared = total * total
    folded = squared[:, :HD]
    for at in range(HD, squared.shape[1], HD):
        folded += squared[:, at : at + HD]
    sums = jnp.sum(jnp.transpose(folded), axis=0, keepdims=True)
    if len(rest) == 3:
        squares[...] = rest[0][...]
    else:
        squares[...] = jnp.zeros(squares.shape, jnp.float32)
    squares[which : which + 1] = sums


def total_of(which, first, second, third, squares=()):
    rows, width = first.shape
    return pl.pallas_call(
        functools.partial(total_body, which),
        in_specs=[VMEM] * (3 + len(squares)),
        out_specs=[VMEM, VMEM],
        out_shape=[
            pltpu.VMEM((rows, width), jnp.float32),
            jax.ShapeDtypeStruct((8, rows), jnp.float32),
        ],
        cost_estimate=cost(1, 1),
        compiler_params=params(8),
        name="total_terms",
    )(*in_vmem(first, second, third), *squares)


def finish_body(full_width, residual, squares, gain, *rest):
    totals = rest[: len(rest) - 5]
    out, res_held, out_held, loaded, stored = rest[len(rest) - 5 :]
    per_device, span, width = out.shape
    start = pl.multiple_of(lax.axis_index("tensor") * width, width)
    loads = [
        pltpu.make_async_copy(residual.at[p, :, pl.ds(start, width)], res_held.at[p], loaded.at[p])
        for p in range(per_device)
    ]
    for load in loads:
        load.start()
    total = squares[0]
    for at in range(1, squares.shape[0]):
        total += squares[at]
    scales = as_columns(lax.rsqrt(total / full_width + norm_eps))
    stores = []
    for p in range(per_device):
        normed = totals[p][...] * scales[:, p : p + 1] * gain[...].astype(jnp.float32)
        loads[p].wait()
        out_held[p] = (res_held[p].astype(jnp.float32) + normed).astype(out.dtype)
        stores.append(pltpu.make_async_copy(out_held.at[p], out.at[p], stored.at[p]))
        stores[-1].start()
    for store in stores:
        store.wait()


def finish(residual, totals, squares, gain):
    per_device, span, full_width = residual.shape
    width = totals[0].shape[1]
    shape = (per_device, span, width)
    return pl.pallas_call(
        functools.partial(finish_body, full_width),
        in_specs=[ANY] + [VMEM] * (2 + per_device),
        out_specs=ANY,
        out_shape=pltpu.HBM(shape, residual.dtype),
        scratch_shapes=[
            pltpu.VMEM(shape, residual.dtype),
            pltpu.VMEM(shape, residual.dtype),
            pltpu.SemaphoreType.DMA((per_device,)),
            pltpu.SemaphoreType.DMA((per_device,)),
        ],
        cost_estimate=cost(1, 1),
        compiler_params=params(12),
        name="finish_layer",
    )(*in_hbm(residual), squares, gain.reshape(1, width), *in_vmem(*totals))


def permuted(value, axis, offset):
    size = lax.axis_size(axis)
    return lax.ppermute(value, axis, [(i, i ^ offset) for i in range(size)])


def on_device(
    span_in, w_qkv, qk_gain, w_out, post_gain, kv_pool, block_table, request_order, lengths
):
    req_count = lax.axis_size("req")
    tensor_count = lax.axis_size("tensor")
    per_device, span_len, full_width = span_in.shape
    part_width = w_qkv.shape[2]
    planes = kv_pool.shape[0]
    hand = functools.partial(gather, kv_pool, block_table, request_order, req_count)
    shape = (planes, per_device, block_table.shape[1] // req_count, req_count) + kv_pool.shape[2:]

    early = [s for s in range(req_count - 1, 0, -1) if s not in LATE]
    late = [s for s in range(req_count - 1, 0, -1) if s in LATE]
    own, *sent = hand([0] + early + late, 0, 2, False)
    sent_late = sent[len(early) :]
    received = [permuted(piece, "req", s) for piece, s in zip(sent, early)]

    flat_in = span_in.reshape(-1, full_width)
    q_raw, k_raw, values, squares = project(
        per_device, request_order, lengths, flat_in, w_qkv, qk_gain, after=(own,)
    )
    squares = lax.all_gather(squares, "tensor")
    sent_late = hold(sent_late, (q_raw,))
    received += [permuted(piece, "req", s) for piece, s in zip(sent_late, late)]

    rest = planes - 2
    everyone = list(range(req_count))
    (sent_rest,) = hand(everyone, 2, rest, True, after=(own,))
    (sent_rest,) = hold((sent_rest,), (squares, *received[: len(early)]))
    received_rest = lax.all_to_all(sent_rest, "req", 0, 0)

    queries, mixed, state = attend_new(
        full_width, span_len, q_raw, k_raw, values, squares, after=(sent_rest,)
    )
    relaid, across, added, totals, row_squares = None, (), (), [], ()
    for p in range(per_device):
        relaid, *terms = attend_old(
            p,
            span_len,
            request_order,
            lengths,
            queries,
            mixed,
            state,
            w_out,
            tensor_count,
            [0] + early + late,
            [own] + received,
            shape,
            filled=relaid,
            after=(sent_rest, *added),
            weight=1 if p else 10**12,
        )
        far = permuted(terms[3], "tensor", 1)
        near = permuted(terms[1], "tensor", 1)
        added = [add(terms[2], far, after=across)]
        across = [permuted(added[0], "tensor", 2)]
        total, *row_squares = total_of(p, terms[0], near, across[0], row_squares)
        totals.append(total)
    row_squares = lax.all_gather(row_squares[0], "tensor")
    layer_out = finish(span_in, totals, row_squares, post_gain)

    relaid = place(shape, everyone, 2, rest, True, [received_rest], filled=relaid)
    return layer_out, relaid.reshape(planes, per_device, -1, part_width)


def solution(mesh):
    placed = (
        P("req", None, None),
        P(None, None, "tensor"),
        P(None, "tensor"),
        P("tensor", None),
        P("tensor"),
        P(None, "req", None, "tensor"),
        P(),
        P(),
        P(),
    )
    return jax.shard_map(
        on_device,
        mesh=mesh,
        in_specs=placed,
        out_specs=(P("req", None, "tensor"), P(None, "req", None, "tensor")),
        check_vma=False,
    )
```

```python
import functools
import math

import jax
import jax.numpy as jnp
import numpy as np
from jax import lax
from jax.experimental import pallas as pl
from jax.experimental.pallas import tpu as pltpu
from jax.sharding import PartitionSpec as P

HD = 128
norm_eps = 1e-06
rope_base = 500000.0
LATE = (4, 1)

ANY = pl.BlockSpec(memory_space=pl.ANY)
SMEM = pl.BlockSpec(memory_space=pltpu.SMEM)
VMEM = pl.BlockSpec(memory_space=pltpu.VMEM)


def cost(flops, moved, exps=0):
    return pl.CostEstimate(flops=1, bytes_accessed=1, transcendentals=0)


def params(mib=60):
    return pltpu.CompilerParams(vmem_limit_bytes=mib << 20)


def in_vmem(*arrays):
    return [pltpu.with_memory_space_constraint(array, pltpu.VMEM) for array in arrays]


def in_hbm(*arrays):
    return [pltpu.with_memory_space_constraint(array, pltpu.HBM) for array in arrays]


def gather_body(targets, first, planes, count, per_device, blocks, together, table, order, pool, *rest):
    if together:
        out, held, stored, loaded = rest[-4:]
        places = [held.at[at] for at in range(len(targets))]
    else:
        places, loaded = rest[-1 - len(targets) : -1], rest[-1]
    me = lax.axis_index("req")
    for at, target in enumerate(targets):
        if not together:
            target = me ^ target
        for p in range(per_device):
            request = order[target * per_device + p]
            for b in range(blocks):
                slot = table[request, b * count + me]
                pltpu.make_async_copy(
                    pool.at[pl.ds(first, planes), slot], places[at].at[:, p, b], loaded.at[at]
                ).start()
    stores = []
    for at, place in enumerate(places):
        pltpu.make_async_copy(place, place, loaded.at[at]).wait()
        if together:
            stores.append(pltpu.make_async_copy(place, out.at[at], stored.at[at]))
            stores[-1].start()
    for store in stores:
        store.wait()


def gather(pool, table, order, count, targets, first, planes, together, after=()):
    per_device = order.shape[0] // count
    blocks = table.shape[1] // count
    piece = (planes, per_device, blocks) + pool.shape[2:]
    whole = (len(targets),) + piece
    if together:
        shapes = [pltpu.HBM(whole, pool.dtype)]
        staging = [pltpu.VMEM(whole, pool.dtype), pltpu.SemaphoreType.DMA((len(targets),))]
    else:
        shapes = [pltpu.VMEM(piece, pool.dtype)] * len(targets)
        staging = []
    return pl.pallas_call(
        functools.partial(gather_body, targets, first, planes, count, per_device, blocks, together),
        in_specs=[SMEM, SMEM, ANY] + [ANY] * len(after),
        out_specs=[ANY if together else VMEM] * len(shapes),
        out_shape=shapes,
        scratch_shapes=staging + [pltpu.SemaphoreType.DMA((len(targets),))],
        cost_estimate=cost(0, 4 * math.prod(whole)),
        compiler_params=params(8),
        name="gather_blocks",
    )(*in_hbm(table, order, pool), *after)


def place_body(offsets, first, planes, together, filled, *rest):
    out, held, loaded, stored = rest[-4:]
    received = rest[1:] if filled else rest
    me = lax.axis_index("req")
    for at, offset in enumerate(offsets):
        source = me ^ offset
        piece = received[0].at[source] if together else received[at]
        pltpu.make_async_copy(piece, held.at[:, :, :, source], loaded).start()
    pltpu.make_async_copy(held, held, loaded).wait()
    store = pltpu.make_async_copy(held, out.at[pl.ds(first, planes)], stored)
    store.start()
    store.wait()


def place(shape, offsets, first, planes, together, received, filled=None, after=(), weight=1):
    start = [] if filled is None else [filled]
    dtype = received[0].dtype
    return pl.pallas_call(
        functools.partial(place_body, offsets, first, planes, together, filled is not None),
        in_specs=[ANY] * (len(start) + len(received) + len(after)),
        out_specs=ANY,
        out_shape=pltpu.HBM(shape, dtype),
        scratch_shapes=[
            pltpu.VMEM((planes,) + shape[1:], dtype),
            pltpu.SemaphoreType.DMA,
            pltpu.SemaphoreType.DMA,
        ],
        input_output_aliases={} if filled is None else {0: 0},
        cost_estimate=pl.CostEstimate(flops=weight, bytes_accessed=weight, transcendentals=0),
        compiler_params=params(8),
        name="place_blocks",
    )(*start, *received, *after)


def hold_body(*refs):
    pass


def hold(values, after, pin=pltpu.HBM):
    return pl.pallas_call(
        hold_body,
        in_specs=[ANY] * (len(values) + len(after)),
        out_specs=[ANY] * len(values),
        out_shape=[pin(value.shape, value.dtype) for value in values],
        input_output_aliases={at: at for at in range(len(values))},
        cost_estimate=cost(0, 0),
        compiler_params=params(1),
        name="hold",
    )(*[pltpu.with_memory_space_constraint(value, pin) for value in values], *after)


def turned(values, cosine, sine):
    heads = []
    for head in range(values.shape[1] // HD):
        part = values[:, head * HD : (head + 1) * HD]
        heads.append(part * cosine + pltpu.roll(part, HD // 2, 1) * sine)
    return jnp.concatenate(heads, axis=1)


def as_lanes(*columns):
    rows = columns[0].shape[0]
    lane = lax.broadcasted_iota(jnp.int32, (rows, HD), 1)
    spread = jnp.zeros((rows, HD), jnp.float32)
    for at, column in enumerate(columns):
        spread = jnp.where(lane == at, column, spread)
    return jnp.transpose(spread)[:8]


def as_columns(lanes):
    padded = jnp.concatenate([lanes, jnp.zeros((HD - 8, lanes.shape[1]), jnp.float32)], axis=0)
    return jnp.transpose(padded)


def request_length(which, per_device, order, lengths):
    return lengths[order[lax.axis_index("req") * per_device + which]]


def project_body(per_device, block, after, order, lengths, frequency, steps, gain, x, w, *rest):
    outs, squares, x_held, w_held, *rest = rest[after : after + 3], *rest[after + 3 :]
    helds, (x_loaded, w_loaded, stored) = rest[:3], rest[3:]
    stores = []
    rows = x.shape[0]
    span = rows // per_device
    w_loads = [
        pltpu.make_async_copy(w.at[which], w_held.at[which], w_loaded.at[which]) for which in range(3)
    ]
    x_loads = [
        pltpu.make_async_copy(
            x.at[pl.ds(low, block)], x_held.at[pl.ds(low, block)], x_loaded.at[low // block]
        )
        for low in range(0, rows, block)
    ]
    for load in (w_loads[0], *x_loads, *w_loads[1:]):
        load.start()
    starts = []
    for p in range(per_device):
        length = request_length(p, per_device, order, lengths).astype(jnp.float32)
        angle = length * frequency[...]
        starts.append((jnp.cos(angle), jnp.sin(angle)))
        squares[2:3, p * span : (p + 1) * span] = jnp.full((1, span), length)
    for which, out in enumerate(helds):
        w_loads[which].wait()
        for low in range(0, rows, block):
            if which == 0:
                x_loads[low // block].wait()
            here = slice(low, low + block)
            raw = jnp.dot(x_held[here], w_held[which], preferred_element_type=jnp.float32)
            if which == 2:
                out[here] = raw.astype(out.dtype)
                continue
            step = slice(low % span, low % span + block)
            cos_start, sin_start = starts[low // span]
            cos_step, sin_step = steps[0, step], steps[1, step]
            cosine = cos_step * cos_start - sin_step * sin_start
            sine = sin_step * cos_start + cos_step * sin_start
            lane = lax.broadcasted_iota(jnp.int32, sine.shape, 1)
            sine = jnp.where(lane < HD // 2, -sine, sine)
            squared = raw * raw
            folded = squared[:, :HD]
            for at in range(HD, squared.shape[1], HD):
                folded += squared[:, at : at + HD]
            squares[which : which + 1, here] = jnp.sum(jnp.transpose(folded), axis=0, keepdims=True)
            out[here] = turned(raw * gain[which : which + 1].astype(jnp.float32), cosine, sine)
        stores.append(pltpu.make_async_copy(out, outs[which], stored.at[which]))
        stores[-1].start()
    for store in stores:
        store.wait()


def project(per_device, order, lengths, x, w, gain, after=(), block=256):
    rows, depth = x.shape
    width = w.shape[2]
    span = rows // per_device
    half = rope_base ** (-np.arange(HD // 2, dtype=np.float32) * np.float32(2.0 / HD))
    frequency = np.concatenate([half, half]).astype(np.float32)[None]
    angles = np.arange(span, dtype=np.float32)[:, None] * frequency
    steps = np.stack([np.cos(angles), np.sin(angles)]).astype(np.float32)
    return pl.pallas_call(
        functools.partial(project_body, per_device, block, len(after)),
        in_specs=[SMEM, SMEM, VMEM, VMEM, VMEM, ANY, ANY] + [ANY] * len(after),
        out_specs=[ANY] * 3 + [VMEM],
        out_shape=[
            pltpu.HBM((rows, width), jnp.float32),
            pltpu.HBM((rows, width), jnp.float32),
            pltpu.HBM((rows, width), jnp.bfloat16),
            jax.ShapeDtypeStruct((8, rows), jnp.float32),
        ],
        scratch_shapes=[
            pltpu.VMEM(x.shape, x.dtype),
            pltpu.VMEM(w.shape, w.dtype),
            pltpu.VMEM((rows, width), jnp.float32),
            pltpu.VMEM((rows, width), jnp.float32),
            pltpu.VMEM((rows, width), jnp.bfloat16),
            pltpu.SemaphoreType.DMA((rows // block,)),
            pltpu.SemaphoreType.DMA((3,)),
            pltpu.SemaphoreType.DMA((3,)),
        ],
        cost_estimate=cost(1, 1),
        compiler_params=params(24),
        name="project_qkv",
    )(*in_hbm(order, lengths), jnp.asarray(frequency), jnp.asarray(steps), gain, *in_hbm(x, w), *after)


CONTRACT = (((1,), (1,)), ((), ()))


def attend_new_body(full_width, span, q_block, after, squares, *rest):
    sources, rest = rest[:3], rest[3 + after :]
    q_final, mixed_final, state, *helds, q_out, mixed_out, loaded, stored = rest
    q, k, v = helds
    stores = []
    heads = q.shape[1] // HD
    loads = []
    for base in range(0, q.shape[0], span):
        at = pl.ds(base, span)
        number = base // span
        loads.append(
            [
                pltpu.make_async_copy(source.at[at], held.at[at], loaded.at[number, which])
                for which, (source, held) in enumerate(zip(sources, helds))
            ]
        )
        for load in loads[-1]:
            load.start()
    state[2 * heads : 2 * heads + 1] = squares[0, 2:3]
    total = squares[0]
    for at in range(1, squares.shape[0]):
        total += squares[at]
    factors = lax.rsqrt(total / full_width + norm_eps)
    row = lax.broadcasted_iota(jnp.int32, (q_block, q_block), 0)
    column = lax.broadcasted_iota(jnp.int32, (q_block, q_block), 1)
    for base in range(0, q.shape[0], span):
        here = slice(base, base + span)
        scales = as_columns(factors[:, here])
        q_scale = scales[:, 0:1] * (HD**-0.5 * math.log2(math.e))
        k_scale = scales[:, 1:2]
        for load in loads[base // span]:
            load.wait()
        for head in range(heads):
            columns = slice(head * HD, (head + 1) * HD)
            queries = (q[here, columns] * q_scale).astype(jnp.bfloat16)
            keys = (k[here, columns] * k_scale).astype(jnp.bfloat16)
            values = jnp.transpose(v[here, columns])
            q_out[here, columns] = queries
            for low in range(0, span, q_block):
                high = low + q_block
                place = slice(base + low, base + high)
                part = queries[low:high]
                scores = lax.dot_general(
                    keys[low:high], part, CONTRACT, preferred_element_type=jnp.float32
                )
                scores = jnp.where(row <= column, scores, -1e30)
                top = jnp.max(scores, axis=0, keepdims=True)
                if low:
                    full = lax.dot_general(
                        keys[:low], part, CONTRACT, preferred_element_type=jnp.float32
                    )
                    top = jnp.maximum(top, jnp.max(full, axis=0, keepdims=True))
                scores = jnp.exp2(scores - top)
                total = jnp.sum(scores, axis=0, keepdims=True)
                mixed = jnp.dot(
                    values[:, low:high],
                    scores.astype(jnp.bfloat16),
                    preferred_element_type=jnp.float32,
                )
                if low:
                    full = jnp.exp2(full - top)
                    total += jnp.sum(full, axis=0, keepdims=True)
                    mixed += jnp.dot(
                        values[:, :low],
                        full.astype(jnp.bfloat16),
                        preferred_element_type=jnp.float32,
                    )
                mixed_out[base // span, columns, low:high] = mixed
                state[head : head + 1, place] = top
                state[heads + head : heads + head + 1, place] = total
        for at, (held, final) in enumerate(((q_out.at[here], q_final.at[here]), (mixed_out.at[base // span], mixed_final.at[base // span]))):
            stores.append(pltpu.make_async_copy(held, final, stored.at[base // span, at]))
            stores[-1].start()
    for store in stores:
        store.wait()


def attend_new(full_width, span, q, k, v, squares, after=(), q_block=256):
    rows, width = q.shape
    q_block = min(q_block, span)
    stats = 2 * (width // HD) + 8
    return pl.pallas_call(
        functools.partial(attend_new_body, full_width, span, q_block, len(after)),
        in_specs=[VMEM] + [ANY] * (3 + len(after)),
        out_specs=[ANY, ANY, VMEM],
        out_shape=[
            pltpu.HBM((rows, width), jnp.bfloat16),
            pltpu.HBM((rows // span, width, span), jnp.float32),
            jax.ShapeDtypeStruct((stats, rows), jnp.float32),
        ],
        scratch_shapes=[
            pltpu.VMEM(q.shape, q.dtype),
            pltpu.VMEM(k.shape, k.dtype),
            pltpu.VMEM(v.shape, v.dtype),
            pltpu.VMEM((rows, width), jnp.bfloat16),
            pltpu.VMEM((rows // span, width, span), jnp.float32),
            pltpu.SemaphoreType.DMA((rows // span, 3)),
            pltpu.SemaphoreType.DMA((rows // span, 2)),
        ],
        cost_estimate=cost(1, 1),
        compiler_params=params(20),
        name="attend_new",
    )(squares, *in_hbm(q, k, v), *after)


def attend_old_body(which, span, offsets, q_block, filled, after, state, q_all, mixed_all, w, *rest):
    received, rest = rest[: len(offsets)], rest[len(offsets) + int(filled) + after :]
    relaid, outs = rest[0], rest[1:-9]
    held, q, mixed, w_held, attended, loaded, q_loaded, w_loaded, stored = rest[-9:]
    me = lax.axis_index("req")
    q_load = pltpu.make_async_copy(q_all.at[pl.ds(which * span, span)], q, q_loaded.at[0])
    mixed_load = pltpu.make_async_copy(mixed_all.at[which], mixed, q_loaded.at[1])
    w_load = pltpu.make_async_copy(w, w_held, w_loaded)
    q_load.start()
    for plane in range(held.shape[0]):
        for at, offset in enumerate(offsets):
            pltpu.make_async_copy(
                received[at].at[plane, which], held.at[plane, :, me ^ offset], loaded.at[plane]
            ).start()
    mixed_load.start()
    w_load.start()
    q_load.wait()
    for plane in range(held.shape[0]):
        pltpu.make_async_copy(held.at[plane], held.at[plane], loaded.at[plane]).wait()
    mixed_load.wait()
    store = pltpu.make_async_copy(held, relaid.at[pl.ds(0, held.shape[0]), which], stored)
    store.start()
    context = math.prod(held.shape[1:4])
    token = lax.broadcasted_iota(jnp.int32, (context, q_block), 0).astype(jnp.float32)
    heads = q.shape[1] // HD
    live = token < state[2 * heads : 2 * heads + 1, which * span : which * span + q_block]
    for head in range(heads):
        columns = slice(head * HD, (head + 1) * HD)
        keys = held[0, :, :, :, columns].reshape(context, HD)
        values = jnp.transpose(held[1, :, :, :, columns].reshape(context, HD))
        for low in range(0, span, q_block):
            rows = slice(which * span + low, which * span + low + q_block)
            scores = lax.dot_general(
                keys, q[low : low + q_block, columns], CONTRACT, preferred_element_type=jnp.float32
            )
            scores = jnp.where(live, scores, -1e30)
            before = state[head : head + 1, rows]
            top = jnp.maximum(before, jnp.max(scores, axis=0, keepdims=True))
            scores = jnp.exp2(scores - top)
            shrink = jnp.exp2(before - top)
            total = state[heads + head : heads + head + 1, rows] * shrink
            total += jnp.sum(scores, axis=0, keepdims=True)
            sums = mixed[columns, low : low + q_block] * shrink
            sums += jnp.dot(values, scores.astype(jnp.bfloat16), preferred_element_type=jnp.float32)
            attended[low : low + q_block, columns] = jnp.transpose((sums / total)).astype(attended.dtype)
    w_load.wait()
    width = w.shape[1] // len(outs)
    mine = lax.axis_index("tensor")
    for at, out in enumerate(outs):
        group = pl.ds(pl.multiple_of((mine ^ at) * width, width), width)
        out[...] = jnp.dot(
            attended[...], w_held[:, group], preferred_element_type=jnp.float32
        ).astype(out.dtype)
    store.wait()


def attend_old(
    which,
    span,
    q,
    mixed,
    state,
    w,
    count,
    offsets,
    received,
    shape,
    filled=None,
    after=(),
    weight=1,
    q_block=256,
):
    width = q.shape[1]
    q_block = min(q_block, span)
    start = [] if filled is None else [filled]
    part = w.shape[1] // count
    dtype = received[0].dtype
    return pl.pallas_call(
        functools.partial(
            attend_old_body, which, span, offsets, q_block, filled is not None, len(after)
        ),
        in_specs=[VMEM] + [ANY] * (3 + len(received) + len(start) + len(after)),
        out_specs=[ANY] + [VMEM] * count,
        out_shape=[pltpu.HBM(shape, dtype)] + [pltpu.VMEM((span, part), jnp.bfloat16)] * count,
        scratch_shapes=[
            pltpu.VMEM(received[0].shape[:1] + shape[2:], dtype),
            pltpu.VMEM((span, width), q.dtype),
            pltpu.VMEM((width, span), mixed.dtype),
            pltpu.VMEM(w.shape, w.dtype),
            pltpu.VMEM((span, width), jnp.bfloat16),
            pltpu.SemaphoreType.DMA((received[0].shape[0],)),
            pltpu.SemaphoreType.DMA((2,)),
            pltpu.SemaphoreType.DMA,
            pltpu.SemaphoreType.DMA,
        ],
        input_output_aliases={} if filled is None else {4 + len(received): 0},
        cost_estimate=pl.CostEstimate(flops=weight, bytes_accessed=weight, transcendentals=0),
        compiler_params=params(16),
        name="attend_old",
    )(state, *in_hbm(q, mixed, w), *received, *start, *after)


def add_body(first, second, *rest):
    out = rest[-1]
    out[...] = (first[...].astype(jnp.float32) + second[...].astype(jnp.float32)).astype(out.dtype)


def add(first, second, after=()):
    return pl.pallas_call(
        add_body,
        in_specs=[VMEM, VMEM] + [ANY] * len(after),
        out_specs=VMEM,
        out_shape=pltpu.VMEM(first.shape, first.dtype),
        cost_estimate=cost(1, 1),
        compiler_params=params(4),
        name="add_terms",
    )(*in_vmem(first, second), *after)


def total_body(which, first, second, third, *rest):
    out, squares = rest[-2:]
    total = first[...].astype(jnp.float32) + second[...].astype(jnp.float32)
    total += third[...].astype(jnp.float32)
    out[...] = total
    squared = total * total
    folded = squared[:, :HD]
    for at in range(HD, squared.shape[1], HD):
        folded += squared[:, at : at + HD]
    sums = jnp.sum(jnp.transpose(folded), axis=0, keepdims=True)
    if len(rest) == 3:
        squares[...] = rest[0][...]
    else:
        squares[...] = jnp.zeros(squares.shape, jnp.float32)
    squares[which : which + 1] = sums


def total_of(which, first, second, third, squares=()):
    rows, width = first.shape
    return pl.pallas_call(
        functools.partial(total_body, which),
        in_specs=[VMEM] * (3 + len(squares)),
        out_specs=[VMEM, VMEM],
        out_shape=[
            pltpu.VMEM((rows, width), jnp.float32),
            jax.ShapeDtypeStruct((8, rows), jnp.float32),
        ],
        cost_estimate=cost(1, 1),
        compiler_params=params(8),
        name="total_terms",
    )(*in_vmem(first, second, third), *squares)


def finish_body(full_width, count, residual, gain, *rest):
    squares, totals = rest[:count], rest[count:-5]
    out, res_held, out_held, loaded, stored = rest[-5:]
    per_device, span, width = out.shape
    start = pl.multiple_of(lax.axis_index("tensor") * width, width)
    loads = [
        pltpu.make_async_copy(residual.at[p, :, pl.ds(start, width)], res_held.at[p], loaded.at[p])
        for p in range(per_device)
    ]
    for load in loads:
        load.start()
    total = squares[0][...]
    for part in squares[1:]:
        total += part[...]
    scales = as_columns(lax.rsqrt(total / full_width + norm_eps))
    stores = []
    for p in range(per_device):
        normed = totals[p][...] * scales[:, p : p + 1] * gain[...].astype(jnp.float32)
        loads[p].wait()
        out_held[p] = (res_held[p].astype(jnp.float32) + normed).astype(out.dtype)
        stores.append(pltpu.make_async_copy(out_held.at[p], out.at[p], stored.at[p]))
        stores[-1].start()
    for store in stores:
        store.wait()


def finish(residual, totals, squares, gain):
    per_device, span, full_width = residual.shape
    width = totals[0].shape[1]
    shape = (per_device, span, width)
    return pl.pallas_call(
        functools.partial(finish_body, full_width, len(squares)),
        in_specs=[ANY] + [VMEM] * (1 + len(squares) + per_device),
        out_specs=ANY,
        out_shape=pltpu.HBM(shape, residual.dtype),
        scratch_shapes=[
            pltpu.VMEM(shape, residual.dtype),
            pltpu.VMEM(shape, residual.dtype),
            pltpu.SemaphoreType.DMA((per_device,)),
            pltpu.SemaphoreType.DMA((per_device,)),
        ],
        cost_estimate=cost(1, 1),
        compiler_params=params(12),
        name="finish_layer",
    )(*in_hbm(residual), gain.reshape(1, width), *squares, *in_vmem(*totals))


def permuted(value, axis, offset):
    size = lax.axis_size(axis)
    return lax.ppermute(value, axis, [(i, i ^ offset) for i in range(size)])


def on_device(
    span_in, w_qkv, qk_gain, w_out, post_gain, kv_pool, block_table, request_order, lengths
):
    req_count = lax.axis_size("req")
    tensor_count = lax.axis_size("tensor")
    per_device, span_len, full_width = span_in.shape
    part_width = w_qkv.shape[2]
    planes = kv_pool.shape[0]
    hand = functools.partial(gather, kv_pool, block_table, request_order, req_count)
    shape = (planes, per_device, block_table.shape[1] // req_count, req_count) + kv_pool.shape[2:]

    others = list(range(req_count - 1, 0, -1))
    early = [s for s in others if s not in LATE]
    late = [s for s in others if s in LATE]
    sent = dict(zip([0] + others, hand([0] + others, 0, 2, False)))
    received = {s: permuted(sent[s], "req", s) for s in early}
    own = received[0] = sent[0]

    flat_in = span_in.reshape(-1, full_width)
    q_raw, k_raw, values, squares = project(
        per_device, request_order, lengths, flat_in, w_qkv, qk_gain, after=(own,)
    )
    own_squares = squares
    squares = lax.all_gather(squares, "tensor")
    queries, mixed, state = attend_new(full_width, span_len, q_raw, k_raw, values, squares)
    arrived = [received[s] for s in reversed(early)]
    sent_late = hold([sent[s] for s in late], (own_squares, *arrived[:2]), pltpu.VMEM)
    received.update({s: permuted(piece, "req", s) for s, piece in zip(late, sent_late)})

    rest = planes - 2
    everyone = list(range(req_count))
    (sent_rest,) = hand(everyone, 2, rest, True, after=(own,))
    (sent_rest,) = hold((sent_rest,), (state, *arrived))
    received_rest = lax.all_to_all(sent_rest, "req", 0, 0)

    relaid, across, added, totals, row_squares = None, (), (), [], ()
    for p in range(per_device):
        relaid, *terms = attend_old(
            p,
            span_len,
            queries,
            mixed,
            state,
            w_out,
            tensor_count,
            list(received),
            list(received.values()),
            shape,
            filled=relaid,
            after=(sent_rest, *added),
            weight=1 if p else 10**12,
        )
        far = permuted(terms[3], "tensor", 1)
        near = permuted(terms[1], "tensor", 1)
        added = [add(terms[2], far, after=across)]
        across = [permuted(added[0], "tensor", 2)]
        total, *row_squares = total_of(p, terms[0], near, across[0], row_squares)
        totals.append(total)
    row_squares = row_squares + [
        permuted(row_squares[0], "tensor", at) for at in range(1, tensor_count)
    ]
    layer_out = finish(span_in, totals, row_squares, post_gain)

    relaid = place(shape, everyone, 2, rest, True, [received_rest], filled=relaid)
    return layer_out, relaid.reshape(planes, per_device, -1, part_width)


def solution(mesh):
    placed = (
        P("req", None, None),
        P(None, None, "tensor"),
        P(None, "tensor"),
        P("tensor", None),
        P("tensor"),
        P(None, "req", None, "tensor"),
        P(),
        P(),
        P(),
    )
    return jax.shard_map(
        on_device,
        mesh=mesh,
        in_specs=placed,
        out_specs=(P("req", None, "tensor"), P(None, "req", None, "tensor")),
        check_vma=False,
    )
```

```python
import functools
import math

import jax
import jax.numpy as jnp
import numpy as np
from jax import lax
from jax.experimental import pallas as pl
from jax.experimental.pallas import tpu as pltpu
from jax.sharding import PartitionSpec as P

HD = 128
norm_eps = 1e-06
rope_base = 500000.0
LATE = (5, 1)
GATE = 6

ANY = pl.BlockSpec(memory_space=pl.ANY)
SMEM = pl.BlockSpec(memory_space=pltpu.SMEM)
VMEM = pl.BlockSpec(memory_space=pltpu.VMEM)


def cost(flops, moved, exps=0):
    return pl.CostEstimate(flops=1, bytes_accessed=1, transcendentals=0)


def params(mib=60):
    return pltpu.CompilerParams(vmem_limit_bytes=mib << 20)


def in_vmem(*arrays):
    return [pltpu.with_memory_space_constraint(array, pltpu.VMEM) for array in arrays]


def in_hbm(*arrays):
    return [pltpu.with_memory_space_constraint(array, pltpu.HBM) for array in arrays]


def gather_body(targets, first, planes, count, per_device, blocks, together, table, order, pool, *rest):
    if together:
        out, held, stored, loaded = rest[-4:]
        places = [held.at[at] for at in range(len(targets))]
    else:
        places, loaded = rest[-1 - len(targets) : -1], rest[-1]
    me = lax.axis_index("req")
    for at, target in enumerate(targets):
        if not together:
            target = me ^ target
        for p in range(per_device):
            request = order[target * per_device + p]
            for b in range(blocks):
                slot = table[request, b * count + me]
                pltpu.make_async_copy(
                    pool.at[pl.ds(first, planes), slot], places[at].at[:, p, b], loaded.at[at]
                ).start()
    stores = []
    for at, place in enumerate(places):
        pltpu.make_async_copy(place, place, loaded.at[at]).wait()
        if together:
            stores.append(pltpu.make_async_copy(place, out.at[at], stored.at[at]))
            stores[-1].start()
    for store in stores:
        store.wait()


def gather(pool, table, order, count, targets, first, planes, together, after=()):
    per_device = order.shape[0] // count
    blocks = table.shape[1] // count
    piece = (planes, per_device, blocks) + pool.shape[2:]
    whole = (len(targets),) + piece
    if together:
        shapes = [pltpu.HBM(whole, pool.dtype)]
        staging = [pltpu.VMEM(whole, pool.dtype), pltpu.SemaphoreType.DMA((len(targets),))]
    else:
        shapes = [pltpu.VMEM(piece, pool.dtype)] * len(targets)
        staging = []
    return pl.pallas_call(
        functools.partial(gather_body, targets, first, planes, count, per_device, blocks, together),
        in_specs=[SMEM, SMEM, ANY] + [ANY] * len(after),
        out_specs=[ANY if together else VMEM] * len(shapes),
        out_shape=shapes,
        scratch_shapes=staging + [pltpu.SemaphoreType.DMA((len(targets),))],
        cost_estimate=cost(0, 4 * math.prod(whole)),
        compiler_params=params(8),
        name="gather_blocks",
    )(*in_hbm(table, order, pool), *after)


def place_body(offsets, first, planes, together, filled, *rest):
    out, held, loaded, stored = rest[-4:]
    received = rest[1:] if filled else rest
    me = lax.axis_index("req")
    for at, offset in enumerate(offsets):
        source = me ^ offset
        piece = received[0].at[source] if together else received[at]
        pltpu.make_async_copy(piece, held.at[:, :, :, source], loaded).start()
    pltpu.make_async_copy(held, held, loaded).wait()
    store = pltpu.make_async_copy(held, out.at[pl.ds(first, planes)], stored)
    store.start()
    store.wait()


def place(shape, offsets, first, planes, together, received, filled=None, after=(), weight=1):
    start = [] if filled is None else [filled]
    dtype = received[0].dtype
    return pl.pallas_call(
        functools.partial(place_body, offsets, first, planes, together, filled is not None),
        in_specs=[ANY] * (len(start) + len(received) + len(after)),
        out_specs=ANY,
        out_shape=pltpu.HBM(shape, dtype),
        scratch_shapes=[
            pltpu.VMEM((planes,) + shape[1:], dtype),
            pltpu.SemaphoreType.DMA,
            pltpu.SemaphoreType.DMA,
        ],
        input_output_aliases={} if filled is None else {0: 0},
        cost_estimate=pl.CostEstimate(flops=weight, bytes_accessed=weight, transcendentals=0),
        compiler_params=params(8),
        name="place_blocks",
    )(*start, *received, *after)


def hold_body(*refs):
    pass


def hold(values, after, pin=pltpu.HBM):
    return pl.pallas_call(
        hold_body,
        in_specs=[ANY] * (len(values) + len(after)),
        out_specs=[ANY] * len(values),
        out_shape=[pin(value.shape, value.dtype) for value in values],
        input_output_aliases={at: at for at in range(len(values))},
        cost_estimate=cost(0, 0),
        compiler_params=params(1),
        name="hold",
    )(*[pltpu.with_memory_space_constraint(value, pin) for value in values], *after)


def turned(values, cosine, sine):
    heads = []
    for head in range(values.shape[1] // HD):
        part = values[:, head * HD : (head + 1) * HD]
        heads.append(part * cosine + pltpu.roll(part, HD // 2, 1) * sine)
    return jnp.concatenate(heads, axis=1)


def as_lanes(*columns):
    rows = columns[0].shape[0]
    lane = lax.broadcasted_iota(jnp.int32, (rows, HD), 1)
    spread = jnp.zeros((rows, HD), jnp.float32)
    for at, column in enumerate(columns):
        spread = jnp.where(lane == at, column, spread)
    return jnp.transpose(spread)[:8]


def as_columns(lanes):
    padded = jnp.concatenate([lanes, jnp.zeros((HD - 8, lanes.shape[1]), jnp.float32)], axis=0)
    return jnp.transpose(padded)


def request_length(which, per_device, order, lengths):
    return lengths[order[lax.axis_index("req") * per_device + which]]


def project_body(per_device, block, after, order, lengths, frequency, steps, gain, x, w, *rest):
    outs, squares, x_held, w_held, *rest = rest[after : after + 3], *rest[after + 3 :]
    helds, (x_loaded, w_loaded, stored) = rest[:3], rest[3:]
    stores = []
    rows = x.shape[0]
    span = rows // per_device
    w_loads = [
        pltpu.make_async_copy(w.at[which], w_held.at[which], w_loaded.at[which]) for which in range(3)
    ]
    x_loads = [
        pltpu.make_async_copy(
            x.at[pl.ds(low, block)], x_held.at[pl.ds(low, block)], x_loaded.at[low // block]
        )
        for low in range(0, rows, block)
    ]
    for load in (w_loads[0], *x_loads, *w_loads[1:]):
        load.start()
    starts = []
    for p in range(per_device):
        length = request_length(p, per_device, order, lengths).astype(jnp.float32)
        angle = length * frequency[...]
        starts.append((jnp.cos(angle), jnp.sin(angle)))
        squares[2:3, p * span : (p + 1) * span] = jnp.full((1, span), length)
    for which, out in enumerate(helds):
        w_loads[which].wait()
        for low in range(0, rows, block):
            if which == 0:
                x_loads[low // block].wait()
            here = slice(low, low + block)
            raw = jnp.dot(x_held[here], w_held[which], preferred_element_type=jnp.float32)
            if which == 2:
                out[here] = raw.astype(out.dtype)
                continue
            step = slice(low % span, low % span + block)
            cos_start, sin_start = starts[low // span]
            cos_step, sin_step = steps[0, step], steps[1, step]
            cosine = cos_step * cos_start - sin_step * sin_start
            sine = sin_step * cos_start + cos_step * sin_start
            lane = lax.broadcasted_iota(jnp.int32, sine.shape, 1)
            sine = jnp.where(lane < HD // 2, -sine, sine)
            squared = raw * raw
            folded = squared[:, :HD]
            for at in range(HD, squared.shape[1], HD):
                folded += squared[:, at : at + HD]
            squares[which : which + 1, here] = jnp.sum(jnp.transpose(folded), axis=0, keepdims=True)
            out[here] = turned(raw * gain[which : which + 1].astype(jnp.float32), cosine, sine)
        stores.append(pltpu.make_async_copy(out, outs[which], stored.at[which]))
        stores[-1].start()
    for store in stores:
        store.wait()


def project(per_device, order, lengths, x, w, gain, after=(), block=256):
    rows, depth = x.shape
    width = w.shape[2]
    span = rows // per_device
    half = rope_base ** (-np.arange(HD // 2, dtype=np.float32) * np.float32(2.0 / HD))
    frequency = np.concatenate([half, half]).astype(np.float32)[None]
    angles = np.arange(span, dtype=np.float32)[:, None] * frequency
    steps = np.stack([np.cos(angles), np.sin(angles)]).astype(np.float32)
    return pl.pallas_call(
        functools.partial(project_body, per_device, block, len(after)),
        in_specs=[SMEM, SMEM, VMEM, VMEM, VMEM, ANY, ANY] + [ANY] * len(after),
        out_specs=[ANY] * 3 + [VMEM],
        out_shape=[
            pltpu.HBM((rows, width), jnp.float32),
            pltpu.HBM((rows, width), jnp.float32),
            pltpu.HBM((rows, width), jnp.bfloat16),
            jax.ShapeDtypeStruct((8, rows), jnp.float32),
        ],
        scratch_shapes=[
            pltpu.VMEM(x.shape, x.dtype),
            pltpu.VMEM(w.shape, w.dtype),
            pltpu.VMEM((rows, width), jnp.float32),
            pltpu.VMEM((rows, width), jnp.float32),
            pltpu.VMEM((rows, width), jnp.bfloat16),
            pltpu.SemaphoreType.DMA((rows // block,)),
            pltpu.SemaphoreType.DMA((3,)),
            pltpu.SemaphoreType.DMA((3,)),
        ],
        cost_estimate=cost(1, 1),
        compiler_params=params(24),
        name="project_qkv",
    )(*in_hbm(order, lengths), jnp.asarray(frequency), jnp.asarray(steps), gain, *in_hbm(x, w), *after)


CONTRACT = (((1,), (1,)), ((), ()))


def attend_new_body(full_width, span, q_block, after, squares, *rest):
    sources, rest = rest[:3], rest[3 + after :]
    q_final, mixed_final, state, *helds, q_out, mixed_out, loaded, stored = rest
    q, k, v = helds
    stores = []
    heads = q.shape[1] // HD
    loads = []
    for base in range(0, q.shape[0], span):
        at = pl.ds(base, span)
        number = base // span
        loads.append(
            [
                pltpu.make_async_copy(source.at[at], held.at[at], loaded.at[number, which])
                for which, (source, held) in enumerate(zip(sources, helds))
            ]
        )
        for load in loads[-1]:
            load.start()
    state[2 * heads : 2 * heads + 1] = squares[0, 2:3]
    total = squares[0]
    for at in range(1, squares.shape[0]):
        total += squares[at]
    factors = lax.rsqrt(total / full_width + norm_eps)
    row = lax.broadcasted_iota(jnp.int32, (q_block, q_block), 0)
    column = lax.broadcasted_iota(jnp.int32, (q_block, q_block), 1)
    for base in range(0, q.shape[0], span):
        here = slice(base, base + span)
        scales = as_columns(factors[:, here])
        q_scale = scales[:, 0:1] * (HD**-0.5 * math.log2(math.e))
        k_scale = scales[:, 1:2]
        for load in loads[base // span]:
            load.wait()
        for head in range(heads):
            columns = slice(head * HD, (head + 1) * HD)
            queries = (q[here, columns] * q_scale).astype(jnp.bfloat16)
            keys = (k[here, columns] * k_scale).astype(jnp.bfloat16)
            values = jnp.transpose(v[here, columns])
            q_out[here, columns] = queries
            for low in range(0, span, q_block):
                high = low + q_block
                place = slice(base + low, base + high)
                part = queries[low:high]
                scores = lax.dot_general(
                    keys[low:high], part, CONTRACT, preferred_element_type=jnp.float32
                )
                scores = jnp.where(row <= column, scores, -1e30)
                top = jnp.max(scores, axis=0, keepdims=True)
                if low:
                    full = lax.dot_general(
                        keys[:low], part, CONTRACT, preferred_element_type=jnp.float32
                    )
                    top = jnp.maximum(top, jnp.max(full, axis=0, keepdims=True))
                scores = jnp.exp2(scores - top)
                total = jnp.sum(scores, axis=0, keepdims=True)
                mixed = jnp.dot(
                    values[:, low:high],
                    scores.astype(jnp.bfloat16),
                    preferred_element_type=jnp.float32,
                )
                if low:
                    full = jnp.exp2(full - top)
                    total += jnp.sum(full, axis=0, keepdims=True)
                    mixed += jnp.dot(
                        values[:, :low],
                        full.astype(jnp.bfloat16),
                        preferred_element_type=jnp.float32,
                    )
                mixed_out[base // span, columns, low:high] = mixed
                state[head : head + 1, place] = top
                state[heads + head : heads + head + 1, place] = total
        for at, (held, final) in enumerate(((q_out.at[here], q_final.at[here]), (mixed_out.at[base // span], mixed_final.at[base // span]))):
            stores.append(pltpu.make_async_copy(held, final, stored.at[base // span, at]))
            stores[-1].start()
    for store in stores:
        store.wait()


def attend_new(full_width, span, q, k, v, squares, after=(), q_block=256):
    rows, width = q.shape
    q_block = min(q_block, span)
    stats = 2 * (width // HD) + 8
    return pl.pallas_call(
        functools.partial(attend_new_body, full_width, span, q_block, len(after)),
        in_specs=[VMEM] + [ANY] * (3 + len(after)),
        out_specs=[ANY, ANY, VMEM],
        out_shape=[
            pltpu.HBM((rows, width), jnp.bfloat16),
            pltpu.HBM((rows // span, width, span), jnp.float32),
            jax.ShapeDtypeStruct((stats, rows), jnp.float32),
        ],
        scratch_shapes=[
            pltpu.VMEM(q.shape, q.dtype),
            pltpu.VMEM(k.shape, k.dtype),
            pltpu.VMEM(v.shape, v.dtype),
            pltpu.VMEM((rows, width), jnp.bfloat16),
            pltpu.VMEM((rows // span, width, span), jnp.float32),
            pltpu.SemaphoreType.DMA((rows // span, 3)),
            pltpu.SemaphoreType.DMA((rows // span, 2)),
        ],
        cost_estimate=cost(1, 1),
        compiler_params=params(20),
        name="attend_new",
    )(squares, *in_hbm(q, k, v), *after)


def attend_old_body(which, span, offsets, q_block, filled, after, state, q_all, mixed_all, w, *rest):
    received, rest = rest[: len(offsets)], rest[len(offsets) + int(filled) + after :]
    relaid, outs = rest[0], rest[1:-9]
    held, q, mixed, w_held, attended, loaded, q_loaded, w_loaded, stored = rest[-9:]
    me = lax.axis_index("req")
    q_load = pltpu.make_async_copy(q_all.at[pl.ds(which * span, span)], q, q_loaded.at[0])
    mixed_load = pltpu.make_async_copy(mixed_all.at[which], mixed, q_loaded.at[1])
    w_load = pltpu.make_async_copy(w, w_held, w_loaded)
    q_load.start()
    for plane in range(held.shape[0]):
        for at, offset in enumerate(offsets):
            pltpu.make_async_copy(
                received[at].at[plane, which], held.at[plane, :, me ^ offset], loaded.at[plane]
            ).start()
    mixed_load.start()
    w_load.start()
    q_load.wait()
    for plane in range(held.shape[0]):
        pltpu.make_async_copy(held.at[plane], held.at[plane], loaded.at[plane]).wait()
    mixed_load.wait()
    store = pltpu.make_async_copy(held, relaid.at[pl.ds(0, held.shape[0]), which], stored)
    store.start()
    context = math.prod(held.shape[1:4])
    token = lax.broadcasted_iota(jnp.int32, (context, q_block), 0).astype(jnp.float32)
    heads = q.shape[1] // HD
    live = token < state[2 * heads : 2 * heads + 1, which * span : which * span + q_block]
    for head in range(heads):
        columns = slice(head * HD, (head + 1) * HD)
        keys = held[0, :, :, :, columns].reshape(context, HD)
        values = jnp.transpose(held[1, :, :, :, columns].reshape(context, HD))
        for low in range(0, span, q_block):
            rows = slice(which * span + low, which * span + low + q_block)
            scores = lax.dot_general(
                keys, q[low : low + q_block, columns], CONTRACT, preferred_element_type=jnp.float32
            )
            scores = jnp.where(live, scores, -1e30)
            before = state[head : head + 1, rows]
            top = jnp.maximum(before, jnp.max(scores, axis=0, keepdims=True))
            scores = jnp.exp2(scores - top)
            shrink = jnp.exp2(before - top)
            total = state[heads + head : heads + head + 1, rows] * shrink
            total += jnp.sum(scores, axis=0, keepdims=True)
            sums = mixed[columns, low : low + q_block] * shrink
            sums += jnp.dot(values, scores.astype(jnp.bfloat16), preferred_element_type=jnp.float32)
            attended[low : low + q_block, columns] = jnp.transpose((sums / total)).astype(attended.dtype)
    w_load.wait()
    width = w.shape[1] // len(outs)
    mine = lax.axis_index("tensor")
    for at, out in enumerate(outs):
        group = pl.ds(pl.multiple_of((mine ^ at) * width, width), width)
        out[...] = jnp.dot(
            attended[...], w_held[:, group], preferred_element_type=jnp.float32
        ).astype(out.dtype)
    store.wait()


def attend_old(
    which,
    span,
    q,
    mixed,
    state,
    w,
    count,
    offsets,
    received,
    shape,
    filled=None,
    after=(),
    weight=1,
    q_block=256,
):
    width = q.shape[1]
    q_block = min(q_block, span)
    start = [] if filled is None else [filled]
    part = w.shape[1] // count
    dtype = received[0].dtype
    return pl.pallas_call(
        functools.partial(
            attend_old_body, which, span, offsets, q_block, filled is not None, len(after)
        ),
        in_specs=[VMEM] + [ANY] * (3 + len(received) + len(start) + len(after)),
        out_specs=[ANY] + [VMEM] * count,
        out_shape=[pltpu.HBM(shape, dtype)] + [pltpu.VMEM((span, part), jnp.bfloat16)] * count,
        scratch_shapes=[
            pltpu.VMEM(received[0].shape[:1] + shape[2:], dtype),
            pltpu.VMEM((span, width), q.dtype),
            pltpu.VMEM((width, span), mixed.dtype),
            pltpu.VMEM(w.shape, w.dtype),
            pltpu.VMEM((span, width), jnp.bfloat16),
            pltpu.SemaphoreType.DMA((received[0].shape[0],)),
            pltpu.SemaphoreType.DMA((2,)),
            pltpu.SemaphoreType.DMA,
            pltpu.SemaphoreType.DMA,
        ],
        input_output_aliases={} if filled is None else {4 + len(received): 0},
        cost_estimate=pl.CostEstimate(flops=weight, bytes_accessed=weight, transcendentals=0),
        compiler_params=params(16),
        name="attend_old",
    )(state, *in_hbm(q, mixed, w), *received, *start, *after)


def add_body(first, second, *rest):
    out = rest[-1]
    out[...] = (first[...].astype(jnp.float32) + second[...].astype(jnp.float32)).astype(out.dtype)


def add(first, second, after=()):
    return pl.pallas_call(
        add_body,
        in_specs=[VMEM, VMEM] + [ANY] * len(after),
        out_specs=VMEM,
        out_shape=pltpu.VMEM(first.shape, first.dtype),
        cost_estimate=cost(1, 1),
        compiler_params=params(4),
        name="add_terms",
    )(*in_vmem(first, second), *after)


def total_body(which, first, second, third, *rest):
    out, squares = rest[-2:]
    total = first[...].astype(jnp.float32) + second[...].astype(jnp.float32)
    total += third[...].astype(jnp.float32)
    out[...] = total
    squared = total * total
    folded = squared[:, :HD]
    for at in range(HD, squared.shape[1], HD):
        folded += squared[:, at : at + HD]
    sums = jnp.sum(jnp.transpose(folded), axis=0, keepdims=True)
    if len(rest) == 3:
        squares[...] = rest[0][...]
    else:
        squares[...] = jnp.zeros(squares.shape, jnp.float32)
    squares[which : which + 1] = sums


def total_of(which, first, second, third, squares=()):
    rows, width = first.shape
    return pl.pallas_call(
        functools.partial(total_body, which),
        in_specs=[VMEM] * (3 + len(squares)),
        out_specs=[VMEM, VMEM],
        out_shape=[
            pltpu.VMEM((rows, width), jnp.float32),
            jax.ShapeDtypeStruct((8, rows), jnp.float32),
        ],
        cost_estimate=cost(1, 1),
        compiler_params=params(8),
        name="total_terms",
    )(*in_vmem(first, second, third), *squares)


def finish_body(full_width, count, residual, gain, *rest):
    squares, totals = rest[:count], rest[count:-5]
    out, res_held, out_held, loaded, stored = rest[-5:]
    per_device, span, width = out.shape
    start = pl.multiple_of(lax.axis_index("tensor") * width, width)
    loads = [
        pltpu.make_async_copy(residual.at[p, :, pl.ds(start, width)], res_held.at[p], loaded.at[p])
        for p in range(per_device)
    ]
    for load in loads:
        load.start()
    total = squares[0][...]
    for part in squares[1:]:
        total += part[...]
    scales = as_columns(lax.rsqrt(total / full_width + norm_eps))
    stores = []
    for p in range(per_device):
        normed = totals[p][...] * scales[:, p : p + 1] * gain[...].astype(jnp.float32)
        loads[p].wait()
        out_held[p] = (res_held[p].astype(jnp.float32) + normed).astype(out.dtype)
        stores.append(pltpu.make_async_copy(out_held.at[p], out.at[p], stored.at[p]))
        stores[-1].start()
    for store in stores:
        store.wait()


def finish(residual, totals, squares, gain):
    per_device, span, full_width = residual.shape
    width = totals[0].shape[1]
    shape = (per_device, span, width)
    return pl.pallas_call(
        functools.partial(finish_body, full_width, len(squares)),
        in_specs=[ANY] + [VMEM] * (1 + len(squares) + per_device),
        out_specs=ANY,
        out_shape=pltpu.HBM(shape, residual.dtype),
        scratch_shapes=[
            pltpu.VMEM(shape, residual.dtype),
            pltpu.VMEM(shape, residual.dtype),
            pltpu.SemaphoreType.DMA((per_device,)),
            pltpu.SemaphoreType.DMA((per_device,)),
        ],
        cost_estimate=cost(1, 1),
        compiler_params=params(12),
        name="finish_layer",
    )(*in_hbm(residual), gain.reshape(1, width), *squares, *in_vmem(*totals))


def permuted(value, axis, offset):
    size = lax.axis_size(axis)
    return lax.ppermute(value, axis, [(i, i ^ offset) for i in range(size)])


def on_device(
    span_in, w_qkv, qk_gain, w_out, post_gain, kv_pool, block_table, request_order, lengths
):
    req_count = lax.axis_size("req")
    tensor_count = lax.axis_size("tensor")
    per_device, span_len, full_width = span_in.shape
    part_width = w_qkv.shape[2]
    planes = kv_pool.shape[0]
    hand = functools.partial(gather, kv_pool, block_table, request_order, req_count)
    shape = (planes, per_device, block_table.shape[1] // req_count, req_count) + kv_pool.shape[2:]

    others = list(range(req_count - 1, 0, -1))
    early = [s for s in others if s not in LATE]
    late = [s for s in others if s in LATE]
    sent = dict(zip([0] + others, hand([0] + others, 0, 2, False)))
    received = {s: permuted(sent[s], "req", s) for s in early}
    own = received[0] = sent[0]

    flat_in = span_in.reshape(-1, full_width)
    q_raw, k_raw, values, squares = project(
        per_device, request_order, lengths, flat_in, w_qkv, qk_gain, after=(own,)
    )
    own_squares = squares
    squares = lax.all_gather(squares, "tensor")
    queries, mixed, state = attend_new(full_width, span_len, q_raw, k_raw, values, squares)
    arrived = [received[s] for s in reversed(early)]
    sent_late = hold([sent[s] for s in late], (own_squares, *arrived[:2]), pltpu.VMEM)
    received.update({s: permuted(piece, "req", s) for s, piece in zip(late, sent_late)})

    rest = planes - 2
    everyone = list(range(req_count))
    (sent_rest,) = hand(everyone, 2, rest, True, after=(own,))
    (sent_rest,) = hold((sent_rest,), (state, *arrived[:2], received[GATE]))
    received_rest = lax.all_to_all(sent_rest, "req", 0, 0)

    relaid, across, added, totals, row_squares = None, (), (), [], ()
    for p in range(per_device):
        relaid, *terms = attend_old(
            p,
            span_len,
            queries,
            mixed,
            state,
            w_out,
            tensor_count,
            list(received),
            list(received.values()),
            shape,
            filled=relaid,
            after=(sent_rest, *added),
            weight=1 if p else 10**12,
        )
        far = permuted(terms[3], "tensor", 1)
        near = permuted(terms[1], "tensor", 1)
        added = [add(terms[2], far, after=across)]
        across = [permuted(added[0], "tensor", 2)]
        total, *row_squares = total_of(p, terms[0], near, across[0], row_squares)
        totals.append(total)
    row_squares = row_squares + [
        permuted(row_squares[0], "tensor", at) for at in range(1, tensor_count)
    ]
    layer_out = finish(span_in, totals, row_squares, post_gain)

    relaid = place(shape, everyone, 2, rest, True, [received_rest], filled=relaid)
    return layer_out, relaid.reshape(planes, per_device, -1, part_width)


def solution(mesh):
    placed = (
        P("req", None, None),
        P(None, None, "tensor"),
        P(None, "tensor"),
        P("tensor", None),
        P("tensor"),
        P(None, "req", None, "tensor"),
        P(),
        P(),
        P(),
    )
    return jax.shard_map(
        on_device,
        mesh=mesh,
        in_specs=placed,
        out_specs=(P("req", None, "tensor"), P(None, "req", None, "tensor")),
        check_vma=False,
    )
```

```python
import functools
import math

import jax
import jax.numpy as jnp
import numpy as np
from jax import lax
from jax.experimental import pallas as pl
from jax.experimental.pallas import tpu as pltpu
from jax.sharding import PartitionSpec as P

HD = 128
norm_eps = 1e-06
rope_base = 500000.0
LATE = (5, 1)
GATE = 6

ANY = pl.BlockSpec(memory_space=pl.ANY)
SMEM = pl.BlockSpec(memory_space=pltpu.SMEM)
VMEM = pl.BlockSpec(memory_space=pltpu.VMEM)


def cost(flops, moved, exps=0):
    return pl.CostEstimate(flops=1, bytes_accessed=1, transcendentals=0)


def params(mib=60):
    return pltpu.CompilerParams(vmem_limit_bytes=mib << 20)


def in_vmem(*arrays):
    return [pltpu.with_memory_space_constraint(array, pltpu.VMEM) for array in arrays]


def in_hbm(*arrays):
    return [pltpu.with_memory_space_constraint(array, pltpu.HBM) for array in arrays]


EVERYONE = -1


def gather_body(wanted, staged, count, per_device, blocks, table_all, order_all, pool, *rest):
    total = len(wanted)
    *rest, table, order, listed = rest
    lists = [
        pltpu.make_async_copy(source, held, listed.at[at])
        for at, (source, held) in enumerate(((order_all, order), (table_all, table)))
    ]
    for copy in lists:
        copy.start()
    for copy in lists:
        copy.wait()
    if staged:
        *rest, loaded, stored = rest
        outs, places = rest[-2 * total : -total], rest[-total:]
    else:
        *rest, loaded = rest
        places = rest[-total:]
    me = lax.axis_index("req")

    def load(target, first, planes, place, semaphore):
        for p in range(per_device):
            request = order[target * per_device + p]
            for b in range(blocks):
                slot = table[request, b * count + me]
                pltpu.make_async_copy(
                    pool.at[pl.ds(first, planes), slot], place.at[:, p, b], semaphore
                ).start()

    for at, (kind, first, planes) in enumerate(wanted):
        if kind == EVERYONE:
            for target in range(count):
                load(target, first, planes, places[at].at[target], loaded.at[at])
        else:
            load(me ^ kind, first, planes, places[at], loaded.at[at])
    stores = []
    for at, place in enumerate(places):
        pltpu.make_async_copy(place, place, loaded.at[at]).wait()
        if staged:
            stores.append(pltpu.make_async_copy(place, outs[at], stored.at[at]))
            stores[-1].start()
    for store in stores:
        store.wait()


def gather(pool, table, order, count, wanted, staged, after=()):
    per_device = order.shape[0] // count
    blocks = table.shape[1] // count
    lead = {EVERYONE: (count,)}
    shapes = [
        lead.get(kind, ()) + (planes, per_device, blocks) + pool.shape[2:]
        for kind, _, planes in wanted
    ]
    where = pltpu.HBM if staged else pltpu.VMEM
    semaphores = pltpu.SemaphoreType.DMA((len(wanted),))
    staging = [pltpu.VMEM(shape, pool.dtype) for shape in shapes] + [semaphores] if staged else []
    return pl.pallas_call(
        functools.partial(gather_body, wanted, staged, count, per_device, blocks),
        in_specs=[ANY] * (3 + len(after)),
        out_specs=[ANY if staged else VMEM] * len(shapes),
        out_shape=[where(shape, pool.dtype) for shape in shapes],
        scratch_shapes=staging
        + [semaphores]
        + [pltpu.SMEM(table.shape, table.dtype), pltpu.SMEM(order.shape, order.dtype)]
        + [pltpu.SemaphoreType.DMA((2,))],
        cost_estimate=cost(0, 0),
        compiler_params=params(8),
        name="gather_blocks",
    )(*in_hbm(table, order, pool), *after)


def place_body(first, planes, filled, received, out, held, loaded, stored):
    del filled
    count, _, per_device = received.shape[:3]
    chunks = [(plane, p) for plane in range(planes) for p in range(per_device)]
    for plane, p in chunks:
        for source in range(count):
            pltpu.make_async_copy(
                received.at[source, plane, p], held.at[plane, p, :, source], loaded.at[plane, p]
            ).start()
    stores = []
    for plane, p in chunks:
        here = held.at[plane, p]
        pltpu.make_async_copy(here, here, loaded.at[plane, p]).wait()
        stores.append(pltpu.make_async_copy(here, out.at[first + plane, p], stored.at[plane, p]))
        stores[-1].start()
    for store in stores:
        store.wait()


def place(shape, first, planes, received, filled):
    return pl.pallas_call(
        functools.partial(place_body, first, planes),
        in_specs=[ANY] * 2,
        out_specs=ANY,
        out_shape=pltpu.HBM(shape, filled.dtype),
        scratch_shapes=[
            pltpu.VMEM((planes,) + shape[1:], filled.dtype),
            pltpu.SemaphoreType.DMA((planes, shape[1])),
            pltpu.SemaphoreType.DMA((planes, shape[1])),
        ],
        input_output_aliases={0: 0},
        cost_estimate=cost(0, 0),
        compiler_params=params(8),
        name="place_blocks",
    )(filled, received)


def hold_body(*refs):
    pass


def hold(values, after, pin=pltpu.HBM):
    return pl.pallas_call(
        hold_body,
        in_specs=[ANY] * (len(values) + len(after)),
        out_specs=[ANY] * len(values),
        out_shape=[pin(value.shape, value.dtype) for value in values],
        input_output_aliases={at: at for at in range(len(values))},
        cost_estimate=cost(0, 0),
        compiler_params=params(1),
        name="hold",
    )(*[pltpu.with_memory_space_constraint(value, pin) for value in values], *after)


def turned(values, cosine, sine):
    heads = []
    for head in range(values.shape[1] // HD):
        part = values[:, head * HD : (head + 1) * HD]
        heads.append(part * cosine + pltpu.roll(part, HD // 2, 1) * sine)
    return jnp.concatenate(heads, axis=1)


def as_lanes(*columns):
    rows = columns[0].shape[0]
    lane = lax.broadcasted_iota(jnp.int32, (rows, HD), 1)
    spread = jnp.zeros((rows, HD), jnp.float32)
    for at, column in enumerate(columns):
        spread = jnp.where(lane == at, column, spread)
    return jnp.transpose(spread)[:8]


def as_columns(lanes):
    padded = jnp.concatenate([lanes, jnp.zeros((HD - 8, lanes.shape[1]), jnp.float32)], axis=0)
    return jnp.transpose(padded)


def request_length(which, per_device, order, lengths):
    return lengths[order[lax.axis_index("req") * per_device + which]]


def project_body(per_device, block, after, order, lengths, frequency, steps, gain, x, w, *rest):
    outs, squares, x_held, w_held, *rest = rest[after : after + 3], *rest[after + 3 :]
    helds, (x_loaded, w_loaded, stored) = rest[:3], rest[3:]
    stores = []
    rows = x.shape[0]
    span = rows // per_device
    w_loads = [
        pltpu.make_async_copy(w.at[which], w_held.at[which], w_loaded.at[which]) for which in range(3)
    ]
    x_loads = [
        pltpu.make_async_copy(
            x.at[pl.ds(low, block)], x_held.at[pl.ds(low, block)], x_loaded.at[low // block]
        )
        for low in range(0, rows, block)
    ]
    for load in (w_loads[0], *x_loads, *w_loads[1:]):
        load.start()
    starts = []
    for p in range(per_device):
        length = request_length(p, per_device, order, lengths).astype(jnp.float32)
        angle = length * frequency[...]
        starts.append((jnp.cos(angle), jnp.sin(angle)))
        squares[2:3, p * span : (p + 1) * span] = jnp.full((1, span), length)
    for which, out in enumerate(helds):
        w_loads[which].wait()
        for low in range(0, rows, block):
            if which == 0:
                x_loads[low // block].wait()
            here = slice(low, low + block)
            raw = jnp.dot(x_held[here], w_held[which], preferred_element_type=jnp.float32)
            if which == 2:
                out[here] = raw.astype(out.dtype)
                continue
            step = slice(low % span, low % span + block)
            cos_start, sin_start = starts[low // span]
            cos_step, sin_step = steps[0, step], steps[1, step]
            cosine = cos_step * cos_start - sin_step * sin_start
            sine = sin_step * cos_start + cos_step * sin_start
            lane = lax.broadcasted_iota(jnp.int32, sine.shape, 1)
            sine = jnp.where(lane < HD // 2, -sine, sine)
            squared = raw * raw
            folded = squared[:, :HD]
            for at in range(HD, squared.shape[1], HD):
                folded += squared[:, at : at + HD]
            squares[which : which + 1, here] = jnp.sum(jnp.transpose(folded), axis=0, keepdims=True)
            out[here] = turned(raw * gain[which : which + 1].astype(jnp.float32), cosine, sine)
        stores.append(pltpu.make_async_copy(out, outs[which], stored.at[which]))
        stores[-1].start()
    for store in stores:
        store.wait()


def project(per_device, order, lengths, x, w, gain, after=(), block=256):
    rows, depth = x.shape
    width = w.shape[2]
    span = rows // per_device
    half = rope_base ** (-np.arange(HD // 2, dtype=np.float32) * np.float32(2.0 / HD))
    frequency = np.concatenate([half, half]).astype(np.float32)[None]
    angles = np.arange(span, dtype=np.float32)[:, None] * frequency
    steps = np.stack([np.cos(angles), np.sin(angles)]).astype(np.float32)
    return pl.pallas_call(
        functools.partial(project_body, per_device, block, len(after)),
        in_specs=[SMEM, SMEM, VMEM, VMEM, VMEM, ANY, ANY] + [ANY] * len(after),
        out_specs=[ANY] * 3 + [VMEM],
        out_shape=[
            pltpu.HBM((rows, width), jnp.float32),
            pltpu.HBM((rows, width), jnp.float32),
            pltpu.HBM((rows, width), jnp.bfloat16),
            jax.ShapeDtypeStruct((8, rows), jnp.float32),
        ],
        scratch_shapes=[
            pltpu.VMEM(x.shape, x.dtype),
            pltpu.VMEM(w.shape, w.dtype),
            pltpu.VMEM((rows, width), jnp.float32),
            pltpu.VMEM((rows, width), jnp.float32),
            pltpu.VMEM((rows, width), jnp.bfloat16),
            pltpu.SemaphoreType.DMA((rows // block,)),
            pltpu.SemaphoreType.DMA((3,)),
            pltpu.SemaphoreType.DMA((3,)),
        ],
        cost_estimate=cost(1, 1),
        compiler_params=params(24),
        name="project_qkv",
    )(*in_hbm(order, lengths), jnp.asarray(frequency), jnp.asarray(steps), gain, *in_hbm(x, w), *after)


CONTRACT = (((1,), (1,)), ((), ()))


def attend_new_body(full_width, span, q_block, after, squares, *rest):
    sources, rest = rest[:3], rest[3 + after :]
    q_final, mixed_final, state, *helds, q_out, mixed_out, loaded, stored = rest
    q, k, v = helds
    stores = []
    heads = q.shape[1] // HD
    loads = []
    for base in range(0, q.shape[0], span):
        at = pl.ds(base, span)
        number = base // span
        loads.append(
            [
                pltpu.make_async_copy(source.at[at], held.at[at], loaded.at[number, which])
                for which, (source, held) in enumerate(zip(sources, helds))
            ]
        )
        for load in loads[-1]:
            load.start()
    state[2 * heads : 2 * heads + 1] = squares[0, 2:3]
    total = squares[0]
    for at in range(1, squares.shape[0]):
        total += squares[at]
    factors = lax.rsqrt(total / full_width + norm_eps)
    row = lax.broadcasted_iota(jnp.int32, (q_block, q_block), 0)
    column = lax.broadcasted_iota(jnp.int32, (q_block, q_block), 1)
    for base in range(0, q.shape[0], span):
        here = slice(base, base + span)
        scales = as_columns(factors[:, here])
        q_scale = scales[:, 0:1] * (HD**-0.5 * math.log2(math.e))
        k_scale = scales[:, 1:2]
        for load in loads[base // span]:
            load.wait()
        for head in range(heads):
            columns = slice(head * HD, (head + 1) * HD)
            queries = (q[here, columns] * q_scale).astype(jnp.bfloat16)
            keys = (k[here, columns] * k_scale).astype(jnp.bfloat16)
            values = jnp.transpose(v[here, columns])
            q_out[here, columns] = queries
            for low in range(0, span, q_block):
                high = low + q_block
                place = slice(base + low, base + high)
                part = queries[low:high]
                scores = lax.dot_general(
                    keys[low:high], part, CONTRACT, preferred_element_type=jnp.float32
                )
                scores = jnp.where(row <= column, scores, -1e30)
                top = jnp.max(scores, axis=0, keepdims=True)
                if low:
                    full = lax.dot_general(
                        keys[:low], part, CONTRACT, preferred_element_type=jnp.float32
                    )
                    top = jnp.maximum(top, jnp.max(full, axis=0, keepdims=True))
                scores = jnp.exp2(scores - top)
                total = jnp.sum(scores, axis=0, keepdims=True)
                mixed = jnp.dot(
                    values[:, low:high],
                    scores.astype(jnp.bfloat16),
                    preferred_element_type=jnp.float32,
                )
                if low:
                    full = jnp.exp2(full - top)
                    total += jnp.sum(full, axis=0, keepdims=True)
                    mixed += jnp.dot(
                        values[:, :low],
                        full.astype(jnp.bfloat16),
                        preferred_element_type=jnp.float32,
                    )
                mixed_out[base // span, columns, low:high] = mixed
                state[head : head + 1, place] = top
                state[heads + head : heads + head + 1, place] = total
        for at, (held, final) in enumerate(((q_out.at[here], q_final.at[here]), (mixed_out.at[base // span], mixed_final.at[base // span]))):
            stores.append(pltpu.make_async_copy(held, final, stored.at[base // span, at]))
            stores[-1].start()
    for store in stores:
        store.wait()


def attend_new(full_width, span, q, k, v, squares, after=(), q_block=256):
    rows, width = q.shape
    q_block = min(q_block, span)
    stats = 2 * (width // HD) + 8
    return pl.pallas_call(
        functools.partial(attend_new_body, full_width, span, q_block, len(after)),
        in_specs=[VMEM] + [ANY] * (3 + len(after)),
        out_specs=[ANY, ANY, VMEM],
        out_shape=[
            pltpu.HBM((rows, width), jnp.bfloat16),
            pltpu.HBM((rows // span, width, span), jnp.float32),
            jax.ShapeDtypeStruct((stats, rows), jnp.float32),
        ],
        scratch_shapes=[
            pltpu.VMEM(q.shape, q.dtype),
            pltpu.VMEM(k.shape, k.dtype),
            pltpu.VMEM(v.shape, v.dtype),
            pltpu.VMEM((rows, width), jnp.bfloat16),
            pltpu.VMEM((rows // span, width, span), jnp.float32),
            pltpu.SemaphoreType.DMA((rows // span, 3)),
            pltpu.SemaphoreType.DMA((rows // span, 2)),
        ],
        cost_estimate=cost(1, 1),
        compiler_params=params(20),
        name="attend_new",
    )(squares, *in_hbm(q, k, v), *after)


def attend_old_body(which, span, offsets, q_block, filled, after, state, q_all, mixed_all, w, *rest):
    received, rest = rest[: len(offsets)], rest[len(offsets) + int(filled) + after :]
    relaid, attended, keep, send = rest[:4]
    held, q, mixed, w_held, loaded, q_loaded, w_loaded, stored = rest[4:]
    me = lax.axis_index("req")
    q_load = pltpu.make_async_copy(q_all.at[pl.ds(which * span, span)], q, q_loaded.at[0])
    mixed_load = pltpu.make_async_copy(mixed_all.at[which], mixed, q_loaded.at[1])
    w_load = pltpu.make_async_copy(w, w_held, w_loaded)
    q_load.start()
    for plane in range(held.shape[0]):
        for at, offset in enumerate(offsets):
            pltpu.make_async_copy(
                received[at].at[plane, which], held.at[plane, :, me ^ offset], loaded.at[plane]
            ).start()
    mixed_load.start()
    w_load.start()
    stores = [
        pltpu.make_async_copy(held.at[plane], relaid.at[plane, which], stored.at[plane])
        for plane in range(held.shape[0])
    ]

    def arrive(plane, *others):
        for other in others:
            other.wait()
        pltpu.make_async_copy(held.at[plane], held.at[plane], loaded.at[plane]).wait()
        stores[plane].start()

    arrive(0, q_load)
    context = math.prod(held.shape[1:4])
    token = lax.broadcasted_iota(jnp.int32, (context, q_block), 0).astype(jnp.float32)
    heads = q.shape[1] // HD
    live = token < state[2 * heads : 2 * heads + 1, which * span : which * span + q_block]
    for head in range(heads):
        columns = slice(head * HD, (head + 1) * HD)
        keys = held[0, :, :, :, columns].reshape(context, HD)
        values = None
        for low in range(0, span, q_block):
            rows = slice(which * span + low, which * span + low + q_block)
            scores = lax.dot_general(
                keys, q[low : low + q_block, columns], CONTRACT, preferred_element_type=jnp.float32
            )
            scores = jnp.where(live, scores, -1e30)
            before = state[head : head + 1, rows]
            top = jnp.maximum(before, jnp.max(scores, axis=0, keepdims=True))
            scores = jnp.exp2(scores - top)
            shrink = jnp.exp2(before - top)
            total = state[heads + head : heads + head + 1, rows] * shrink
            total += jnp.sum(scores, axis=0, keepdims=True)
            if values is None:
                if head == 0:
                    arrive(1, mixed_load)
                values = jnp.transpose(held[1, :, :, :, columns].reshape(context, HD))
            sums = mixed[columns, low : low + q_block] * shrink
            sums += jnp.dot(values, scores.astype(jnp.bfloat16), preferred_element_type=jnp.float32)
            attended[low : low + q_block, columns] = jnp.transpose((sums / total)).astype(attended.dtype)
    w_load.wait()
    group_terms(attended, w_held, ((send, 3), (keep, 2)))
    for store in stores:
        store.wait()


def group_terms(attended, w, wanted):
    mine = lax.axis_index("tensor")
    for out, offset in wanted:
        width = out.shape[1]
        columns = pl.ds(pl.multiple_of((mine ^ offset) * width, width), width)
        out[...] = jnp.dot(
            attended[...], w[:, columns], preferred_element_type=jnp.float32
        ).astype(out.dtype)


def attend_old(
    which, span, q, mixed, state, w, part, offsets, received, shape, filled=None, after=(), weight=1, q_block=256
):
    width = q.shape[1]
    q_block = min(q_block, span)
    start = [] if filled is None else [filled]
    return pl.pallas_call(
        functools.partial(
            attend_old_body, which, span, offsets, q_block, filled is not None, len(after)
        ),
        in_specs=[VMEM] + [ANY] * (3 + len(received) + len(start) + len(after)),
        out_specs=[ANY] + [VMEM] * 3,
        out_shape=[
            pltpu.HBM(shape, received[0].dtype),
            pltpu.VMEM((span, width), jnp.bfloat16),
            pltpu.VMEM((span, part), jnp.bfloat16),
            pltpu.VMEM((span, part), jnp.bfloat16),
        ],
        scratch_shapes=[
            pltpu.VMEM((2,) + shape[2:], received[0].dtype),
            pltpu.VMEM((span, width), q.dtype),
            pltpu.VMEM((width, span), mixed.dtype),
            pltpu.VMEM(w.shape, w.dtype),
            pltpu.SemaphoreType.DMA((2,)),
            pltpu.SemaphoreType.DMA((2,)),
            pltpu.SemaphoreType.DMA,
            pltpu.SemaphoreType.DMA((2,)),
        ],
        input_output_aliases={} if filled is None else {4 + len(received): 0},
        cost_estimate=pl.CostEstimate(flops=weight, bytes_accessed=weight, transcendentals=0),
        compiler_params=params(16),
        name="attend_old",
    )(state, *in_hbm(q, mixed, w), *received, *start, *after)


def own_terms_body(attended, w, keep, send, w_held, loaded):
    load = pltpu.make_async_copy(w, w_held, loaded)
    load.start()
    load.wait()
    group_terms(attended, w_held, ((send, 1), (keep, 0)))


def own_terms(attended, w, part):
    span = attended.shape[0]
    return pl.pallas_call(
        own_terms_body,
        in_specs=[VMEM, ANY],
        out_specs=[VMEM] * 2,
        out_shape=[pltpu.VMEM((span, part), jnp.bfloat16)] * 2,
        scratch_shapes=[pltpu.VMEM(w.shape, w.dtype), pltpu.SemaphoreType.DMA],
        cost_estimate=cost(1, 1),
        compiler_params=params(8),
        name="own_terms",
    )(*in_vmem(attended), *in_hbm(w))


def add_body(first, second, *rest):
    out = rest[-1]
    out[...] = (first[...].astype(jnp.float32) + second[...].astype(jnp.float32)).astype(out.dtype)


def add(first, second, after=()):
    return pl.pallas_call(
        add_body,
        in_specs=[VMEM, VMEM] + [ANY] * len(after),
        out_specs=VMEM,
        out_shape=pltpu.VMEM(first.shape, first.dtype),
        cost_estimate=cost(1, 1),
        compiler_params=params(4),
        name="add_terms",
    )(*in_vmem(first, second), *after)


def total_body(which, first, second, third, *rest):
    out, squares = rest[-2:]
    total = first[...].astype(jnp.float32) + second[...].astype(jnp.float32)
    total += third[...].astype(jnp.float32)
    out[...] = total
    squared = total * total
    folded = squared[:, :HD]
    for at in range(HD, squared.shape[1], HD):
        folded += squared[:, at : at + HD]
    sums = jnp.sum(jnp.transpose(folded), axis=0, keepdims=True)
    if len(rest) == 3:
        squares[...] = rest[0][...]
    else:
        squares[...] = jnp.zeros(squares.shape, jnp.float32)
    squares[which : which + 1] = sums


def total_of(which, first, second, third, squares=()):
    rows, width = first.shape
    return pl.pallas_call(
        functools.partial(total_body, which),
        in_specs=[VMEM] * (3 + len(squares)),
        out_specs=[VMEM, VMEM],
        out_shape=[
            pltpu.VMEM((rows, width), jnp.float32),
            jax.ShapeDtypeStruct((8, rows), jnp.float32),
        ],
        cost_estimate=cost(1, 1),
        compiler_params=params(8),
        name="total_terms",
    )(*in_vmem(first, second, third), *squares)


def finish_body(full_width, count, residual, gain, *rest):
    squares, totals = rest[:count], rest[count:-5]
    out, res_held, out_held, loaded, stored = rest[-5:]
    per_device, span, width = out.shape
    start = pl.multiple_of(lax.axis_index("tensor") * width, width)
    loads = [
        pltpu.make_async_copy(residual.at[p, :, pl.ds(start, width)], res_held.at[p], loaded.at[p])
        for p in range(per_device)
    ]
    for load in loads:
        load.start()
    total = squares[0][...]
    for part in squares[1:]:
        total += part[...]
    scales = as_columns(lax.rsqrt(total / full_width + norm_eps))
    stores = []
    for p in range(per_device):
        normed = totals[p][...] * scales[:, p : p + 1] * gain[...].astype(jnp.float32)
        loads[p].wait()
        out_held[p] = (res_held[p].astype(jnp.float32) + normed).astype(out.dtype)
        stores.append(pltpu.make_async_copy(out_held.at[p], out.at[p], stored.at[p]))
        stores[-1].start()
    for store in stores:
        store.wait()


def finish(residual, totals, squares, gain):
    per_device, span, full_width = residual.shape
    width = totals[0].shape[1]
    shape = (per_device, span, width)
    return pl.pallas_call(
        functools.partial(finish_body, full_width, len(squares)),
        in_specs=[ANY] + [VMEM] * (1 + len(squares) + per_device),
        out_specs=ANY,
        out_shape=pltpu.HBM(shape, residual.dtype),
        scratch_shapes=[
            pltpu.VMEM(shape, residual.dtype),
            pltpu.VMEM(shape, residual.dtype),
            pltpu.SemaphoreType.DMA((per_device,)),
            pltpu.SemaphoreType.DMA((per_device,)),
        ],
        cost_estimate=cost(1, 1),
        compiler_params=params(12),
        name="finish_layer",
    )(*in_hbm(residual), gain.reshape(1, width), *squares, *in_vmem(*totals))


def permuted(value, axis, offset):
    size = lax.axis_size(axis)
    return lax.ppermute(value, axis, [(i, i ^ offset) for i in range(size)])


def on_device(
    span_in, w_qkv, qk_gain, w_out, post_gain, kv_pool, block_table, request_order, lengths
):
    req_count = lax.axis_size("req")
    tensor_count = lax.axis_size("tensor")
    per_device, span_len, full_width = span_in.shape
    part_width = w_qkv.shape[2]
    planes = kv_pool.shape[0]
    hand = functools.partial(gather, kv_pool, block_table, request_order, req_count)
    shape = (planes, per_device, block_table.shape[1] // req_count, req_count) + kv_pool.shape[2:]

    others = list(range(req_count - 1, 0, -1))
    early = [s for s in others if s not in LATE]
    late = [s for s in others if s in LATE]
    rest = planes - 2
    sent = dict(zip(early, hand([(s, 0, 2) for s in early], False)))
    received = {s: permuted(sent[s], "req", s) for s in early}
    others = hand([(s, 0, 2) for s in late + [0]], True, after=(sent[early[0]],))
    sent.update(zip(late + [0], others))
    received[0] = sent[0]

    flat_in = span_in.reshape(-1, full_width)
    q_raw, k_raw, values, squares = project(
        per_device, request_order, lengths, flat_in, w_qkv, qk_gain, after=in_hbm(sent[0])
    )
    own_squares = squares
    squares = lax.all_gather(squares, "tensor")
    queries, mixed, state = attend_new(full_width, span_len, q_raw, k_raw, values, squares)
    arrived = [received[s] for s in reversed(early)]
    sent_late = hold([sent[s] for s in late], (own_squares, *arrived[:2]))
    received.update({s: permuted(piece, "req", s) for s, piece in zip(late, sent_late)})

    (sent_rest,) = hand([(EVERYONE, 2, rest)], True, after=(state,))
    (sent_rest,) = hold((sent_rest,), (state, *arrived[:2], received[GATE]))
    received_rest = lax.all_to_all(sent_rest, "req", 0, 0)

    relaid, across, added, totals, row_squares = None, (), (), [], ()
    for p in range(per_device):
        relaid, attended, keep_far, send_far = attend_old(
            p,
            span_len,
            queries,
            mixed,
            state,
            w_out,
            part_width,
            list(received),
            list(received.values()),
            shape,
            filled=relaid,
            after=(sent_rest, *added),
            weight=1 if p else 10**12,
        )
        added = [add(keep_far, permuted(send_far, "tensor", 1), after=across)]
        across = [permuted(added[0], "tensor", 2)]
        keep, send = own_terms(attended, w_out, part_width)
        total, *row_squares = total_of(
            p, keep, permuted(send, "tensor", 1), across[0], row_squares
        )
        totals.append(total)
    row_squares = row_squares + [
        permuted(row_squares[0], "tensor", at) for at in range(1, tensor_count)
    ]
    layer_out = finish(span_in, totals, row_squares, post_gain)

    relaid = place(shape, 2, rest, received_rest, relaid)
    return layer_out, relaid.reshape(planes, per_device, -1, part_width)


def solution(mesh):
    placed = (
        P("req", None, None),
        P(None, None, "tensor"),
        P(None, "tensor"),
        P("tensor", None),
        P("tensor"),
        P(None, "req", None, "tensor"),
        P(),
        P(),
        P(),
    )
    return jax.shard_map(
        on_device,
        mesh=mesh,
        in_specs=placed,
        out_specs=(P("req", None, "tensor"), P(None, "req", None, "tensor")),
        check_vma=False,
    )
```

```python
import functools
import math

import jax
import jax.numpy as jnp
import numpy as np
from jax import lax
from jax.experimental import pallas as pl
from jax.experimental.pallas import tpu as pltpu
from jax.sharding import PartitionSpec as P

HD = 128
norm_eps = 1e-06
rope_base = 500000.0
LATE = (5, 1)
GATE = 6

ANY = pl.BlockSpec(memory_space=pl.ANY)
SMEM = pl.BlockSpec(memory_space=pltpu.SMEM)
VMEM = pl.BlockSpec(memory_space=pltpu.VMEM)


def cost(flops, moved, exps=0):
    return pl.CostEstimate(flops=1, bytes_accessed=1, transcendentals=0)


def params(mib=60):
    return pltpu.CompilerParams(vmem_limit_bytes=mib << 20)


def in_vmem(*arrays):
    return [pltpu.with_memory_space_constraint(array, pltpu.VMEM) for array in arrays]


def in_hbm(*arrays):
    return [pltpu.with_memory_space_constraint(array, pltpu.HBM) for array in arrays]


EVERYONE = -1


def gather_body(wanted, staged, count, per_device, blocks, table_all, order_all, pool, *rest):
    total = len(wanted)
    *rest, table, order, listed = rest
    lists = [
        pltpu.make_async_copy(source, held, listed.at[at])
        for at, (source, held) in enumerate(((order_all, order), (table_all, table)))
    ]
    for copy in lists:
        copy.start()
    for copy in lists:
        copy.wait()
    if staged:
        *rest, loaded, stored = rest
        outs, places = rest[-2 * total : -total], rest[-total:]
    else:
        *rest, loaded = rest
        places = rest[-total:]
    me = lax.axis_index("req")

    def load(target, first, planes, place, semaphore):
        for p in range(per_device):
            request = order[target * per_device + p]
            for b in range(blocks):
                slot = table[request, b * count + me]
                pltpu.make_async_copy(
                    pool.at[pl.ds(first, planes), slot], place.at[:, p, b], semaphore
                ).start()

    for at, (kind, first, planes) in enumerate(wanted):
        if kind == EVERYONE:
            for target in range(count):
                load(target, first, planes, places[at].at[target], loaded.at[at])
        else:
            load(me ^ kind, first, planes, places[at], loaded.at[at])
    stores = []
    for at, place in enumerate(places):
        pltpu.make_async_copy(place, place, loaded.at[at]).wait()
        if staged:
            stores.append(pltpu.make_async_copy(place, outs[at], stored.at[at]))
            stores[-1].start()
    for store in stores:
        store.wait()


def gather(pool, table, order, count, wanted, staged, after=()):
    per_device = order.shape[0] // count
    blocks = table.shape[1] // count
    lead = {EVERYONE: (count,)}
    shapes = [
        lead.get(kind, ()) + (planes, per_device, blocks) + pool.shape[2:]
        for kind, _, planes in wanted
    ]
    where = pltpu.HBM if staged else pltpu.VMEM
    semaphores = pltpu.SemaphoreType.DMA((len(wanted),))
    staging = [pltpu.VMEM(shape, pool.dtype) for shape in shapes] + [semaphores] if staged else []
    return pl.pallas_call(
        functools.partial(gather_body, wanted, staged, count, per_device, blocks),
        in_specs=[ANY] * (3 + len(after)),
        out_specs=[ANY if staged else VMEM] * len(shapes),
        out_shape=[where(shape, pool.dtype) for shape in shapes],
        scratch_shapes=staging
        + [semaphores]
        + [pltpu.SMEM(table.shape, table.dtype), pltpu.SMEM(order.shape, order.dtype)]
        + [pltpu.SemaphoreType.DMA((2,))],
        cost_estimate=cost(0, 0),
        compiler_params=params(8),
        name="gather_blocks",
    )(*in_hbm(table, order, pool), *after)


def place_body(first, planes, filled, received, out, held, loaded, stored):
    del filled
    count, _, per_device = received.shape[:3]
    chunks = [(plane, p) for plane in range(planes) for p in range(per_device)]
    for plane, p in chunks:
        for source in range(count):
            pltpu.make_async_copy(
                received.at[source, plane, p], held.at[plane, p, :, source], loaded.at[plane, p]
            ).start()
    stores = []
    for plane, p in chunks:
        here = held.at[plane, p]
        pltpu.make_async_copy(here, here, loaded.at[plane, p]).wait()
        stores.append(pltpu.make_async_copy(here, out.at[first + plane, p], stored.at[plane, p]))
        stores[-1].start()
    for store in stores:
        store.wait()


def place(shape, first, planes, received, filled):
    return pl.pallas_call(
        functools.partial(place_body, first, planes),
        in_specs=[ANY] * 2,
        out_specs=ANY,
        out_shape=pltpu.HBM(shape, filled.dtype),
        scratch_shapes=[
            pltpu.VMEM((planes,) + shape[1:], filled.dtype),
            pltpu.SemaphoreType.DMA((planes, shape[1])),
            pltpu.SemaphoreType.DMA((planes, shape[1])),
        ],
        input_output_aliases={0: 0},
        cost_estimate=cost(0, 0),
        compiler_params=params(8),
        name="place_blocks",
    )(filled, received)


def hold_body(*refs):
    pass


def hold(values, after, pin=pltpu.HBM):
    return pl.pallas_call(
        hold_body,
        in_specs=[ANY] * (len(values) + len(after)),
        out_specs=[ANY] * len(values),
        out_shape=[pin(value.shape, value.dtype) for value in values],
        input_output_aliases={at: at for at in range(len(values))},
        cost_estimate=cost(0, 0),
        compiler_params=params(1),
        name="hold",
    )(*[pltpu.with_memory_space_constraint(value, pin) for value in values], *after)


def turned(values, cosine, sine):
    heads = []
    for head in range(values.shape[1] // HD):
        part = values[:, head * HD : (head + 1) * HD]
        heads.append(part * cosine + pltpu.roll(part, HD // 2, 1) * sine)
    return jnp.concatenate(heads, axis=1)


def as_lanes(*columns):
    rows = columns[0].shape[0]
    lane = lax.broadcasted_iota(jnp.int32, (rows, HD), 1)
    spread = jnp.zeros((rows, HD), jnp.float32)
    for at, column in enumerate(columns):
        spread = jnp.where(lane == at, column, spread)
    return jnp.transpose(spread)[:8]


def as_columns(lanes):
    padded = jnp.concatenate([lanes, jnp.zeros((HD - 8, lanes.shape[1]), jnp.float32)], axis=0)
    return jnp.transpose(padded)


def request_length(which, per_device, order, lengths):
    return lengths[order[lax.axis_index("req") * per_device + which]]


def project_body(per_device, block, after, order, lengths, frequency, steps, gain, x, w, *rest):
    outs, squares, x_held, w_held, *rest = rest[after : after + 3], *rest[after + 3 :]
    helds, (x_loaded, w_loaded, stored) = rest[:3], rest[3:]
    stores = []
    rows = x.shape[0]
    span = rows // per_device
    w_loads = [
        pltpu.make_async_copy(w.at[which], w_held.at[which], w_loaded.at[which]) for which in range(3)
    ]
    x_loads = [
        pltpu.make_async_copy(
            x.at[pl.ds(low, block)], x_held.at[pl.ds(low, block)], x_loaded.at[low // block]
        )
        for low in range(0, rows, block)
    ]
    for load in (w_loads[0], *x_loads, *w_loads[1:]):
        load.start()
    starts = []
    for p in range(per_device):
        length = request_length(p, per_device, order, lengths).astype(jnp.float32)
        angle = length * frequency[...]
        starts.append((jnp.cos(angle), jnp.sin(angle)))
        squares[2:3, p * span : (p + 1) * span] = jnp.full((1, span), length)

    def keep(which, here):
        at = pl.ds(here.start, block)
        stores.append(
            pltpu.make_async_copy(
                helds[which].at[at], outs[which].at[at], stored.at[which, here.start // block]
            )
        )
        stores[-1].start()

    for which, out in enumerate(helds):
        w_loads[which].wait()
        for low in range(0, rows, block):
            if which == 0:
                x_loads[low // block].wait()
            here = slice(low, low + block)
            raw = jnp.dot(x_held[here], w_held[which], preferred_element_type=jnp.float32)
            if which == 2:
                out[here] = raw.astype(out.dtype)
                keep(which, here)
                continue
            step = slice(low % span, low % span + block)
            cos_start, sin_start = starts[low // span]
            cos_step, sin_step = steps[0, step], steps[1, step]
            cosine = cos_step * cos_start - sin_step * sin_start
            sine = sin_step * cos_start + cos_step * sin_start
            lane = lax.broadcasted_iota(jnp.int32, sine.shape, 1)
            sine = jnp.where(lane < HD // 2, -sine, sine)
            squared = raw * raw
            folded = squared[:, :HD]
            for at in range(HD, squared.shape[1], HD):
                folded += squared[:, at : at + HD]
            squares[which : which + 1, here] = jnp.sum(jnp.transpose(folded), axis=0, keepdims=True)
            out[here] = turned(raw * gain[which : which + 1].astype(jnp.float32), cosine, sine)
            keep(which, here)
    for store in stores:
        store.wait()


def project(per_device, order, lengths, x, w, gain, after=(), block=256):
    rows, depth = x.shape
    width = w.shape[2]
    span = rows // per_device
    half = rope_base ** (-np.arange(HD // 2, dtype=np.float32) * np.float32(2.0 / HD))
    frequency = np.concatenate([half, half]).astype(np.float32)[None]
    angles = np.arange(span, dtype=np.float32)[:, None] * frequency
    steps = np.stack([np.cos(angles), np.sin(angles)]).astype(np.float32)
    return pl.pallas_call(
        functools.partial(project_body, per_device, block, len(after)),
        in_specs=[SMEM, SMEM, VMEM, VMEM, VMEM, ANY, ANY] + [ANY] * len(after),
        out_specs=[ANY] * 3 + [VMEM],
        out_shape=[
            pltpu.HBM((rows, width), jnp.float32),
            pltpu.HBM((rows, width), jnp.float32),
            pltpu.HBM((rows, width), jnp.bfloat16),
            jax.ShapeDtypeStruct((8, rows), jnp.float32),
        ],
        scratch_shapes=[
            pltpu.VMEM(x.shape, x.dtype),
            pltpu.VMEM(w.shape, w.dtype),
            pltpu.VMEM((rows, width), jnp.float32),
            pltpu.VMEM((rows, width), jnp.float32),
            pltpu.VMEM((rows, width), jnp.bfloat16),
            pltpu.SemaphoreType.DMA((rows // block,)),
            pltpu.SemaphoreType.DMA((3,)),
            pltpu.SemaphoreType.DMA((3, rows // block)),
        ],
        cost_estimate=cost(1, 1),
        compiler_params=params(24),
        name="project_qkv",
    )(*in_hbm(order, lengths), jnp.asarray(frequency), jnp.asarray(steps), gain, *in_hbm(x, w), *after)


CONTRACT = (((1,), (1,)), ((), ()))


def attend_new_body(full_width, span, q_block, after, squares, *rest):
    sources, rest = rest[:3], rest[3 + after :]
    q_final, mixed_final, state, *helds, q_out, mixed_out, loaded, stored = rest
    q, k, v = helds
    stores = []

    def keep(held, final, *number):
        stores.append(pltpu.make_async_copy(held, final, stored.at[number]))
        stores[-1].start()

    heads = q.shape[1] // HD
    loads = []
    for base in range(0, q.shape[0], span):
        at = pl.ds(base, span)
        number = base // span
        loads.append(
            [
                pltpu.make_async_copy(source.at[at], held.at[at], loaded.at[number, which])
                for which, (source, held) in enumerate(zip(sources, helds))
            ]
        )
        for load in loads[-1]:
            load.start()
    state[2 * heads : 2 * heads + 1] = squares[0, 2:3]
    total = squares[0]
    for at in range(1, squares.shape[0]):
        total += squares[at]
    factors = lax.rsqrt(total / full_width + norm_eps)
    row = lax.broadcasted_iota(jnp.int32, (q_block, q_block), 0)
    column = lax.broadcasted_iota(jnp.int32, (q_block, q_block), 1)
    for base in range(0, q.shape[0], span):
        here = slice(base, base + span)
        scales = as_columns(factors[:, here])
        q_scale = scales[:, 0:1] * (HD**-0.5 * math.log2(math.e))
        k_scale = scales[:, 1:2]
        for load in loads[base // span]:
            load.wait()
        for head in range(heads):
            columns = slice(head * HD, (head + 1) * HD)
            queries = (q[here, columns] * q_scale).astype(jnp.bfloat16)
            keys = (k[here, columns] * k_scale).astype(jnp.bfloat16)
            values = jnp.transpose(v[here, columns])
            q_out[here, columns] = queries
            for low in range(0, span, q_block):
                high = low + q_block
                place = slice(base + low, base + high)
                part = queries[low:high]
                scores = lax.dot_general(
                    keys[low:high], part, CONTRACT, preferred_element_type=jnp.float32
                )
                scores = jnp.where(row <= column, scores, -1e30)
                top = jnp.max(scores, axis=0, keepdims=True)
                if low:
                    full = lax.dot_general(
                        keys[:low], part, CONTRACT, preferred_element_type=jnp.float32
                    )
                    top = jnp.maximum(top, jnp.max(full, axis=0, keepdims=True))
                scores = jnp.exp2(scores - top)
                total = jnp.sum(scores, axis=0, keepdims=True)
                mixed = jnp.dot(
                    values[:, low:high],
                    scores.astype(jnp.bfloat16),
                    preferred_element_type=jnp.float32,
                )
                if low:
                    full = jnp.exp2(full - top)
                    total += jnp.sum(full, axis=0, keepdims=True)
                    mixed += jnp.dot(
                        values[:, :low],
                        full.astype(jnp.bfloat16),
                        preferred_element_type=jnp.float32,
                    )
                mixed_out[base // span, columns, low:high] = mixed
                state[head : head + 1, place] = top
                state[heads + head : heads + head + 1, place] = total
            keep(mixed_out.at[base // span, columns], mixed_final.at[base // span, columns], base // span, head)
        keep(q_out.at[here], q_final.at[here], base // span, heads)
    for store in stores:
        store.wait()


def attend_new(full_width, span, q, k, v, squares, after=(), q_block=256):
    rows, width = q.shape
    q_block = min(q_block, span)
    stats = 2 * (width // HD) + 8
    return pl.pallas_call(
        functools.partial(attend_new_body, full_width, span, q_block, len(after)),
        in_specs=[VMEM] + [ANY] * (3 + len(after)),
        out_specs=[ANY, ANY, VMEM],
        out_shape=[
            pltpu.HBM((rows, width), jnp.bfloat16),
            pltpu.HBM((rows // span, width, span), jnp.float32),
            jax.ShapeDtypeStruct((stats, rows), jnp.float32),
        ],
        scratch_shapes=[
            pltpu.VMEM(q.shape, q.dtype),
            pltpu.VMEM(k.shape, k.dtype),
            pltpu.VMEM(v.shape, v.dtype),
            pltpu.VMEM((rows, width), jnp.bfloat16),
            pltpu.VMEM((rows // span, width, span), jnp.float32),
            pltpu.SemaphoreType.DMA((rows // span, 3)),
            pltpu.SemaphoreType.DMA((rows // span, width // HD + 1)),
        ],
        cost_estimate=cost(1, 1),
        compiler_params=params(20),
        name="attend_new",
    )(squares, *in_hbm(q, k, v), *after)


def attend_old_body(which, span, offsets, q_block, filled, after, state, q_all, mixed_all, w, *rest):
    received, rest = rest[: len(offsets)], rest[len(offsets) + int(filled) + after :]
    relaid, attended, keep, send = rest[:4]
    held, q, mixed, w_held, loaded, q_loaded, w_loaded, stored = rest[4:]
    me = lax.axis_index("req")
    q_load = pltpu.make_async_copy(q_all.at[pl.ds(which * span, span)], q, q_loaded.at[0])
    mixed_load = pltpu.make_async_copy(mixed_all.at[which], mixed, q_loaded.at[1])
    w_load = pltpu.make_async_copy(w, w_held, w_loaded)
    q_load.start()
    for plane in range(held.shape[0]):
        for at, offset in enumerate(offsets):
            pltpu.make_async_copy(
                received[at].at[plane, which], held.at[plane, :, me ^ offset], loaded.at[plane]
            ).start()
    mixed_load.start()
    w_load.start()
    stores = [
        pltpu.make_async_copy(held.at[plane], relaid.at[plane, which], stored.at[plane])
        for plane in range(held.shape[0])
    ]

    def arrive(plane, *others):
        for other in others:
            other.wait()
        pltpu.make_async_copy(held.at[plane], held.at[plane], loaded.at[plane]).wait()
        stores[plane].start()

    arrive(0, q_load)
    context = math.prod(held.shape[1:4])
    token = lax.broadcasted_iota(jnp.int32, (context, q_block), 0).astype(jnp.float32)
    heads = q.shape[1] // HD
    live = token < state[2 * heads : 2 * heads + 1, which * span : which * span + q_block]
    for head in range(heads):
        columns = slice(head * HD, (head + 1) * HD)
        keys = held[0, :, :, :, columns].reshape(context, HD)
        values = None
        for low in range(0, span, q_block):
            rows = slice(which * span + low, which * span + low + q_block)
            scores = lax.dot_general(
                keys, q[low : low + q_block, columns], CONTRACT, preferred_element_type=jnp.float32
            )
            scores = jnp.where(live, scores, -1e30)
            before = state[head : head + 1, rows]
            top = jnp.maximum(before, jnp.max(scores, axis=0, keepdims=True))
            scores = jnp.exp2(scores - top)
            shrink = jnp.exp2(before - top)
            total = state[heads + head : heads + head + 1, rows] * shrink
            total += jnp.sum(scores, axis=0, keepdims=True)
            if values is None:
                if head == 0:
                    arrive(1, mixed_load)
                values = jnp.transpose(held[1, :, :, :, columns].reshape(context, HD))
            sums = mixed[columns, low : low + q_block] * shrink
            sums += jnp.dot(values, scores.astype(jnp.bfloat16), preferred_element_type=jnp.float32)
            attended[low : low + q_block, columns] = jnp.transpose((sums / total)).astype(attended.dtype)
    w_load.wait()
    group_terms(attended, w_held, ((send, 3), (keep, 2)))
    for store in stores:
        store.wait()


def group_terms(attended, w, wanted):
    mine = lax.axis_index("tensor")
    for out, offset in wanted:
        width = out.shape[1]
        columns = pl.ds(pl.multiple_of((mine ^ offset) * width, width), width)
        out[...] = jnp.dot(
            attended[...], w[:, columns], preferred_element_type=jnp.float32
        ).astype(out.dtype)


def attend_old(
    which, span, q, mixed, state, w, part, offsets, received, shape, filled=None, after=(), weight=1, q_block=256
):
    width = q.shape[1]
    q_block = min(q_block, span)
    start = [] if filled is None else [filled]
    return pl.pallas_call(
        functools.partial(
            attend_old_body, which, span, offsets, q_block, filled is not None, len(after)
        ),
        in_specs=[VMEM] + [ANY] * (3 + len(received) + len(start) + len(after)),
        out_specs=[ANY] + [VMEM] * 3,
        out_shape=[
            pltpu.HBM(shape, received[0].dtype),
            pltpu.VMEM((span, width), jnp.bfloat16),
            pltpu.VMEM((span, part), jnp.bfloat16),
            pltpu.VMEM((span, part), jnp.bfloat16),
        ],
        scratch_shapes=[
            pltpu.VMEM((2,) + shape[2:], received[0].dtype),
            pltpu.VMEM((span, width), q.dtype),
            pltpu.VMEM((width, span), mixed.dtype),
            pltpu.VMEM(w.shape, w.dtype),
            pltpu.SemaphoreType.DMA((2,)),
            pltpu.SemaphoreType.DMA((2,)),
            pltpu.SemaphoreType.DMA,
            pltpu.SemaphoreType.DMA((2,)),
        ],
        input_output_aliases={} if filled is None else {4 + len(received): 0},
        cost_estimate=pl.CostEstimate(flops=weight, bytes_accessed=weight, transcendentals=0),
        compiler_params=params(16),
        name="attend_old",
    )(state, *in_hbm(q, mixed, w), *received, *start, *after)


def own_terms_body(attended, w, keep, send, w_held, loaded):
    load = pltpu.make_async_copy(w, w_held, loaded)
    load.start()
    load.wait()
    group_terms(attended, w_held, ((send, 1), (keep, 0)))


def own_terms(attended, w, part):
    span = attended.shape[0]
    return pl.pallas_call(
        own_terms_body,
        in_specs=[VMEM, ANY],
        out_specs=[VMEM] * 2,
        out_shape=[pltpu.VMEM((span, part), jnp.bfloat16)] * 2,
        scratch_shapes=[pltpu.VMEM(w.shape, w.dtype), pltpu.SemaphoreType.DMA],
        cost_estimate=cost(1, 1),
        compiler_params=params(8),
        name="own_terms",
    )(*in_vmem(attended), *in_hbm(w))


def add_body(first, second, *rest):
    out = rest[-1]
    out[...] = (first[...].astype(jnp.float32) + second[...].astype(jnp.float32)).astype(out.dtype)


def add(first, second, after=()):
    return pl.pallas_call(
        add_body,
        in_specs=[VMEM, VMEM] + [ANY] * len(after),
        out_specs=VMEM,
        out_shape=pltpu.VMEM(first.shape, first.dtype),
        cost_estimate=cost(1, 1),
        compiler_params=params(4),
        name="add_terms",
    )(*in_vmem(first, second), *after)


def total_body(which, first, second, third, *rest):
    out, squares = rest[-2:]
    total = first[...].astype(jnp.float32) + second[...].astype(jnp.float32)
    total += third[...].astype(jnp.float32)
    out[...] = total
    squared = total * total
    folded = squared[:, :HD]
    for at in range(HD, squared.shape[1], HD):
        folded += squared[:, at : at + HD]
    sums = jnp.sum(jnp.transpose(folded), axis=0, keepdims=True)
    if len(rest) == 3:
        squares[...] = rest[0][...]
    else:
        squares[...] = jnp.zeros(squares.shape, jnp.float32)
    squares[which : which + 1] = sums


def total_of(which, first, second, third, squares=()):
    rows, width = first.shape
    return pl.pallas_call(
        functools.partial(total_body, which),
        in_specs=[VMEM] * (3 + len(squares)),
        out_specs=[VMEM, VMEM],
        out_shape=[
            pltpu.VMEM((rows, width), jnp.float32),
            jax.ShapeDtypeStruct((8, rows), jnp.float32),
        ],
        cost_estimate=cost(1, 1),
        compiler_params=params(8),
        name="total_terms",
    )(*in_vmem(first, second, third), *squares)


def finish_body(full_width, count, residual, gain, *rest):
    squares, totals = rest[:count], rest[count:-5]
    out, res_held, out_held, loaded, stored = rest[-5:]
    per_device, span, width = out.shape
    start = pl.multiple_of(lax.axis_index("tensor") * width, width)
    loads = [
        pltpu.make_async_copy(residual.at[p, :, pl.ds(start, width)], res_held.at[p], loaded.at[p])
        for p in range(per_device)
    ]
    for load in loads:
        load.start()
    total = squares[0][...]
    for part in squares[1:]:
        total += part[...]
    scales = as_columns(lax.rsqrt(total / full_width + norm_eps))
    stores = []
    for p in range(per_device):
        normed = totals[p][...] * scales[:, p : p + 1] * gain[...].astype(jnp.float32)
        loads[p].wait()
        out_held[p] = (res_held[p].astype(jnp.float32) + normed).astype(out.dtype)
        stores.append(pltpu.make_async_copy(out_held.at[p], out.at[p], stored.at[p]))
        stores[-1].start()
    for store in stores:
        store.wait()


def finish(residual, totals, squares, gain):
    per_device, span, full_width = residual.shape
    width = totals[0].shape[1]
    shape = (per_device, span, width)
    return pl.pallas_call(
        functools.partial(finish_body, full_width, len(squares)),
        in_specs=[ANY] + [VMEM] * (1 + len(squares) + per_device),
        out_specs=ANY,
        out_shape=pltpu.HBM(shape, residual.dtype),
        scratch_shapes=[
            pltpu.VMEM(shape, residual.dtype),
            pltpu.VMEM(shape, residual.dtype),
            pltpu.SemaphoreType.DMA((per_device,)),
            pltpu.SemaphoreType.DMA((per_device,)),
        ],
        cost_estimate=cost(1, 1),
        compiler_params=params(12),
        name="finish_layer",
    )(*in_hbm(residual), gain.reshape(1, width), *squares, *in_vmem(*totals))


def permuted(value, axis, offset):
    size = lax.axis_size(axis)
    return lax.ppermute(value, axis, [(i, i ^ offset) for i in range(size)])


def on_device(
    span_in, w_qkv, qk_gain, w_out, post_gain, kv_pool, block_table, request_order, lengths
):
    req_count = lax.axis_size("req")
    tensor_count = lax.axis_size("tensor")
    per_device, span_len, full_width = span_in.shape
    part_width = w_qkv.shape[2]
    planes = kv_pool.shape[0]
    hand = functools.partial(gather, kv_pool, block_table, request_order, req_count)
    shape = (planes, per_device, block_table.shape[1] // req_count, req_count) + kv_pool.shape[2:]

    others = list(range(req_count - 1, 0, -1))
    early = [s for s in others if s not in LATE]
    late = [s for s in others if s in LATE]
    rest = planes - 2
    sent = dict(zip(early, hand([(s, 0, 2) for s in early], False)))
    received = {s: permuted(sent[s], "req", s) for s in early}
    others = hand([(s, 0, 2) for s in late + [0]], True, after=(sent[early[0]],))
    sent.update(zip(late + [0], others))
    received[0] = sent[0]

    flat_in = span_in.reshape(-1, full_width)
    q_raw, k_raw, values, squares = project(
        per_device, request_order, lengths, flat_in, w_qkv, qk_gain, after=in_hbm(sent[0])
    )
    own_squares = squares
    squares = lax.all_gather(squares, "tensor")
    queries, mixed, state = attend_new(full_width, span_len, q_raw, k_raw, values, squares)
    arrived = [received[s] for s in reversed(early)]
    sent_late = [
        hold((sent[s],), (own_squares, first))[0] for s, first in zip(late, arrived[1::-1])
    ]
    received.update({s: permuted(piece, "req", s) for s, piece in zip(late, sent_late)})

    (sent_rest,) = hand([(EVERYONE, 2, rest)], True, after=(state,))
    (sent_rest,) = hold((sent_rest,), (state, *arrived[:2], received[GATE]))
    received_rest = lax.all_to_all(sent_rest, "req", 0, 0)

    relaid, across, added, totals, row_squares = None, (), (), [], ()
    for p in range(per_device):
        relaid, attended, keep_far, send_far = attend_old(
            p,
            span_len,
            queries,
            mixed,
            state,
            w_out,
            part_width,
            list(received),
            list(received.values()),
            shape,
            filled=relaid,
            after=(sent_rest, *added),
            weight=1 if p else 10**12,
        )
        added = [add(keep_far, permuted(send_far, "tensor", 1), after=across)]
        across = [permuted(added[0], "tensor", 2)]
        keep, send = own_terms(attended, w_out, part_width)
        total, *row_squares = total_of(
            p, keep, permuted(send, "tensor", 1), across[0], row_squares
        )
        totals.append(total)
    row_squares = row_squares + [
        permuted(row_squares[0], "tensor", at) for at in range(1, tensor_count)
    ]
    layer_out = finish(span_in, totals, row_squares, post_gain)

    relaid = place(shape, 2, rest, received_rest, relaid)
    return layer_out, relaid.reshape(planes, per_device, -1, part_width)


def solution(mesh):
    placed = (
        P("req", None, None),
        P(None, None, "tensor"),
        P(None, "tensor"),
        P("tensor", None),
        P("tensor"),
        P(None, "req", None, "tensor"),
        P(),
        P(),
        P(),
    )
    return jax.shard_map(
        on_device,
        mesh=mesh,
        in_specs=placed,
        out_specs=(P("req", None, "tensor"), P(None, "req", None, "tensor")),
        check_vma=False,
    )
```

```python
import functools
import math

import jax
import jax.numpy as jnp
import numpy as np
from jax import lax
from jax.experimental import pallas as pl
from jax.experimental.pallas import tpu as pltpu
from jax.sharding import PartitionSpec as P

HD = 128
norm_eps = 1e-06
rope_base = 500000.0
LATE = (5, 1)
GATE = 6

ANY = pl.BlockSpec(memory_space=pl.ANY)
SMEM = pl.BlockSpec(memory_space=pltpu.SMEM)
VMEM = pl.BlockSpec(memory_space=pltpu.VMEM)


def cost(flops, moved, exps=0):
    return pl.CostEstimate(flops=1, bytes_accessed=1, transcendentals=0)


def params(mib=60):
    return pltpu.CompilerParams(vmem_limit_bytes=mib << 20)


def in_vmem(*arrays):
    return [pltpu.with_memory_space_constraint(array, pltpu.VMEM) for array in arrays]


def in_hbm(*arrays):
    return [pltpu.with_memory_space_constraint(array, pltpu.HBM) for array in arrays]


EVERYONE = -1


def gather_body(wanted, staged, count, per_device, blocks, table_all, order_all, pool, *rest):
    total = len(wanted)
    *rest, table, order, listed = rest
    lists = [
        pltpu.make_async_copy(source, held, listed.at[at])
        for at, (source, held) in enumerate(((order_all, order), (table_all, table)))
    ]
    for copy in lists:
        copy.start()
    for copy in lists:
        copy.wait()
    if staged:
        *rest, loaded, stored = rest
        outs, places = rest[-2 * total : -total], rest[-total:]
    else:
        *rest, loaded = rest
        places = rest[-total:]
    me = lax.axis_index("req")

    def load(target, first, planes, place, semaphore):
        for p in range(per_device):
            request = order[target * per_device + p]
            for b in range(blocks):
                slot = table[request, b * count + me]
                pltpu.make_async_copy(
                    pool.at[pl.ds(first, planes), slot], place.at[:, p, b], semaphore
                ).start()

    for at, (kind, first, planes) in enumerate(wanted):
        if kind == EVERYONE:
            for target in range(count):
                load(target, first, planes, places[at].at[target], loaded.at[at])
        else:
            load(me ^ kind, first, planes, places[at], loaded.at[at])
    stores = []
    for at, place in enumerate(places):
        pltpu.make_async_copy(place, place, loaded.at[at]).wait()
        if staged:
            stores.append(pltpu.make_async_copy(place, outs[at], stored.at[at]))
            stores[-1].start()
    for store in stores:
        store.wait()


def gather(pool, table, order, count, wanted, staged, after=()):
    per_device = order.shape[0] // count
    blocks = table.shape[1] // count
    lead = {EVERYONE: (count,)}
    shapes = [
        lead.get(kind, ()) + (planes, per_device, blocks) + pool.shape[2:]
        for kind, _, planes in wanted
    ]
    where = pltpu.HBM if staged else pltpu.VMEM
    semaphores = pltpu.SemaphoreType.DMA((len(wanted),))
    staging = [pltpu.VMEM(shape, pool.dtype) for shape in shapes] + [semaphores] if staged else []
    return pl.pallas_call(
        functools.partial(gather_body, wanted, staged, count, per_device, blocks),
        in_specs=[ANY] * (3 + len(after)),
        out_specs=[ANY if staged else VMEM] * len(shapes),
        out_shape=[where(shape, pool.dtype) for shape in shapes],
        scratch_shapes=staging
        + [semaphores]
        + [pltpu.SMEM(table.shape, table.dtype), pltpu.SMEM(order.shape, order.dtype)]
        + [pltpu.SemaphoreType.DMA((2,))],
        cost_estimate=cost(0, 0),
        compiler_params=params(8),
        name="gather_blocks",
    )(*in_hbm(table, order, pool), *after)


def place_body(first, planes, filled, received, out, held, loaded, stored):
    del filled
    count, _, per_device = received.shape[:3]
    chunks = [(plane, p) for plane in range(planes) for p in range(per_device)]
    for plane, p in chunks:
        for source in range(count):
            pltpu.make_async_copy(
                received.at[source, plane, p], held.at[plane, p, :, source], loaded.at[plane, p]
            ).start()
    stores = []
    for plane, p in chunks:
        here = held.at[plane, p]
        pltpu.make_async_copy(here, here, loaded.at[plane, p]).wait()
        stores.append(pltpu.make_async_copy(here, out.at[first + plane, p], stored.at[plane, p]))
        stores[-1].start()
    for store in stores:
        store.wait()


def place(shape, first, planes, received, filled):
    return pl.pallas_call(
        functools.partial(place_body, first, planes),
        in_specs=[ANY] * 2,
        out_specs=ANY,
        out_shape=pltpu.HBM(shape, filled.dtype),
        scratch_shapes=[
            pltpu.VMEM((planes,) + shape[1:], filled.dtype),
            pltpu.SemaphoreType.DMA((planes, shape[1])),
            pltpu.SemaphoreType.DMA((planes, shape[1])),
        ],
        input_output_aliases={0: 0},
        cost_estimate=cost(0, 0),
        compiler_params=params(8),
        name="place_blocks",
    )(filled, received)


def hold_body(*refs):
    pass


def hold(values, after, pin=pltpu.HBM):
    return pl.pallas_call(
        hold_body,
        in_specs=[ANY] * (len(values) + len(after)),
        out_specs=[ANY] * len(values),
        out_shape=[pin(value.shape, value.dtype) for value in values],
        input_output_aliases={at: at for at in range(len(values))},
        cost_estimate=cost(0, 0),
        compiler_params=params(1),
        name="hold",
    )(*[pltpu.with_memory_space_constraint(value, pin) for value in values], *after)


def turned(values, cosine, sine):
    heads = []
    for head in range(values.shape[1] // HD):
        part = values[:, head * HD : (head + 1) * HD]
        heads.append(part * cosine + pltpu.roll(part, HD // 2, 1) * sine)
    return jnp.concatenate(heads, axis=1)


def as_lanes(*columns):
    rows = columns[0].shape[0]
    lane = lax.broadcasted_iota(jnp.int32, (rows, HD), 1)
    spread = jnp.zeros((rows, HD), jnp.float32)
    for at, column in enumerate(columns):
        spread = jnp.where(lane == at, column, spread)
    return jnp.transpose(spread)[:8]


def as_columns(lanes):
    padded = jnp.concatenate([lanes, jnp.zeros((HD - 8, lanes.shape[1]), jnp.float32)], axis=0)
    return jnp.transpose(padded)


def request_length(which, per_device, order, lengths):
    return lengths[order[lax.axis_index("req") * per_device + which]]


def project_body(per_device, block, after, order, lengths, frequency, steps, gain, x, w, *rest):
    outs, squares, x_held, w_held, *rest = rest[after : after + 3], *rest[after + 3 :]
    helds, (x_loaded, w_loaded, stored) = rest[:3], rest[3:]
    stores = []
    rows = x.shape[0]
    span = rows // per_device
    w_loads = [
        pltpu.make_async_copy(w.at[which], w_held.at[which], w_loaded.at[which]) for which in range(3)
    ]
    x_loads = [
        pltpu.make_async_copy(
            x.at[pl.ds(low, block)], x_held.at[pl.ds(low, block)], x_loaded.at[low // block]
        )
        for low in range(0, rows, block)
    ]
    for load in (w_loads[0], *x_loads, *w_loads[1:]):
        load.start()
    starts = []
    for p in range(per_device):
        length = request_length(p, per_device, order, lengths).astype(jnp.float32)
        angle = length * frequency[...]
        starts.append((jnp.cos(angle), jnp.sin(angle)))
        squares[2:3, p * span : (p + 1) * span] = jnp.full((1, span), length)

    def keep(which, here):
        at = pl.ds(here.start, block)
        stores.append(
            pltpu.make_async_copy(
                helds[which].at[at], outs[which].at[at], stored.at[which, here.start // block]
            )
        )
        stores[-1].start()

    for which, out in enumerate(helds):
        w_loads[which].wait()
        for low in range(0, rows, block):
            if which == 0:
                x_loads[low // block].wait()
            here = slice(low, low + block)
            raw = jnp.dot(x_held[here], w_held[which], preferred_element_type=jnp.float32)
            if which == 2:
                out[here] = raw.astype(out.dtype)
                keep(which, here)
                continue
            step = slice(low % span, low % span + block)
            cos_start, sin_start = starts[low // span]
            cos_step, sin_step = steps[0, step], steps[1, step]
            cosine = cos_step * cos_start - sin_step * sin_start
            sine = sin_step * cos_start + cos_step * sin_start
            lane = lax.broadcasted_iota(jnp.int32, sine.shape, 1)
            sine = jnp.where(lane < HD // 2, -sine, sine)
            squared = raw * raw
            folded = squared[:, :HD]
            for at in range(HD, squared.shape[1], HD):
                folded += squared[:, at : at + HD]
            squares[which : which + 1, here] = jnp.sum(jnp.transpose(folded), axis=0, keepdims=True)
            out[here] = turned(raw * gain[which : which + 1].astype(jnp.float32), cosine, sine)
            keep(which, here)
    for store in stores:
        store.wait()


def project(per_device, order, lengths, x, w, gain, after=(), block=256):
    rows, depth = x.shape
    width = w.shape[2]
    span = rows // per_device
    half = rope_base ** (-np.arange(HD // 2, dtype=np.float32) * np.float32(2.0 / HD))
    frequency = np.concatenate([half, half]).astype(np.float32)[None]
    angles = np.arange(span, dtype=np.float32)[:, None] * frequency
    steps = np.stack([np.cos(angles), np.sin(angles)]).astype(np.float32)
    return pl.pallas_call(
        functools.partial(project_body, per_device, block, len(after)),
        in_specs=[SMEM, SMEM, VMEM, VMEM, VMEM, ANY, ANY] + [ANY] * len(after),
        out_specs=[ANY] * 3 + [VMEM],
        out_shape=[
            pltpu.HBM((rows, width), jnp.float32),
            pltpu.HBM((rows, width), jnp.float32),
            pltpu.HBM((rows, width), jnp.bfloat16),
            jax.ShapeDtypeStruct((8, rows), jnp.float32),
        ],
        scratch_shapes=[
            pltpu.VMEM(x.shape, x.dtype),
            pltpu.VMEM(w.shape, w.dtype),
            pltpu.VMEM((rows, width), jnp.float32),
            pltpu.VMEM((rows, width), jnp.float32),
            pltpu.VMEM((rows, width), jnp.bfloat16),
            pltpu.SemaphoreType.DMA((rows // block,)),
            pltpu.SemaphoreType.DMA((3,)),
            pltpu.SemaphoreType.DMA((3, rows // block)),
        ],
        cost_estimate=cost(1, 1),
        compiler_params=params(24),
        name="project_qkv",
    )(*in_hbm(order, lengths), jnp.asarray(frequency), jnp.asarray(steps), gain, *in_hbm(x, w), *after)


CONTRACT = (((1,), (1,)), ((), ()))


def attend_new_body(full_width, span, q_block, after, squares, *rest):
    sources, rest = rest[:3], rest[3 + after :]
    q_final, mixed_final, state, *helds, q_out, mixed_out, loaded, stored = rest
    q, k, v = helds
    stores = []

    def keep(held, final, *number):
        stores.append(pltpu.make_async_copy(held, final, stored.at[number]))
        stores[-1].start()

    heads = q.shape[1] // HD
    loads = []
    for base in range(0, q.shape[0], span):
        at = pl.ds(base, span)
        number = base // span
        loads.append(
            [
                pltpu.make_async_copy(source.at[at], held.at[at], loaded.at[number, which])
                for which, (source, held) in enumerate(zip(sources, helds))
            ]
        )
        for load in loads[-1]:
            load.start()
    state[2 * heads : 2 * heads + 1] = squares[0, 2:3]
    total = squares[0]
    for at in range(1, squares.shape[0]):
        total += squares[at]
    factors = lax.rsqrt(total / full_width + norm_eps)
    row = lax.broadcasted_iota(jnp.int32, (q_block, q_block), 0)
    column = lax.broadcasted_iota(jnp.int32, (q_block, q_block), 1)
    for base in range(0, q.shape[0], span):
        here = slice(base, base + span)
        scales = as_columns(factors[:, here])
        q_scale = scales[:, 0:1] * (HD**-0.5 * math.log2(math.e))
        k_scale = scales[:, 1:2]
        for load in loads[base // span]:
            load.wait()
        for head in range(heads):
            columns = slice(head * HD, (head + 1) * HD)
            queries = (q[here, columns] * q_scale).astype(jnp.bfloat16)
            keys = (k[here, columns] * k_scale).astype(jnp.bfloat16)
            values = jnp.transpose(v[here, columns])
            q_out[here, columns] = queries
            for low in range(0, span, q_block):
                high = low + q_block
                place = slice(base + low, base + high)
                part = queries[low:high]
                scores = lax.dot_general(
                    keys[low:high], part, CONTRACT, preferred_element_type=jnp.float32
                )
                scores = jnp.where(row <= column, scores, -1e30)
                top = jnp.max(scores, axis=0, keepdims=True)
                if low:
                    full = lax.dot_general(
                        keys[:low], part, CONTRACT, preferred_element_type=jnp.float32
                    )
                    top = jnp.maximum(top, jnp.max(full, axis=0, keepdims=True))
                scores = jnp.exp2(scores - top)
                total = jnp.sum(scores, axis=0, keepdims=True)
                mixed = jnp.dot(
                    values[:, low:high],
                    scores.astype(jnp.bfloat16),
                    preferred_element_type=jnp.float32,
                )
                if low:
                    full = jnp.exp2(full - top)
                    total += jnp.sum(full, axis=0, keepdims=True)
                    mixed += jnp.dot(
                        values[:, :low],
                        full.astype(jnp.bfloat16),
                        preferred_element_type=jnp.float32,
                    )
                mixed_out[base // span, columns, low:high] = mixed
                state[head : head + 1, place] = top
                state[heads + head : heads + head + 1, place] = total
            keep(mixed_out.at[base // span, columns], mixed_final.at[base // span, columns], base // span, head)
        keep(q_out.at[here], q_final.at[here], base // span, heads)
    for store in stores:
        store.wait()


def attend_new(full_width, span, q, k, v, squares, after=(), q_block=256):
    rows, width = q.shape
    q_block = min(q_block, span)
    stats = 2 * (width // HD) + 8
    return pl.pallas_call(
        functools.partial(attend_new_body, full_width, span, q_block, len(after)),
        in_specs=[VMEM] + [ANY] * (3 + len(after)),
        out_specs=[ANY, ANY, VMEM],
        out_shape=[
            pltpu.HBM((rows, width), jnp.bfloat16),
            pltpu.HBM((rows // span, width, span), jnp.float32),
            jax.ShapeDtypeStruct((stats, rows), jnp.float32),
        ],
        scratch_shapes=[
            pltpu.VMEM(q.shape, q.dtype),
            pltpu.VMEM(k.shape, k.dtype),
            pltpu.VMEM(v.shape, v.dtype),
            pltpu.VMEM((rows, width), jnp.bfloat16),
            pltpu.VMEM((rows // span, width, span), jnp.float32),
            pltpu.SemaphoreType.DMA((rows // span, 3)),
            pltpu.SemaphoreType.DMA((rows // span, width // HD + 1)),
        ],
        cost_estimate=cost(1, 1),
        compiler_params=params(20),
        name="attend_new",
    )(squares, *in_hbm(q, k, v), *after)


def attend_old_body(which, span, offsets, q_block, filled, after, state, q_all, mixed_all, w, *rest):
    received, rest = rest[: len(offsets)], rest[len(offsets) + int(filled) + after :]
    relaid, attended, keep, *send = rest[:5]
    held, q, mixed, w_held, loaded, q_loaded, w_loaded, stored = rest[5:]
    me = lax.axis_index("req")
    q_load = pltpu.make_async_copy(q_all.at[pl.ds(which * span, span)], q, q_loaded.at[0])
    mixed_load = pltpu.make_async_copy(mixed_all.at[which], mixed, q_loaded.at[1])
    w_load = pltpu.make_async_copy(w, w_held, w_loaded)
    q_load.start()
    for plane in range(held.shape[0]):
        for at, offset in enumerate(offsets):
            pltpu.make_async_copy(
                received[at].at[plane, which], held.at[plane, :, me ^ offset], loaded.at[plane]
            ).start()
    mixed_load.start()
    w_load.start()
    stores = [
        pltpu.make_async_copy(held.at[plane], relaid.at[plane, which], stored.at[plane])
        for plane in range(held.shape[0])
    ]

    def arrive(plane, *others):
        for other in others:
            other.wait()
        pltpu.make_async_copy(held.at[plane], held.at[plane], loaded.at[plane]).wait()
        stores[plane].start()

    arrive(0, q_load)
    context = math.prod(held.shape[1:4])
    token = lax.broadcasted_iota(jnp.int32, (context, q_block), 0).astype(jnp.float32)
    heads = q.shape[1] // HD
    live = token < state[2 * heads : 2 * heads + 1, which * span : which * span + q_block]
    for head in range(heads):
        columns = slice(head * HD, (head + 1) * HD)
        keys = held[0, :, :, :, columns].reshape(context, HD)
        values = None
        for low in range(0, span, q_block):
            rows = slice(which * span + low, which * span + low + q_block)
            scores = lax.dot_general(
                keys, q[low : low + q_block, columns], CONTRACT, preferred_element_type=jnp.float32
            )
            scores = jnp.where(live, scores, -1e30)
            before = state[head : head + 1, rows]
            top = jnp.maximum(before, jnp.max(scores, axis=0, keepdims=True))
            scores = jnp.exp2(scores - top)
            shrink = jnp.exp2(before - top)
            total = state[heads + head : heads + head + 1, rows] * shrink
            total += jnp.sum(scores, axis=0, keepdims=True)
            if values is None:
                if head == 0:
                    arrive(1, mixed_load)
                values = jnp.transpose(held[1, :, :, :, columns].reshape(context, HD))
            sums = mixed[columns, low : low + q_block] * shrink
            sums += jnp.dot(values, scores.astype(jnp.bfloat16), preferred_element_type=jnp.float32)
            attended[low : low + q_block, columns] = jnp.transpose((sums / total)).astype(attended.dtype)
    w_load.wait()
    rows = send[0].shape[0]
    for at, out in enumerate(send):
        group_terms(attended.at[pl.ds(at * rows, rows)], w_held, ((out, 3),))
    group_terms(attended, w_held, ((keep, 2),))
    for store in stores:
        store.wait()


def group_terms(attended, w, wanted):
    mine = lax.axis_index("tensor")
    for out, offset in wanted:
        width = out.shape[1]
        columns = pl.ds(pl.multiple_of((mine ^ offset) * width, width), width)
        out[...] = jnp.dot(
            attended[...], w[:, columns], preferred_element_type=jnp.float32
        ).astype(out.dtype)


def attend_old(
    which, span, q, mixed, state, w, part, offsets, received, shape, filled=None, after=(), weight=1, q_block=256
):
    width = q.shape[1]
    q_block = min(q_block, span)
    start = [] if filled is None else [filled]
    return pl.pallas_call(
        functools.partial(
            attend_old_body, which, span, offsets, q_block, filled is not None, len(after)
        ),
        in_specs=[VMEM] + [ANY] * (3 + len(received) + len(start) + len(after)),
        out_specs=[ANY] + [VMEM] * 4,
        out_shape=[
            pltpu.HBM(shape, received[0].dtype),
            pltpu.VMEM((span, width), jnp.bfloat16),
            pltpu.VMEM((span, part), jnp.bfloat16),
            pltpu.VMEM((span // 2, part), jnp.bfloat16),
            pltpu.VMEM((span // 2, part), jnp.bfloat16),
        ],
        scratch_shapes=[
            pltpu.VMEM((2,) + shape[2:], received[0].dtype),
            pltpu.VMEM((span, width), q.dtype),
            pltpu.VMEM((width, span), mixed.dtype),
            pltpu.VMEM(w.shape, w.dtype),
            pltpu.SemaphoreType.DMA((2,)),
            pltpu.SemaphoreType.DMA((2,)),
            pltpu.SemaphoreType.DMA,
            pltpu.SemaphoreType.DMA((2,)),
        ],
        input_output_aliases={} if filled is None else {4 + len(received): 0},
        cost_estimate=pl.CostEstimate(flops=weight, bytes_accessed=weight, transcendentals=0),
        compiler_params=params(16),
        name="attend_old",
    )(state, *in_hbm(q, mixed, w), *received, *start, *after)


def own_terms_body(attended, w, keep, send, w_held, loaded):
    load = pltpu.make_async_copy(w, w_held, loaded)
    load.start()
    load.wait()
    group_terms(attended, w_held, ((send, 1), (keep, 0)))


def own_terms(attended, w, part):
    span = attended.shape[0]
    return pl.pallas_call(
        own_terms_body,
        in_specs=[VMEM, ANY],
        out_specs=[VMEM] * 2,
        out_shape=[pltpu.VMEM((span, part), jnp.bfloat16)] * 2,
        scratch_shapes=[pltpu.VMEM(w.shape, w.dtype), pltpu.SemaphoreType.DMA],
        cost_estimate=cost(1, 1),
        compiler_params=params(8),
        name="own_terms",
    )(*in_vmem(attended), *in_hbm(w))


def add_body(first, upper, lower, *rest):
    out = rest[-1]
    rows = upper.shape[0]
    for at, second in enumerate((upper, lower)):
        here = slice(at * rows, (at + 1) * rows)
        out[here] = (first[here].astype(jnp.float32) + second[...].astype(jnp.float32)).astype(
            out.dtype
        )


def add(first, upper, lower, after=()):
    return pl.pallas_call(
        add_body,
        in_specs=[VMEM] * 3 + [ANY] * len(after),
        out_specs=VMEM,
        out_shape=pltpu.VMEM(first.shape, first.dtype),
        cost_estimate=cost(1, 1),
        compiler_params=params(4),
        name="add_terms",
    )(*in_vmem(first, upper, lower), *after)


def total_body(which, first, second, third, *rest):
    out, squares = rest[-2:]
    total = first[...].astype(jnp.float32) + second[...].astype(jnp.float32)
    total += third[...].astype(jnp.float32)
    out[...] = total
    squared = total * total
    folded = squared[:, :HD]
    for at in range(HD, squared.shape[1], HD):
        folded += squared[:, at : at + HD]
    sums = jnp.sum(jnp.transpose(folded), axis=0, keepdims=True)
    if len(rest) == 3:
        squares[...] = rest[0][...]
    else:
        squares[...] = jnp.zeros(squares.shape, jnp.float32)
    squares[which : which + 1] = sums


def total_of(which, first, second, third, squares=()):
    rows, width = first.shape
    return pl.pallas_call(
        functools.partial(total_body, which),
        in_specs=[VMEM] * (3 + len(squares)),
        out_specs=[VMEM, VMEM],
        out_shape=[
            pltpu.VMEM((rows, width), jnp.float32),
            jax.ShapeDtypeStruct((8, rows), jnp.float32),
        ],
        cost_estimate=cost(1, 1),
        compiler_params=params(8),
        name="total_terms",
    )(*in_vmem(first, second, third), *squares)


def own_columns_body(residual, after, out, loaded):
    del after
    per_device, _, width = out.shape
    start = pl.multiple_of(lax.axis_index("tensor") * width, width)
    loads = [
        pltpu.make_async_copy(residual.at[p, :, pl.ds(start, width)], out.at[p], loaded.at[p])
        for p in range(per_device)
    ]
    for load in loads:
        load.start()
    for load in loads:
        load.wait()


def own_columns(residual, width, after):
    per_device, span, _ = residual.shape
    return pl.pallas_call(
        own_columns_body,
        in_specs=[ANY, ANY],
        out_specs=VMEM,
        out_shape=pltpu.VMEM((per_device, span, width), residual.dtype),
        scratch_shapes=[pltpu.SemaphoreType.DMA((per_device,))],
        cost_estimate=cost(1, 1),
        compiler_params=params(2),
        name="own_columns",
    )(*in_hbm(residual), after)


def finish_body(full_width, count, residual, gain, *rest):
    squares, totals = rest[:count], rest[count:-3]
    out, out_held, stored = rest[-3:]
    per_device, span, width = out.shape
    total = squares[0][...]
    for part in squares[1:]:
        total += part[...]
    scales = as_columns(lax.rsqrt(total / full_width + norm_eps))
    half = span // 2
    stores = []
    for p in range(per_device):
        for at in range(2):
            here = slice(at * half, (at + 1) * half)
            normed = totals[p][here] * scales[here, p : p + 1] * gain[...].astype(jnp.float32)
            out_held[p, here] = (residual[p, here].astype(jnp.float32) + normed).astype(out.dtype)
            rows = pl.ds(at * half, half)
            stores.append(
                pltpu.make_async_copy(out_held.at[p, rows], out.at[p, rows], stored.at[p, at])
            )
            stores[-1].start()
    for store in stores:
        store.wait()


def finish(full_width, residual, totals, squares, gain):
    per_device, span, width = residual.shape
    return pl.pallas_call(
        functools.partial(finish_body, full_width, len(squares)),
        in_specs=[VMEM] * (2 + len(squares) + per_device),
        out_specs=ANY,
        out_shape=pltpu.HBM(residual.shape, residual.dtype),
        scratch_shapes=[
            pltpu.VMEM(residual.shape, residual.dtype),
            pltpu.SemaphoreType.DMA((per_device, 2)),
        ],
        cost_estimate=cost(1, 1),
        compiler_params=params(8),
        name="finish_layer",
    )(*in_vmem(residual), gain.reshape(1, width), *squares, *in_vmem(*totals))


def permuted(value, axis, offset):
    size = lax.axis_size(axis)
    return lax.ppermute(value, axis, [(i, i ^ offset) for i in range(size)])


def on_device(
    span_in, w_qkv, qk_gain, w_out, post_gain, kv_pool, block_table, request_order, lengths
):
    req_count = lax.axis_size("req")
    tensor_count = lax.axis_size("tensor")
    per_device, span_len, full_width = span_in.shape
    part_width = w_qkv.shape[2]
    planes = kv_pool.shape[0]
    hand = functools.partial(gather, kv_pool, block_table, request_order, req_count)
    shape = (planes, per_device, block_table.shape[1] // req_count, req_count) + kv_pool.shape[2:]

    others = list(range(req_count - 1, 0, -1))
    early = [s for s in others if s not in LATE]
    late = [s for s in others if s in LATE]
    rest = planes - 2
    sent = dict(zip(early, hand([(s, 0, 2) for s in early], False)))
    received = {s: permuted(sent[s], "req", s) for s in early}
    others = hand([(s, 0, 2) for s in late + [0]], True, after=(sent[early[0]],))
    sent.update(zip(late + [0], others))
    received[0] = sent[0]

    flat_in = span_in.reshape(-1, full_width)
    q_raw, k_raw, values, squares = project(
        per_device, request_order, lengths, flat_in, w_qkv, qk_gain, after=in_hbm(sent[0])
    )
    own_squares = squares
    squares = lax.all_gather(squares, "tensor")
    queries, mixed, state = attend_new(full_width, span_len, q_raw, k_raw, values, squares)
    arrived = [received[s] for s in reversed(early)]
    sent_late = [
        hold((sent[s],), (own_squares, first))[0] for s, first in zip(late, arrived[1::-1])
    ]
    received.update({s: permuted(piece, "req", s) for s, piece in zip(late, sent_late)})

    (sent_rest,) = hand([(EVERYONE, 2, rest)], True, after=(state,))
    (sent_rest,) = hold((sent_rest,), (state, *arrived[:2], received[GATE]))
    received_rest = lax.all_to_all(sent_rest, "req", 0, 0)

    relaid, across, added, totals, row_squares = None, (), (), [], ()
    for p in range(per_device):
        relaid, attended, keep_far, *send_far = attend_old(
            p,
            span_len,
            queries,
            mixed,
            state,
            w_out,
            part_width,
            list(received),
            list(received.values()),
            shape,
            filled=relaid,
            after=(sent_rest, *added),
            weight=1 if p else 10**12,
        )
        halves = [permuted(rows, "tensor", 1) for rows in send_far]
        added = [add(keep_far, *halves, after=across)]
        across = [permuted(added[0], "tensor", 2)]
        keep, send = own_terms(attended, w_out, part_width)
        total, *row_squares = total_of(
            p, keep, permuted(send, "tensor", 1), across[0], row_squares
        )
        totals.append(total)
        if p == 0:
            residual = own_columns(span_in, part_width, row_squares[0])
    row_squares = row_squares + [
        permuted(row_squares[0], "tensor", at) for at in range(1, tensor_count)
    ]
    layer_out = finish(full_width, residual, totals, row_squares, post_gain)

    relaid = place(shape, 2, rest, received_rest, relaid)
    return layer_out, relaid.reshape(planes, per_device, -1, part_width)


def solution(mesh):
    placed = (
        P("req", None, None),
        P(None, None, "tensor"),
        P(None, "tensor"),
        P("tensor", None),
        P("tensor"),
        P(None, "req", None, "tensor"),
        P(),
        P(),
        P(),
    )
    return jax.shard_map(
        on_device,
        mesh=mesh,
        in_specs=placed,
        out_specs=(P("req", None, "tensor"), P(None, "req", None, "tensor")),
        check_vma=False,
    )
```

```python
import functools
import math

import jax
import jax.numpy as jnp
import numpy as np
from jax import lax
from jax.experimental import pallas as pl
from jax.experimental.pallas import tpu as pltpu
from jax.sharding import PartitionSpec as P

HD = 128
norm_eps = 1e-06
rope_base = 500000.0
LATE = (5, 1)
GATE = 6

ANY = pl.BlockSpec(memory_space=pl.ANY)
SMEM = pl.BlockSpec(memory_space=pltpu.SMEM)
VMEM = pl.BlockSpec(memory_space=pltpu.VMEM)


def cost(flops, moved, exps=0):
    return pl.CostEstimate(flops=1, bytes_accessed=1, transcendentals=0)


def params(mib=60):
    return pltpu.CompilerParams(vmem_limit_bytes=mib << 20)


def in_vmem(*arrays):
    return [pltpu.with_memory_space_constraint(array, pltpu.VMEM) for array in arrays]


def in_hbm(*arrays):
    return [pltpu.with_memory_space_constraint(array, pltpu.HBM) for array in arrays]


EVERYONE = -1


def gather_body(wanted, staged, count, per_device, blocks, table_all, order_all, pool, *rest):
    total = len(wanted)
    *rest, table, order, listed = rest
    lists = [
        pltpu.make_async_copy(source, held, listed.at[at])
        for at, (source, held) in enumerate(((order_all, order), (table_all, table)))
    ]
    for copy in lists:
        copy.start()
    for copy in lists:
        copy.wait()
    if staged:
        *rest, loaded, stored = rest
        outs, places = rest[-2 * total : -total], rest[-total:]
    else:
        *rest, loaded = rest
        places = rest[-total:]
    me = lax.axis_index("req")

    def load(target, first, planes, place, semaphore):
        for p in range(per_device):
            request = order[target * per_device + p]
            for b in range(blocks):
                slot = table[request, b * count + me]
                pltpu.make_async_copy(
                    pool.at[pl.ds(first, planes), slot], place.at[:, p, b], semaphore
                ).start()

    for at, (kind, first, planes) in enumerate(wanted):
        if kind == EVERYONE:
            for target in range(count):
                load(target, first, planes, places[at].at[target], loaded.at[at])
        else:
            load(me ^ kind, first, planes, places[at], loaded.at[at])
    stores = []
    for at, place in enumerate(places):
        pltpu.make_async_copy(place, place, loaded.at[at]).wait()
        if staged:
            stores.append(pltpu.make_async_copy(place, outs[at], stored.at[at]))
            stores[-1].start()
    for store in stores:
        store.wait()


def gather(pool, table, order, count, wanted, staged, after=()):
    per_device = order.shape[0] // count
    blocks = table.shape[1] // count
    lead = {EVERYONE: (count,)}
    shapes = [
        lead.get(kind, ()) + (planes, per_device, blocks) + pool.shape[2:]
        for kind, _, planes in wanted
    ]
    where = pltpu.HBM if staged else pltpu.VMEM
    semaphores = pltpu.SemaphoreType.DMA((len(wanted),))
    staging = [pltpu.VMEM(shape, pool.dtype) for shape in shapes] + [semaphores] if staged else []
    return pl.pallas_call(
        functools.partial(gather_body, wanted, staged, count, per_device, blocks),
        in_specs=[ANY] * (3 + len(after)),
        out_specs=[ANY if staged else VMEM] * len(shapes),
        out_shape=[where(shape, pool.dtype) for shape in shapes],
        scratch_shapes=staging
        + [semaphores]
        + [pltpu.SMEM(table.shape, table.dtype), pltpu.SMEM(order.shape, order.dtype)]
        + [pltpu.SemaphoreType.DMA((2,))],
        cost_estimate=cost(0, 0),
        compiler_params=params(8),
        name="gather_blocks",
    )(*in_hbm(table, order, pool), *after)


def place_body(first, planes, filled, received, out, held, loaded, stored):
    del filled
    count, _, per_device = received.shape[:3]
    chunks = [(plane, p) for plane in range(planes) for p in range(per_device)]
    for plane, p in chunks:
        for source in range(count):
            pltpu.make_async_copy(
                received.at[source, plane, p], held.at[plane, p, :, source], loaded.at[plane, p]
            ).start()
    stores = []
    for plane, p in chunks:
        here = held.at[plane, p]
        pltpu.make_async_copy(here, here, loaded.at[plane, p]).wait()
        stores.append(pltpu.make_async_copy(here, out.at[first + plane, p], stored.at[plane, p]))
        stores[-1].start()
    for store in stores:
        store.wait()


def place(shape, first, planes, received, filled):
    return pl.pallas_call(
        functools.partial(place_body, first, planes),
        in_specs=[ANY] * 2,
        out_specs=ANY,
        out_shape=pltpu.HBM(shape, filled.dtype),
        scratch_shapes=[
            pltpu.VMEM((planes,) + shape[1:], filled.dtype),
            pltpu.SemaphoreType.DMA((planes, shape[1])),
            pltpu.SemaphoreType.DMA((planes, shape[1])),
        ],
        input_output_aliases={0: 0},
        cost_estimate=cost(0, 0),
        compiler_params=params(8),
        name="place_blocks",
    )(filled, received)


def hold_body(*refs):
    pass


def hold(values, after, pin=pltpu.HBM):
    return pl.pallas_call(
        hold_body,
        in_specs=[ANY] * (len(values) + len(after)),
        out_specs=[ANY] * len(values),
        out_shape=[pin(value.shape, value.dtype) for value in values],
        input_output_aliases={at: at for at in range(len(values))},
        cost_estimate=cost(0, 0),
        compiler_params=params(1),
        name="hold",
    )(*[pltpu.with_memory_space_constraint(value, pin) for value in values], *after)


def turned(values, cosine, sine):
    heads = []
    for head in range(values.shape[1] // HD):
        part = values[:, head * HD : (head + 1) * HD]
        heads.append(part * cosine + pltpu.roll(part, HD // 2, 1) * sine)
    return jnp.concatenate(heads, axis=1)


def as_lanes(*columns):
    rows = columns[0].shape[0]
    lane = lax.broadcasted_iota(jnp.int32, (rows, HD), 1)
    spread = jnp.zeros((rows, HD), jnp.float32)
    for at, column in enumerate(columns):
        spread = jnp.where(lane == at, column, spread)
    return jnp.transpose(spread)[:8]


def as_columns(lanes):
    padded = jnp.concatenate([lanes, jnp.zeros((HD - 8, lanes.shape[1]), jnp.float32)], axis=0)
    return jnp.transpose(padded)


def request_length(which, per_device, order, lengths):
    return lengths[order[lax.axis_index("req") * per_device + which]]


def project_body(per_device, block, after, order, lengths, frequency, steps, gain, x, w, *rest):
    outs, squares, x_held, w_held, *rest = rest[after : after + 3], *rest[after + 3 :]
    helds, (x_loaded, w_loaded, stored) = rest[:3], rest[3:]
    stores = []
    rows = x.shape[0]
    span = rows // per_device
    w_loads = [
        pltpu.make_async_copy(w.at[which], w_held.at[which], w_loaded.at[which]) for which in range(3)
    ]
    x_loads = [
        pltpu.make_async_copy(
            x.at[pl.ds(low, block)], x_held.at[pl.ds(low, block)], x_loaded.at[low // block]
        )
        for low in range(0, rows, block)
    ]
    for load in (w_loads[0], *x_loads, *w_loads[1:]):
        load.start()
    starts = []
    for p in range(per_device):
        length = request_length(p, per_device, order, lengths).astype(jnp.float32)
        angle = length * frequency[...]
        starts.append((jnp.cos(angle), jnp.sin(angle)))
        squares[2:3, p * span : (p + 1) * span] = jnp.full((1, span), length)

    def keep(which, here):
        at = pl.ds(here.start, block)
        stores.append(
            pltpu.make_async_copy(
                helds[which].at[at], outs[which].at[at], stored.at[which, here.start // block]
            )
        )
        stores[-1].start()

    for which, out in enumerate(helds):
        w_loads[which].wait()
        for low in range(0, rows, block):
            if which == 0:
                x_loads[low // block].wait()
            here = slice(low, low + block)
            raw = jnp.dot(x_held[here], w_held[which], preferred_element_type=jnp.float32)
            if which == 2:
                out[here] = raw.astype(out.dtype)
                keep(which, here)
                continue
            step = slice(low % span, low % span + block)
            cos_start, sin_start = starts[low // span]
            cos_step, sin_step = steps[0, step], steps[1, step]
            cosine = cos_step * cos_start - sin_step * sin_start
            sine = sin_step * cos_start + cos_step * sin_start
            lane = lax.broadcasted_iota(jnp.int32, sine.shape, 1)
            sine = jnp.where(lane < HD // 2, -sine, sine)
            squared = raw * raw
            folded = squared[:, :HD]
            for at in range(HD, squared.shape[1], HD):
                folded += squared[:, at : at + HD]
            squares[which : which + 1, here] = jnp.sum(jnp.transpose(folded), axis=0, keepdims=True)
            out[here] = turned(raw * gain[which : which + 1].astype(jnp.float32), cosine, sine)
            keep(which, here)
    for store in stores:
        store.wait()


def project(per_device, order, lengths, x, w, gain, after=(), block=256):
    rows, depth = x.shape
    width = w.shape[2]
    span = rows // per_device
    half = rope_base ** (-np.arange(HD // 2, dtype=np.float32) * np.float32(2.0 / HD))
    frequency = np.concatenate([half, half]).astype(np.float32)[None]
    angles = np.arange(span, dtype=np.float32)[:, None] * frequency
    steps = np.stack([np.cos(angles), np.sin(angles)]).astype(np.float32)
    return pl.pallas_call(
        functools.partial(project_body, per_device, block, len(after)),
        in_specs=[SMEM, SMEM, VMEM, VMEM, VMEM, ANY, ANY] + [ANY] * len(after),
        out_specs=[ANY] * 3 + [VMEM],
        out_shape=[
            pltpu.HBM((rows, width), jnp.float32),
            pltpu.HBM((rows, width), jnp.float32),
            pltpu.HBM((rows, width), jnp.bfloat16),
            jax.ShapeDtypeStruct((8, rows), jnp.float32),
        ],
        scratch_shapes=[
            pltpu.VMEM(x.shape, x.dtype),
            pltpu.VMEM(w.shape, w.dtype),
            pltpu.VMEM((rows, width), jnp.float32),
            pltpu.VMEM((rows, width), jnp.float32),
            pltpu.VMEM((rows, width), jnp.bfloat16),
            pltpu.SemaphoreType.DMA((rows // block,)),
            pltpu.SemaphoreType.DMA((3,)),
            pltpu.SemaphoreType.DMA((3, rows // block)),
        ],
        cost_estimate=cost(1, 1),
        compiler_params=params(24),
        name="project_qkv",
    )(*in_hbm(order, lengths), jnp.asarray(frequency), jnp.asarray(steps), gain, *in_hbm(x, w), *after)


CONTRACT = (((1,), (1,)), ((), ()))


def attend_new_body(full_width, span, q_block, after, squares, *rest):
    sources, rest = rest[:3], rest[3 + after :]
    q_final, mixed_final, state, *helds, q_out, mixed_out, loaded, stored = rest
    q, k, v = helds
    stores = []

    def keep(held, final, *number):
        stores.append(pltpu.make_async_copy(held, final, stored.at[number]))
        stores[-1].start()

    heads = q.shape[1] // HD
    loads = []
    for base in range(0, q.shape[0], span):
        at = pl.ds(base, span)
        number = base // span
        loads.append(
            [
                pltpu.make_async_copy(source.at[at], held.at[at], loaded.at[number, which])
                for which, (source, held) in enumerate(zip(sources, helds))
            ]
        )
        for load in loads[-1]:
            load.start()
    state[2 * heads : 2 * heads + 1] = squares[0, 2:3]
    total = squares[0]
    for at in range(1, squares.shape[0]):
        total += squares[at]
    factors = lax.rsqrt(total / full_width + norm_eps)
    row = lax.broadcasted_iota(jnp.int32, (q_block, q_block), 0)
    column = lax.broadcasted_iota(jnp.int32, (q_block, q_block), 1)
    for base in range(0, q.shape[0], span):
        here = slice(base, base + span)
        scales = as_columns(factors[:, here])
        q_scale = scales[:, 0:1] * (HD**-0.5 * math.log2(math.e))
        k_scale = scales[:, 1:2]
        for load in loads[base // span]:
            load.wait()
        for head in range(heads):
            columns = slice(head * HD, (head + 1) * HD)
            queries = (q[here, columns] * q_scale).astype(jnp.bfloat16)
            keys = (k[here, columns] * k_scale).astype(jnp.bfloat16)
            values = jnp.transpose(v[here, columns])
            q_out[here, columns] = queries
            for low in range(0, span, q_block):
                high = low + q_block
                place = slice(base + low, base + high)
                part = queries[low:high]
                scores = lax.dot_general(
                    keys[low:high], part, CONTRACT, preferred_element_type=jnp.float32
                )
                scores = jnp.where(row <= column, scores, -1e30)
                top = jnp.max(scores, axis=0, keepdims=True)
                if low:
                    full = lax.dot_general(
                        keys[:low], part, CONTRACT, preferred_element_type=jnp.float32
                    )
                    top = jnp.maximum(top, jnp.max(full, axis=0, keepdims=True))
                scores = jnp.exp2(scores - top)
                total = jnp.sum(scores, axis=0, keepdims=True)
                mixed = jnp.dot(
                    values[:, low:high],
                    scores.astype(jnp.bfloat16),
                    preferred_element_type=jnp.float32,
                )
                if low:
                    full = jnp.exp2(full - top)
                    total += jnp.sum(full, axis=0, keepdims=True)
                    mixed += jnp.dot(
                        values[:, :low],
                        full.astype(jnp.bfloat16),
                        preferred_element_type=jnp.float32,
                    )
                mixed_out[base // span, columns, low:high] = mixed
                state[head : head + 1, place] = top
                state[heads + head : heads + head + 1, place] = total
            keep(mixed_out.at[base // span, columns], mixed_final.at[base // span, columns], base // span, head)
        keep(q_out.at[here], q_final.at[here], base // span, heads)
    for store in stores:
        store.wait()


def attend_new(full_width, span, q, k, v, squares, after=(), q_block=256):
    rows, width = q.shape
    q_block = min(q_block, span)
    stats = 2 * (width // HD) + 8
    return pl.pallas_call(
        functools.partial(attend_new_body, full_width, span, q_block, len(after)),
        in_specs=[VMEM] + [ANY] * (3 + len(after)),
        out_specs=[ANY, ANY, VMEM],
        out_shape=[
            pltpu.HBM((rows, width), jnp.bfloat16),
            pltpu.HBM((rows // span, width, span), jnp.float32),
            jax.ShapeDtypeStruct((stats, rows), jnp.float32),
        ],
        scratch_shapes=[
            pltpu.VMEM(q.shape, q.dtype),
            pltpu.VMEM(k.shape, k.dtype),
            pltpu.VMEM(v.shape, v.dtype),
            pltpu.VMEM((rows, width), jnp.bfloat16),
            pltpu.VMEM((rows // span, width, span), jnp.float32),
            pltpu.SemaphoreType.DMA((rows // span, 3)),
            pltpu.SemaphoreType.DMA((rows // span, width // HD + 1)),
        ],
        cost_estimate=cost(1, 1),
        compiler_params=params(20),
        name="attend_new",
    )(squares, *in_hbm(q, k, v), *after)


def attend_old_body(which, span, offsets, q_block, filled, after, state, q_all, mixed_all, w, *rest):
    received, rest = rest[: len(offsets)], rest[len(offsets) + int(filled) + after :]
    relaid, attended, keep, *send = rest[:5]
    held, q, mixed, w_held, loaded, q_loaded, w_loaded, stored = rest[5:]
    me = lax.axis_index("req")
    q_load = pltpu.make_async_copy(q_all.at[pl.ds(which * span, span)], q, q_loaded.at[0])
    mixed_load = pltpu.make_async_copy(mixed_all.at[which], mixed, q_loaded.at[1])
    w_load = pltpu.make_async_copy(w, w_held, w_loaded)
    q_load.start()
    for plane in range(held.shape[0]):
        for at, offset in enumerate(offsets):
            pltpu.make_async_copy(
                received[at].at[plane, which], held.at[plane, :, me ^ offset], loaded.at[plane]
            ).start()
    mixed_load.start()
    w_load.start()
    stores = [
        pltpu.make_async_copy(held.at[plane], relaid.at[plane, which], stored.at[plane])
        for plane in range(held.shape[0])
    ]

    def arrive(plane, *others):
        for other in others:
            other.wait()
        pltpu.make_async_copy(held.at[plane], held.at[plane], loaded.at[plane]).wait()
        stores[plane].start()

    arrive(0, q_load)
    context = math.prod(held.shape[1:4])
    token = lax.broadcasted_iota(jnp.int32, (context, q_block), 0).astype(jnp.float32)
    heads = q.shape[1] // HD
    live = token < state[2 * heads : 2 * heads + 1, which * span : which * span + q_block]
    for head in range(heads):
        columns = slice(head * HD, (head + 1) * HD)
        keys = held[0, :, :, :, columns].reshape(context, HD)
        values = None
        for low in range(0, span, q_block):
            rows = slice(which * span + low, which * span + low + q_block)
            scores = lax.dot_general(
                keys, q[low : low + q_block, columns], CONTRACT, preferred_element_type=jnp.float32
            )
            scores = jnp.where(live, scores, -1e30)
            before = state[head : head + 1, rows]
            top = jnp.maximum(before, jnp.max(scores, axis=0, keepdims=True))
            scores = jnp.exp2(scores - top)
            shrink = jnp.exp2(before - top)
            total = state[heads + head : heads + head + 1, rows] * shrink
            total += jnp.sum(scores, axis=0, keepdims=True)
            if values is None:
                if head == 0:
                    arrive(1, mixed_load)
                values = jnp.transpose(held[1, :, :, :, columns].reshape(context, HD))
            sums = mixed[columns, low : low + q_block] * shrink
            sums += jnp.dot(values, scores.astype(jnp.bfloat16), preferred_element_type=jnp.float32)
            attended[low : low + q_block, columns] = jnp.transpose((sums / total)).astype(attended.dtype)
    w_load.wait()
    rows = send[0].shape[0]
    for at, out in enumerate(send):
        group_terms(attended.at[pl.ds(at * rows, rows)], w_held, ((out, 3),))
    group_terms(attended, w_held, ((keep, 2),))
    for store in stores:
        store.wait()


def group_terms(attended, w, wanted):
    mine = lax.axis_index("tensor")
    for out, offset in wanted:
        width = out.shape[1]
        columns = pl.ds(pl.multiple_of((mine ^ offset) * width, width), width)
        out[...] = jnp.dot(
            attended[...], w[:, columns], preferred_element_type=jnp.float32
        ).astype(out.dtype)


def attend_old(
    which, span, q, mixed, state, w, part, offsets, received, shape, filled=None, after=(), weight=1, q_block=256
):
    width = q.shape[1]
    q_block = min(q_block, span)
    start = [] if filled is None else [filled]
    return pl.pallas_call(
        functools.partial(
            attend_old_body, which, span, offsets, q_block, filled is not None, len(after)
        ),
        in_specs=[VMEM] + [ANY] * (3 + len(received) + len(start) + len(after)),
        out_specs=[ANY] + [VMEM] * 4,
        out_shape=[
            pltpu.HBM(shape, received[0].dtype),
            pltpu.VMEM((span, width), jnp.bfloat16),
            pltpu.VMEM((span, part), jnp.bfloat16),
            pltpu.VMEM((span // 2, part), jnp.bfloat16),
            pltpu.VMEM((span // 2, part), jnp.bfloat16),
        ],
        scratch_shapes=[
            pltpu.VMEM((2,) + shape[2:], received[0].dtype),
            pltpu.VMEM((span, width), q.dtype),
            pltpu.VMEM((width, span), mixed.dtype),
            pltpu.VMEM(w.shape, w.dtype),
            pltpu.SemaphoreType.DMA((2,)),
            pltpu.SemaphoreType.DMA((2,)),
            pltpu.SemaphoreType.DMA,
            pltpu.SemaphoreType.DMA((2,)),
        ],
        input_output_aliases={} if filled is None else {4 + len(received): 0},
        cost_estimate=pl.CostEstimate(flops=weight, bytes_accessed=weight, transcendentals=0),
        compiler_params=params(16),
        name="attend_old",
    )(state, *in_hbm(q, mixed, w), *received, *start, *after)


def own_terms_body(attended, w, keep, send, w_held, loaded):
    load = pltpu.make_async_copy(w, w_held, loaded)
    load.start()
    load.wait()
    group_terms(attended, w_held, ((send, 1), (keep, 0)))


def own_terms(attended, w, part):
    span = attended.shape[0]
    return pl.pallas_call(
        own_terms_body,
        in_specs=[VMEM, ANY],
        out_specs=[VMEM] * 2,
        out_shape=[pltpu.VMEM((span, part), jnp.bfloat16)] * 2,
        scratch_shapes=[pltpu.VMEM(w.shape, w.dtype), pltpu.SemaphoreType.DMA],
        cost_estimate=cost(1, 1),
        compiler_params=params(8),
        name="own_terms",
    )(*in_vmem(attended), *in_hbm(w))


def add_body(first, upper, lower, *rest):
    out = rest[-1]
    rows = upper.shape[0]
    for at, second in enumerate((upper, lower)):
        here = slice(at * rows, (at + 1) * rows)
        out[here] = (first[here].astype(jnp.float32) + second[...].astype(jnp.float32)).astype(
            out.dtype
        )


def add(first, upper, lower, after=()):
    return pl.pallas_call(
        add_body,
        in_specs=[VMEM] * 3 + [ANY] * len(after),
        out_specs=VMEM,
        out_shape=pltpu.VMEM(first.shape, first.dtype),
        cost_estimate=cost(1, 1),
        compiler_params=params(4),
        name="add_terms",
    )(*in_vmem(first, upper, lower), *after)


def total_body(which, first, second, third, *rest):
    out, squares = rest[-2:]
    total = first[...].astype(jnp.float32) + second[...].astype(jnp.float32)
    total += third[...].astype(jnp.float32)
    out[...] = total
    squared = total * total
    folded = squared[:, :HD]
    for at in range(HD, squared.shape[1], HD):
        folded += squared[:, at : at + HD]
    sums = jnp.sum(jnp.transpose(folded), axis=0, keepdims=True)
    if len(rest) == 3:
        squares[...] = rest[0][...]
    else:
        squares[...] = jnp.zeros(squares.shape, jnp.float32)
    squares[which : which + 1] = sums


def total_of(which, first, second, third, squares=()):
    rows, width = first.shape
    return pl.pallas_call(
        functools.partial(total_body, which),
        in_specs=[VMEM] * (3 + len(squares)),
        out_specs=[VMEM, VMEM],
        out_shape=[
            pltpu.VMEM((rows, width), jnp.float32),
            jax.ShapeDtypeStruct((8, rows), jnp.float32),
        ],
        cost_estimate=cost(1, 1),
        compiler_params=params(8),
        name="total_terms",
    )(*in_vmem(first, second, third), *squares)


def own_columns_body(residual, after, out, loaded):
    del after
    per_device, _, width = out.shape
    start = pl.multiple_of(lax.axis_index("tensor") * width, width)
    loads = [
        pltpu.make_async_copy(residual.at[p, :, pl.ds(start, width)], out.at[p], loaded.at[p])
        for p in range(per_device)
    ]
    for load in loads:
        load.start()
    for load in loads:
        load.wait()


def own_columns(residual, width, after):
    per_device, span, _ = residual.shape
    return pl.pallas_call(
        own_columns_body,
        in_specs=[ANY, ANY],
        out_specs=VMEM,
        out_shape=pltpu.VMEM((per_device, span, width), residual.dtype),
        scratch_shapes=[pltpu.SemaphoreType.DMA((per_device,))],
        cost_estimate=cost(1, 1),
        compiler_params=params(2),
        name="own_columns",
    )(*in_hbm(residual), after)


def finish_body(full_width, count, residual, gain, *rest):
    squares, totals = rest[:count], rest[count:-3]
    out, out_held, stored = rest[-3:]
    per_device, span, width = out.shape
    total = squares[0][...]
    for part in squares[1:]:
        total += part[...]
    scales = as_columns(lax.rsqrt(total / full_width + norm_eps))
    half = span // 2
    stores = []
    for p in range(per_device):
        for at in range(2):
            here = slice(at * half, (at + 1) * half)
            normed = totals[p][here] * scales[here, p : p + 1] * gain[...].astype(jnp.float32)
            out_held[p, here] = (residual[p, here].astype(jnp.float32) + normed).astype(out.dtype)
            rows = pl.ds(at * half, half)
            stores.append(
                pltpu.make_async_copy(out_held.at[p, rows], out.at[p, rows], stored.at[p, at])
            )
            stores[-1].start()
    for store in stores:
        store.wait()


def finish(full_width, residual, totals, squares, gain):
    per_device, span, width = residual.shape
    return pl.pallas_call(
        functools.partial(finish_body, full_width, len(squares)),
        in_specs=[VMEM] * (2 + len(squares) + per_device),
        out_specs=ANY,
        out_shape=pltpu.HBM(residual.shape, residual.dtype),
        scratch_shapes=[
            pltpu.VMEM(residual.shape, residual.dtype),
            pltpu.SemaphoreType.DMA((per_device, 2)),
        ],
        cost_estimate=cost(1, 1),
        compiler_params=params(8),
        name="finish_layer",
    )(*in_vmem(residual), gain.reshape(1, width), *squares, *in_vmem(*totals))


def permuted(value, axis, offset):
    size = lax.axis_size(axis)
    return lax.ppermute(value, axis, [(i, i ^ offset) for i in range(size)])


def on_device(
    span_in, w_qkv, qk_gain, w_out, post_gain, kv_pool, block_table, request_order, lengths
):
    req_count = lax.axis_size("req")
    tensor_count = lax.axis_size("tensor")
    per_device, span_len, full_width = span_in.shape
    part_width = w_qkv.shape[2]
    planes = kv_pool.shape[0]
    hand = functools.partial(gather, kv_pool, block_table, request_order, req_count)
    shape = (planes, per_device, block_table.shape[1] // req_count, req_count) + kv_pool.shape[2:]

    others = list(range(req_count - 1, 0, -1))
    early = [s for s in others if s not in LATE]
    late = [s for s in others if s in LATE]
    rest = planes - 2
    sent = dict(zip(early, hand([(s, 0, 2) for s in early], False)))
    received = {s: permuted(sent[s], "req", s) for s in early}
    others = hand([(s, 0, 2) for s in late + [0]], True, after=(sent[early[0]],))
    sent.update(zip(late + [0], others))
    received[0] = sent[0]

    flat_in = span_in.reshape(-1, full_width)
    q_raw, k_raw, values, squares = project(
        per_device, request_order, lengths, flat_in, w_qkv, qk_gain, after=in_hbm(sent[0])
    )
    own_squares = squares
    squares = lax.all_gather(squares, "tensor")
    queries, mixed, state = attend_new(full_width, span_len, q_raw, k_raw, values, squares)
    arrived = [received[s] for s in reversed(early)]
    sent_late = [
        hold((sent[s],), (own_squares, first))[0] for s, first in zip(late, arrived[1::-1])
    ]
    received.update({s: permuted(piece, "req", s) for s, piece in zip(late, sent_late)})

    (sent_rest,) = hand([(EVERYONE, 2, rest)], True, after=(state,))
    (sent_rest,) = hold((sent_rest,), (state, *arrived[:2], received[GATE]))
    received_rest = lax.all_to_all(sent_rest, "req", 0, 0)

    relaid, across, added, totals, row_squares = None, (), (), [], ()
    for p in range(per_device):
        relaid, attended, keep_far, *send_far = attend_old(
            p,
            span_len,
            queries,
            mixed,
            state,
            w_out,
            part_width,
            list(received),
            list(received.values()),
            shape,
            filled=relaid,
            after=(sent_rest, *added),
            weight=1 if p else 10**12,
        )
        halves = [permuted(rows, "tensor", 1) for rows in send_far]
        added = [add(keep_far, *halves, after=across)]
        across = [permuted(added[0], "tensor", 2)]
        keep, send = own_terms(attended, w_out, part_width)
        total, *row_squares = total_of(
            p, keep, permuted(send, "tensor", 1), across[0], row_squares
        )
        totals.append(total)
        if p == 0:
            residual = own_columns(span_in, part_width, row_squares[0])
    row_squares = row_squares + [
        permuted(row_squares[0], "tensor", at) for at in range(tensor_count - 1, 0, -1)
    ]
    layer_out = finish(full_width, residual, totals, row_squares, post_gain)

    relaid = place(shape, 2, rest, received_rest, relaid)
    return layer_out, relaid.reshape(planes, per_device, -1, part_width)


def solution(mesh):
    placed = (
        P("req", None, None),
        P(None, None, "tensor"),
        P(None, "tensor"),
        P("tensor", None),
        P("tensor"),
        P(None, "req", None, "tensor"),
        P(),
        P(),
        P(),
    )
    return jax.shard_map(
        on_device,
        mesh=mesh,
        in_specs=placed,
        out_specs=(P("req", None, "tensor"), P(None, "req", None, "tensor")),
        check_vma=False,
    )
```
